128 devices in a mesh: db: 16 (over x, z), head: 8 (over y, core).
Axes of the slice: x: 4, y: 4, z: 4, core: 2. Of those that a mesh axis runs over, the one named last changes fastest.
Arguments:
- queries: bfloat16 [2048, 4096], P('db', 'head'), may hold values from -6 to 6
- w_key: bfloat16 [896, 4096], P(None, 'head'), may hold values from -0.1875 to 0.1875
- w_value: bfloat16 [896, 4096], P(None, 'head'), may hold values from -0.1875 to 0.1875
- w_out: bfloat16 [4096, 4096], P('head'), may hold values from -0.375 to 0.375
- encodings: bfloat16 [1024, 128, 896], P('db', 'head'), may hold values from -6 to 6
- nbr_row: int32 [32, 8], P('db'), may hold values from 0 to 63
- nbr_owner: int32 [32, 8], P('db'), may hold values from 0 to 15, all different within a row; in each aligned block of 2 rows (0 to 1, 2 to 3, ...) at most 2 rows name the same one
- nbr_count: int32 [32], P('db'), may hold values from 2 to 8
- grad_out: bfloat16 [2048, 4096], P('db', 'head'), may hold values from -6 to 6
Outputs:
- attended: bfloat16 [2048, 4096], P('db', 'head')
- grad_queries: bfloat16 [2048, 4096], P('db', 'head')
- grad_wk: float32 [896, 4096], P('db', 'head')
- grad_wv: float32 [896, 4096], P('db', 'head')
- grad_wo: float32 [4096, 4096], P('head', 'db')
The draws below stay inside these ranges and needn't reach their ends.
Inputs may be any that keep to these rules, and one draw needn't show every extreme that they name: `nbr_owner`: the 8 owners named by one group are all different.
All inputs are finite; a program needn't handle non-finite values.
Results may differ from the reference program's by a relative error of at most 0.023.
Values may be sent and summed in bfloat16 or wider, within the bound.
No kernel may reach another device: no remote copies, remote signals or barrier semaphores. Data moves between devices by JAX's collectives and lax.ppermute only.
A program may use at most 128 MiB of HBM per device.

```python
import math
import jax
import jax.numpy as jnp
import numpy as np
from jax import lax

D = 4096
HEADS = 32
HD = 128
E = 896
NT = 128
CL = 64
K = 8
CH_DEV = 2
NB_DEV = 64
GROUPS = 32
TOKENS = 2048
NBR = 1024
N_DB = 16


def plant(drawn, rng, low, top_value):
    index_at = [jax.random.randint(jax.random.fold_in(rng, axis), (), 0, length) for axis, length in enumerate(drawn.shape)]
    widest = drawn.shape.index(max(drawn.shape))
    next_to = index_at[:widest] + [(index_at[widest] + 1) % drawn.shape[widest]] + index_at[widest + 1:]
    return drawn.at[tuple(index_at)].set(low).at[tuple(next_to)].set(top_value)


def strengthened(array, rng, source, target, shards_of, factor):
    def block_of(axis_at):
        return (jnp.arange(array.shape[axis_at]) // (array.shape[axis_at] // shards_of)).reshape((-1,) + (1,) * (array.ndim - 1 - axis_at))

    first = jax.random.permutation(rng, shards_of)[block_of(target)]
    second = (block_of(target) + shards_of // 2) % shards_of
    return jnp.where((block_of(source) == first) | (block_of(source) == second), factor * array, array)


def block_levels(own_key, extent, shards, least, high):
    def one(position, blocks):
        draws = jax.random.uniform(jax.random.fold_in(jax.random.fold_in(own_key, 6), position), (blocks,), jnp.float32, least / len(shards), high / len(shards))
        return jnp.repeat(jnp.exp(draws), extent[position] // blocks).reshape((-1,) + (1,) * (len(extent) - position - 1))

    gain = one(*shards[0])
    for cut in shards[1:]:
        gain = gain * one(*cut)
    return gain


def deal_out(key, own, number, rows, amount, top, reach, lean):
    order = jax.random.permutation(key, amount)
    packed, common = shares(amount, rows * top, reach, lean, True), shares(amount, rows * top, reach, lean, False)
    places = jnp.arange(amount)

    def named(tallies, turn):
        used = int((tallies > 0).sum())
        fixed = max(1, used // 4)
        shifted = fixed + (places - fixed + turn * (used - fixed)) % max(1, amount - fixed)
        return jnp.zeros((amount,), jnp.int32).at[order[jnp.where(places < fixed, places, shifted)]].set(jnp.asarray(tallies, jnp.int32))

    tallies = jnp.where(number % 4 == 0, named(packed, number // 4), named(common, number - number // 4 - 1))
    mixed = jax.random.permutation(jax.random.fold_in(own, 3), amount)
    source_of, receiver = mixed[0:amount // 2 * 2:2], mixed[1:amount // 2 * 2:2]
    margin = jnp.minimum(tallies[source_of] - 1, reach - tallies[receiver]) // 2
    margin = jnp.where((source_of == order[0]) | (receiver == order[0]) | (tallies[receiver] == 0), 0, jnp.maximum(margin, 0))
    shifted = jax.random.randint(jax.random.fold_in(own, 4), (amount // 2,), 0, 1 << 20) % (margin + 1)
    tallies = tallies.at[source_of].add(-shifted).at[receiver].add(shifted)
    labels = jnp.searchsorted(jnp.cumsum(tallies), jnp.arange(rows * top), side="right").astype(jnp.int32)
    grid = labels.reshape(top, rows).T
    grid = grid[jax.random.permutation(jax.random.fold_in(own, 1), rows)]
    turn = jax.random.randint(jax.random.fold_in(own, 2), (rows, 1), 0, top)
    return jnp.take_along_axis(grid, (jnp.arange(top)[None, :] + turn) % top, axis=1)


def shares(number_of, total, reach, lean, full):
    portions = [(1 << 20) // math.isqrt(grade ** lean) + 1 for grade in range(1, number_of + 1)]
    largest = reach if full else min(reach, max(-(-total // number_of), total * portions[0] // sum(portions)))
    least = 1 if total - largest >= number_of - 1 else 0
    given, rest = [largest] + [least] * (number_of - 1), total - largest - least * (number_of - 1)
    while rest > 0:
        movable = [i for i in range(1, number_of) if given[i] < largest] or [i for i in range(1, number_of) if given[i] < reach]
        mass, budget = sum([portions[i] for i in movable]), rest
        for i in movable:
            addition = min(reach - given[i], max(1, budget * portions[i] // mass), rest)
            given[i] = given[i] + addition
            rest = rest - addition
    return np.array(given)


def centred(rng, extent, deviation, limit, cuts=(), kind=jnp.bfloat16):
    result = jax.random.normal(rng, extent, jnp.float32) * deviation
    if len(cuts) > 0:
        result = block_levels(rng, extent, cuts, -0.22, 0.18) * result
    return jnp.clip(result, min=-limit, max=limit).astype(kind)


def noise_with(own_key, shape, deviation, reach, shards, heavy, held_as=jnp.bfloat16):
    values = deviation * jax.random.normal(own_key, shape, jnp.float32)
    if shards:
        values = values * block_levels(own_key, shape, shards, -0.22, 0.18)
    return jnp.clip(strengthened(values, jax.random.fold_in(own_key, 3), *heavy), -reach, reach).astype(held_as)


def setup_inputs(seed: int = 0) -> dict:
    splits = jax.random.split(jax.random.key(seed), 10)
    queries = centred(splits[0], (TOKENS, D), 1.0, 6.0, ((0, 16), (1, 8)))
    w_key = centred(splits[1], (E, D), E ** -0.5, 0.1875, ((1, 8),))
    w_value = centred(splits[2], (E, D), E ** -0.5, 0.1875, ((1, 8),))
    w_out = centred(splits[3], (D, D), (D // 16) ** -0.5, 0.375, ((0, 8),))
    encodings = centred(splits[4], (NBR, NT, E), 1.0, 6.0, ((0, 16), (1, 8)))
    nbr_row = plant(jax.random.randint(splits[5], (GROUPS, K), 0, NB_DEV), jax.random.fold_in(splits[5], 1), 0, NB_DEV - 1).astype(jnp.int32)
    nbr_owner_keys = jax.random.split(jax.random.fold_in(splits[6], 1), GROUPS // CH_DEV)
    nbr_owner_turns = jax.random.permutation(jax.random.fold_in(splits[6], 3), GROUPS // CH_DEV)
    nbr_owner = jax.vmap(lambda own, number: deal_out(jax.random.fold_in(splits[6], 2), own, number, CH_DEV, N_DB, K, CH_DEV, 1))(nbr_owner_keys, nbr_owner_turns).reshape((GROUPS, K))
    nbr_count = plant(jax.random.randint(splits[7], (GROUPS,), 2, K + 1), jax.random.fold_in(splits[7], 1), 2, K).astype(jnp.int32)
    grad_out = noise_with(splits[8], (TOKENS, D), 1.0, 6.0, ((0, 16), (1, 8)), (0, 1, 16, 2.0))
    return dict(queries=queries, w_key=w_key, w_value=w_value, w_out=w_out, encodings=encodings, nbr_row=nbr_row, nbr_owner=nbr_owner, nbr_count=nbr_count, grad_out=grad_out)


def rounded(value):
    return lax.optimization_barrier(value.astype(jnp.bfloat16))

def reference(queries, w_key, w_value, w_out, encodings, nbr_row, nbr_owner, nbr_count, grad_out):
    factor = 1.0 / math.sqrt(HD)
    global_rows = (nbr_owner * NB_DEV + nbr_row).astype(jnp.int32)
    query_blocks = queries.reshape(GROUPS, CL, D)
    cotangent_blocks = grad_out.reshape(GROUPS, CL, D)

    def one_group(carry, inputs):
        acc_key, acc_value, acc_out = carry
        query_group, grad_group, row_ids, count = inputs
        slots = jnp.take(encodings, row_ids, axis=0).reshape(K * NT, E)
        keys = rounded(jnp.dot(slots, w_key, preferred_element_type=jnp.float32))
        values = rounded(jnp.dot(slots, w_value, preferred_element_type=jnp.float32))
        query_heads = query_group.astype(jnp.float32).reshape(CL, HEADS, HD)
        key_heads = keys.astype(jnp.float32).reshape(K * NT, HEADS, HD)
        value_heads = values.astype(jnp.float32).reshape(K * NT, HEADS, HD)
        scores = jnp.einsum('qhd,khd->hqk', query_heads, key_heads) * factor
        live = jnp.arange(K * NT, dtype=jnp.int32) // NT < count
        expo = jnp.where(live[None, None, :], jnp.exp(scores), jnp.float32(0.0))
        probs = expo / lax.optimization_barrier(jnp.sum(expo, axis=-1, keepdims=True))
        probs_b = rounded(probs).astype(jnp.float32)
        mixed = rounded(jnp.einsum('hqk,khd->qhd', probs_b, value_heads)).reshape(CL, D)
        output = jnp.dot(mixed, w_out, preferred_element_type=jnp.float32).astype(jnp.bfloat16)
        d_mixed = rounded(jnp.dot(grad_group, w_out.T, preferred_element_type=jnp.float32))
        acc_out = acc_out + jnp.dot(mixed.T, grad_group, preferred_element_type=jnp.float32)
        d_mixed_heads = d_mixed.astype(jnp.float32).reshape(CL, HEADS, HD)
        d_probs = jnp.einsum('qhd,khd->hqk', d_mixed_heads, value_heads)
        inner = lax.optimization_barrier(jnp.sum(probs * d_probs, axis=-1, keepdims=True))
        d_scores = rounded(probs * (d_probs - inner) * factor).astype(jnp.float32)
        d_query = jnp.einsum('hqk,khd->qhd', d_scores, key_heads).astype(jnp.bfloat16).reshape(CL, D)
        d_keys = jnp.einsum('hqk,qhd->khd', d_scores, query_heads).astype(jnp.bfloat16).reshape(K * NT, D)
        d_values = jnp.einsum('hqk,qhd->khd', probs_b, d_mixed_heads).astype(jnp.bfloat16).reshape(K * NT, D)
        acc_key = acc_key + jnp.dot(slots.T, d_keys, preferred_element_type=jnp.float32)
        acc_value = acc_value + jnp.dot(slots.T, d_values, preferred_element_type=jnp.float32)
        return ((acc_key, acc_value, acc_out), (output, d_query))
    start = (jnp.zeros((E, D), jnp.float32), jnp.zeros((E, D), jnp.float32), jnp.zeros((D, D), jnp.float32))
    totals, pieces = lax.scan(one_group, start, (query_blocks, cotangent_blocks, global_rows, nbr_count))
    attended = pieces[0].reshape(TOKENS, D)
    grad_queries = pieces[1].reshape(TOKENS, D)
    return (attended, grad_queries, totals[0], totals[1], totals[2])
```

```python
import functools
import math

import jax
import jax.numpy as jnp
from jax import lax
from jax.experimental import pallas as pl
from jax.experimental.pallas import tpu as pltpu
from jax.sharding import PartitionSpec as P

HD = 128
BF = jnp.bfloat16
F32 = jnp.float32
VMEM_LIMIT = 40 * 1024 * 1024


def mm(a, b, ca, cb):
    return lax.dot_general(a, b, (((ca,), (cb,)), ((), ())), preferred_element_type=F32)


def params():
    return pltpu.CompilerParams(vmem_limit_bytes=VMEM_LIMIT)


ANY = pl.BlockSpec(memory_space=pl.ANY)
VM = pl.BlockSpec(memory_space=pltpu.VMEM)
SM = pl.BlockSpec(memory_space=pltpu.SMEM)


def pick_kernel(rows_ref, src_ref, *rest, counts):
    outs, sem = rest[: len(counts)], rest[-1]
    copies, k = [], 0
    for out, count in zip(outs, counts):
        for n in range(count):
            copies.append(pltpu.make_async_copy(src_ref.at[rows_ref[k]], out.at[n], sem.at[k]))
            k += 1
    for copy in copies:
        copy.start()
    for copy in copies:
        copy.wait()


def pick(rows, src, counts):
    item = src.shape[1:]
    return pl.pallas_call(
        functools.partial(pick_kernel, counts=counts),
        out_shape=[jax.ShapeDtypeStruct((n, *item), src.dtype) for n in counts],
        in_specs=[SM, ANY],
        out_specs=[ANY] * len(counts),
        scratch_shapes=[pltpu.SemaphoreType.DMA((sum(counts),))],
        compiler_params=params(),
    )(rows, src)


def prep_kernel(g_ref, wo_ref, q_ref, wk_ref, wv_ref, dm_ref, qt_ref, dt_ref, gc_ref):
    blocks, rows, width = g_ref.shape
    groups = qt_ref.shape[0]
    part = rows // groups
    acc = jnp.zeros((rows, width), F32)
    for j in range(blocks):
        acc += mm(g_ref[j], wo_ref[:, j * width : (j + 1) * width], 1, 1)
        half = width * blocks // gc_ref.shape[0]
        for p in range(width // half):
            gc_ref[j * (width // half) + p] = g_ref[j, :, p * half : (p + 1) * half]
    dm = acc.astype(BF)
    dm_ref[...] = dm
    for h in range(width // HD):
        cols = slice(h * HD, (h + 1) * HD)
        back_q = mm(q_ref[:, cols], wk_ref[:, cols], 1, 1).astype(BF)
        back_d = mm(dm[:, cols], wv_ref[:, cols], 1, 1).astype(BF)
        for c in range(groups):
            qt_ref[c, h * part : (h + 1) * part] = back_q[c * part : (c + 1) * part]
            dt_ref[c, h * part : (h + 1) * part] = back_d[c * part : (c + 1) * part]


def prep(g, wo, q, wk, wv, groups, db_count):
    blocks, rows, width = g.shape
    heads = width // HD
    enc = wk.shape[0]
    tall = (groups, heads * rows // groups, enc)
    return pl.pallas_call(
        prep_kernel,
        out_shape=[
            jax.ShapeDtypeStruct((rows, width), BF),
            jax.ShapeDtypeStruct(tall, BF),
            jax.ShapeDtypeStruct(tall, BF),
            jax.ShapeDtypeStruct((db_count, rows, width * blocks // db_count), BF),
        ],
        in_specs=[VM] * 5,
        out_specs=[VM] * 4,
        compiler_params=params(),
        cost_estimate=pl.CostEstimate(flops=1_000_000_000, bytes_accessed=10_000_000, transcendentals=0),
    )(g, wo, q, wk, wv)


def attn_kernel(count_ref, *refs, c, pieces, last):
    x_refs, refs = refs[:pieces], refs[pieces:]
    qt_ref, dt_ref, wk_ref, wv_ref, wo_ref = refs[:5]
    refs = refs[5:]
    if last:
        q_ref, dm_ref, t0_ref, u0_ref, mixed_ref, out_ref, gq_ref, gw_ref, x_ref, sem = refs
    else:
        mixed_ref, out_ref, gq_ref, t_ref, u_ref, x_ref, sem = refs
    slots, sub, enc = x_refs[0].shape
    copies = [
        pltpu.make_async_copy(x_refs[p], x_ref.at[pl.ds(p * slots, slots)], sem.at[p])
        for p in range(pieces)
    ]
    for copy in copies:
        copy.start()
    for copy in copies:
        copy.wait()
    factor = 1.0 / math.sqrt(HD)
    x = x_ref[...].reshape(pieces * slots * sub, enc)
    keys = x.shape[0]
    s = mm(qt_ref[c], x, 1, 1) * factor
    slot = (lax.broadcasted_iota(jnp.int32, (1, keys), 1) // sub) % slots
    expo = jnp.where(slot < count_ref[c], jnp.exp(s), 0.0)
    probs = expo / jnp.sum(expo, axis=-1, keepdims=True)
    t = mm(probs.astype(BF), x, 1, 0).astype(BF)
    width = wk_ref.shape[1]
    heads = width // HD
    part = t.shape[0] // heads
    for h in range(heads):
        cols = slice(h * HD, (h + 1) * HD)
        mixed_ref[:, cols] = mm(t[h * part : (h + 1) * part], wv_ref[:, cols], 1, 0).astype(BF)
    mixed = mixed_ref[...]
    for j in range(out_ref.shape[0]):
        out_ref[j] = mm(mixed, wo_ref[:, j * width : (j + 1) * width], 1, 0).astype(BF)
    d = mm(dt_ref[c], x, 1, 1)
    inner = jnp.sum(probs * d, axis=-1, keepdims=True)
    ds = (probs * (d - inner) * factor).astype(BF)
    u = mm(ds, x, 1, 0).astype(BF)
    for h in range(heads):
        cols = slice(h * HD, (h + 1) * HD)
        gq_ref[:, cols] = mm(u[h * part : (h + 1) * part], wk_ref[:, cols], 1, 0).astype(BF)
    if not last:
        t_ref[...] = t
        u_ref[...] = u
        return
    for h in range(heads):
        rows = slice(h * part, (h + 1) * part)
        cols = slice(h * HD, (h + 1) * HD)
        u_all = jnp.concatenate([u0_ref[rows], u[rows]], axis=0)
        t_all = jnp.concatenate([t0_ref[rows], t[rows]], axis=0)
        gw_ref[:, cols] = mm(u_all, q_ref[:, cols], 0, 0).astype(BF)
        gw_ref[:, width + h * HD : width + (h + 1) * HD] = mm(t_all, dm_ref[:, cols], 0, 0).astype(BF)


def attn(count, xs, qt, dt, wk, wv, wo, c, head_count, extra=None):
    slots, sub, enc = xs[0].shape
    width = wk.shape[1]
    heads = width // HD
    part = qt.shape[1] // heads
    last = extra is not None
    out_shape = [
        jax.ShapeDtypeStruct((part, width), BF),
        jax.ShapeDtypeStruct((head_count, part, width), BF),
        jax.ShapeDtypeStruct((part, width), BF),
    ]
    if last:
        out_shape += [jax.ShapeDtypeStruct((enc, 2 * width), BF)]
    else:
        out_shape += [jax.ShapeDtypeStruct(qt.shape[1:], BF)] * 2
    more = list(extra) if last else []
    return pl.pallas_call(
        functools.partial(attn_kernel, c=c, pieces=len(xs), last=last),
        out_shape=out_shape,
        in_specs=[SM] + [ANY] * len(xs) + [VM] * (5 + len(more)),
        out_specs=[VM] * len(out_shape),
        scratch_shapes=[
            pltpu.VMEM((len(xs) * slots, sub, enc), BF),
            pltpu.SemaphoreType.DMA((len(xs),)),
        ],
        compiler_params=params(),
        cost_estimate=pl.CostEstimate(flops=4_000_000_000, bytes_accessed=12_000_000, transcendentals=262144),
    )(count, *xs, qt, dt, wk, wv, wo, *more)


def spread_head(x, head_count):
    chips = head_count // 2

    def along(v, step):
        return lax.ppermute(
            v, "head", [(i, ((i // 2 + step) % chips) * 2 + i % 2) for i in range(head_count)]
        )

    steps = sorted(range(1, chips), key=lambda s: min(s, chips - s))
    mine = [x] + [along(x, s) for s in steps]
    other = [lax.ppermute(v, "head", [(i, i ^ 1) for i in range(head_count)]) for v in mine]
    return mine + other


def exchange(x, axis):
    return lax.all_to_all(x, axis, split_axis=0, concat_axis=0, tiled=True)


def shards(queries, w_key, w_value, w_out, encodings, nbr_row, nbr_owner, nbr_count, grad_out):
    db_count = lax.axis_size("db")
    head_count = lax.axis_size("head")
    groups, slot_count = nbr_row.shape
    tok_rows, width = queries.shape
    part = tok_rows // groups
    enc = encodings.shape[2]
    owner_ids = lax.broadcasted_iota(jnp.int32, (db_count, 1, 1), 0)
    wanted = jnp.sum(jnp.where(nbr_owner[None] == owner_ids, nbr_row[None], 0), axis=2)
    incoming = exchange(wanted, "db")
    grad_all = exchange(jnp.broadcast_to(grad_out[None], (head_count, *grad_out.shape)), "head")
    tables = pick(incoming.T.reshape(-1), encodings, (db_count,) * groups)
    received = [exchange(t, "db") for t in tables]
    dm, qt, dt, grad_cols = prep(grad_all, w_out, queries, w_key, w_value, groups, db_count)
    spread = []
    for c in range(groups):
        (mine,) = pick(nbr_owner[c], received[c], (slot_count,))
        spread.append(spread_head(mine, head_count))
    grad_tok = exchange(grad_cols, "db")
    mixed, outs, grad_q, kept = [], [], [], []
    for c in range(groups):
        last = c == groups - 1
        extra = (queries, dm, *kept) if last else None
        m, o, gq, *kept = attn(nbr_count, spread[c], qt, dt, w_key, w_value, w_out, c, head_count, extra)
        mixed.append(exchange(jnp.broadcast_to(m[None], (db_count, *m.shape)), "db"))
        outs.append(exchange(o, "head"))
        grad_q.append(gq)
    (grad_w,) = kept
    grad_w = exchange(grad_w.reshape(db_count, enc // db_count, 2 * width), "db")
    attended = jnp.concatenate(
        [jnp.sum(o.astype(F32), axis=0).astype(BF) for o in outs], axis=0
    )
    summed = jnp.sum(grad_w.astype(F32), axis=0)
    grad_tok = grad_tok.reshape(db_count, groups, part, -1)
    grad_wo = sum(
        lax.dot_general(
            mixed[c], grad_tok[:, c], (((0, 1), (0, 1)), ((), ())), preferred_element_type=F32
        )
        for c in range(groups)
    )
    return (
        attended,
        jnp.concatenate(grad_q, axis=0),
        summed[:, :width],
        summed[:, width:],
        grad_wo,
    )


def solution(mesh):
    placed = (
        P("db", "head"),
        P(None, "head"),
        P(None, "head"),
        P("head", None),
        P("db", "head", None),
        P("db", None),
        P("db", None),
        P("db"),
        P("db", "head"),
    )
    return jax.shard_map(
        shards,
        mesh=mesh,
        in_specs=placed,
        out_specs=(
            P("db", "head"),
            P("db", "head"),
            P("db", "head"),
            P("db", "head"),
            P("head", "db"),
        ),
        check_vma=False,
    )
```

```python
import functools
import math

import jax
import jax.numpy as jnp
from jax import lax
from jax.experimental import pallas as pl
from jax.experimental.pallas import tpu as pltpu
from jax.sharding import PartitionSpec as P

HD = 128
BF = jnp.bfloat16
F32 = jnp.float32
VMEM_LIMIT = 40 * 1024 * 1024


def mm(a, b, ca, cb):
    return lax.dot_general(a, b, (((ca,), (cb,)), ((), ())), preferred_element_type=F32)


def params():
    return pltpu.CompilerParams(vmem_limit_bytes=VMEM_LIMIT)


ANY = pl.BlockSpec(memory_space=pl.ANY)
VM = pl.BlockSpec(memory_space=pltpu.VMEM)
SM = pl.BlockSpec(memory_space=pltpu.SMEM)


def pick_kernel(rows_ref, src_ref, *rest, counts):
    outs, sem = rest[: len(counts)], rest[-1]
    copies, k = [], 0
    for out, count in zip(outs, counts):
        for n in range(count):
            copies.append(pltpu.make_async_copy(src_ref.at[rows_ref[k]], out.at[n], sem.at[k]))
            k += 1
    for copy in copies:
        copy.start()
    for copy in copies:
        copy.wait()


def pick(rows, src, counts):
    item = src.shape[1:]
    return pl.pallas_call(
        functools.partial(pick_kernel, counts=counts),
        out_shape=[jax.ShapeDtypeStruct((n, *item), src.dtype) for n in counts],
        in_specs=[SM, ANY],
        out_specs=[ANY] * len(counts),
        scratch_shapes=[pltpu.SemaphoreType.DMA((sum(counts),))],
        compiler_params=params(),
    )(rows, src)


def prep_kernel(at_ref, near_ref, far_ref, wo_ref, q_ref, wk_ref, wv_ref, dm_ref, qt_ref, dt_ref, gc_ref):
    chips, rows, width = near_ref.shape
    groups = qt_ref.shape[0]
    part = rows // groups
    cuts = gc_ref.shape[0] // (2 * chips)
    piece = width // cuts
    acc = jnp.zeros((rows, width), F32)
    for core, g_ref in enumerate((near_ref, far_ref)):
        for s in range(chips):
            j = lax.rem(at_ref[0] + chips - s, chips) * 2 + lax.rem(at_ref[1] + core, 2)
            cols = pl.ds(pl.multiple_of(j * width, width), width)
            acc += mm(g_ref[s], wo_ref[:, cols], 1, 1)
            for p in range(cuts):
                gc_ref[j * cuts + p] = g_ref[s, :, p * piece : (p + 1) * piece]
    dm = acc.astype(BF)
    dm_ref[...] = dm
    for h in range(width // HD):
        cols = slice(h * HD, (h + 1) * HD)
        back_q = mm(q_ref[:, cols], wk_ref[:, cols], 1, 1).astype(BF)
        back_d = mm(dm[:, cols], wv_ref[:, cols], 1, 1).astype(BF)
        for c in range(groups):
            qt_ref[c, h * part : (h + 1) * part] = back_q[c * part : (c + 1) * part]
            dt_ref[c, h * part : (h + 1) * part] = back_d[c * part : (c + 1) * part]


def prep(at, near, far, wo, q, wk, wv, groups, db_count):
    chips, rows, width = near.shape
    heads = width // HD
    enc = wk.shape[0]
    tall = (groups, heads * rows // groups, enc)
    return pl.pallas_call(
        prep_kernel,
        out_shape=[
            jax.ShapeDtypeStruct((rows, width), BF),
            jax.ShapeDtypeStruct(tall, BF),
            jax.ShapeDtypeStruct(tall, BF),
            jax.ShapeDtypeStruct((db_count, rows, 2 * chips * width // db_count), BF),
        ],
        in_specs=[SM] + [VM] * 6,
        out_specs=[VM] * 4,
        compiler_params=params(),
        cost_estimate=pl.CostEstimate(flops=1_000_000_000, bytes_accessed=10_000_000, transcendentals=0),
    )(at, near, far, wo, q, wk, wv)


def attn_kernel(at_ref, count_ref, *refs, c, pieces, last):
    x_refs, refs = refs[:pieces], refs[pieces:]
    qt_ref, dt_ref, wk_ref, wv_ref, wo_ref = refs[:5]
    refs = refs[5:]
    if last:
        q_ref, dm_ref, t0_ref, u0_ref, send_ref, keep_ref, give_ref, gq_ref, x_ref, sem = refs
    else:
        send_ref, keep_ref, give_ref, gq_ref, t_ref, u_ref, x_ref, sem = refs
    slots, sub, enc = x_refs[0].shape
    copies = [
        pltpu.make_async_copy(x_refs[p], x_ref.at[pl.ds(p * slots, slots)], sem.at[p])
        for p in range(pieces)
    ]
    for copy in copies:
        copy.start()
    for copy in copies:
        copy.wait()
    factor = 1.0 / math.sqrt(HD)
    x = x_ref[...].reshape(pieces * slots * sub, enc)
    keys = x.shape[0]
    s = mm(qt_ref[c], x, 1, 1) * factor
    slot = (lax.broadcasted_iota(jnp.int32, (1, keys), 1) // sub) % slots
    expo = jnp.where(slot < count_ref[c], jnp.exp(s), 0.0)
    probs = expo / jnp.sum(expo, axis=-1, keepdims=True)
    t = mm(probs.astype(BF), x, 1, 0).astype(BF)
    width = wk_ref.shape[1]
    heads = width // HD
    part = t.shape[0] // heads
    mixed = jnp.concatenate(
        [
            mm(t[h * part : (h + 1) * part], wv_ref[:, h * HD : (h + 1) * HD], 1, 0).astype(BF)
            for h in range(heads)
        ],
        axis=1,
    )
    db_count = send_ref.shape[0]
    for i in range(db_count):
        send_ref[i, :part] = mixed
    chips = keep_ref.shape[0]
    for core, block_ref in enumerate((keep_ref, give_ref)):
        for step in range(chips):
            j = lax.rem(at_ref[0] + step, chips) * 2 + lax.rem(at_ref[1] + core, 2)
            cols = pl.ds(pl.multiple_of(j * width, width), width)
            block_ref[step] = mm(mixed, wo_ref[:, cols], 1, 0).astype(BF)
    d = mm(dt_ref[c], x, 1, 1)
    inner = jnp.sum(probs * d, axis=-1, keepdims=True)
    ds = (probs * (d - inner) * factor).astype(BF)
    u = mm(ds, x, 1, 0).astype(BF)
    for h in range(heads):
        cols = slice(h * HD, (h + 1) * HD)
        gq_ref[:, cols] = mm(u[h * part : (h + 1) * part], wk_ref[:, cols], 1, 0).astype(BF)
    if not last:
        t_ref[...] = t
        u_ref[...] = u
        return
    for h in range(heads):
        rows = slice(h * part, (h + 1) * part)
        cols = slice(h * HD, (h + 1) * HD)
        u_all = jnp.concatenate([u0_ref[rows], u[rows]], axis=0)
        t_all = jnp.concatenate([t0_ref[rows], t[rows]], axis=0)
        sums = (mm(u_all, q_ref[:, cols], 0, 0), mm(t_all, dm_ref[:, cols], 0, 0))
        share = enc // db_count
        for k, total in enumerate(sums):
            for i in range(db_count):
                at = part + k * share
                send_ref[i, at : at + share, cols] = total[i * share : (i + 1) * share].astype(BF)


def attn(at, count, xs, qt, dt, wk, wv, wo, c, db_count, head_count, extra=None):
    slots, sub, enc = xs[0].shape
    width = wk.shape[1]
    heads = width // HD
    part = qt.shape[1] // heads
    last = extra is not None
    half = jax.ShapeDtypeStruct((head_count // 2, part, width), BF)
    sent = part + (2 * enc // db_count if last else 0)
    out_shape = [
        jax.ShapeDtypeStruct((db_count, sent, width), BF),
        half,
        half,
        jax.ShapeDtypeStruct((part, width), BF),
    ]
    if not last:
        out_shape += [jax.ShapeDtypeStruct(qt.shape[1:], BF)] * 2
    more = list(extra) if last else []
    return pl.pallas_call(
        functools.partial(attn_kernel, c=c, pieces=len(xs), last=last),
        out_shape=out_shape,
        in_specs=[SM, SM] + [ANY] * len(xs) + [VM] * (5 + len(more)),
        out_specs=[VM] * len(out_shape),
        scratch_shapes=[
            pltpu.VMEM((len(xs) * slots, sub, enc), BF),
            pltpu.SemaphoreType.DMA((len(xs),)),
        ],
        compiler_params=params(),
        cost_estimate=pl.CostEstimate(flops=4_000_000_000, bytes_accessed=12_000_000, transcendentals=262144),
    )(at, count, *xs, qt, dt, wk, wv, wo, *more)


def along(v, step, count):
    chips = count // 2
    return lax.ppermute(v, "head", [(i, ((i // 2 + step) % chips) * 2 + i % 2) for i in range(count)])


def swap(v, count):
    return lax.ppermute(v, "head", [(i, i ^ 1) for i in range(count)])


def ring_steps(count):
    chips = count // 2
    return sorted(range(1, chips), key=lambda s: min(s, chips - s))


def exchange(x, axis):
    return lax.all_to_all(x, axis, split_axis=0, concat_axis=0, tiled=True)


def after(x, *others):
    return lax.optimization_barrier((x, *others))[0]


def shards(queries, w_key, w_value, w_out, encodings, nbr_row, nbr_owner, nbr_count, grad_out):
    db_count = lax.axis_size("db")
    head_count = lax.axis_size("head")
    chips = head_count // 2
    groups, slot_count = nbr_row.shape
    tok_rows, width = queries.shape
    part = tok_rows // groups
    enc = encodings.shape[2]
    head_at = lax.axis_index("head")
    at = jnp.stack([head_at // 2, head_at % 2]).astype(jnp.int32)
    owner_ids = lax.broadcasted_iota(jnp.int32, (db_count, 1, 1), 0)
    wanted = jnp.sum(jnp.where(nbr_owner[None] == owner_ids, nbr_row[None], 0), axis=2)
    incoming = exchange(wanted, "db")
    steps = ring_steps(head_count)
    near = [grad_out] + [along(grad_out, s, head_count) for s in steps]
    near = jnp.stack([near[([0] + steps).index(s)] for s in range(chips)])
    far = swap(near, head_count)
    tables = pick(incoming.T.reshape(-1), encodings, (db_count,) * groups)
    dm, qt, dt, grad_cols = prep(at, near, far, w_out, queries, w_key, w_value, groups, db_count)
    spread, token = [], None
    for c in range(groups):
        table = tables[c] if c == 0 else after(tables[c], token, dm)
        received = exchange(table, "db")
        (mine,) = pick(nbr_owner[c], received, (slot_count,))
        token = mine
        pieces = [mine] + [along(mine, s, head_count) for s in steps]
        spread.append(pieces + [swap(v, head_count) for v in pieces])
    grad_tok = exchange(after(grad_cols, token), "db")
    sent, keep, give, grad_q, kept = [], [], [], [], []
    for c in range(groups):
        last = c == groups - 1
        extra = (queries, dm, *kept) if last else None
        m, k, g, gq, *kept = attn(
            at, nbr_count, spread[c], qt, dt, w_key, w_value, w_out, c, db_count, head_count, extra
        )
        sent.append(exchange(m, "db"))
        keep.append(k)
        give.append(g)
        grad_q.append(gq)
    keep = jnp.concatenate(keep, axis=1)
    other = swap(jnp.concatenate(give, axis=1), head_count)
    pair = (keep.astype(F32) + other.astype(F32)).astype(BF)
    terms = [pair[0]] + [along(pair[s], s, head_count) for s in steps]
    attended = sum(t.astype(F32) for t in terms).astype(BF)
    share = enc // db_count
    grad_tok = grad_tok.reshape(db_count, groups, part, -1)
    grad_wo = sum(
        lax.dot_general(
            sent[c][:, :part], grad_tok[:, c], (((0, 1), (0, 1)), ((), ())), preferred_element_type=F32
        )
        for c in range(groups)
    )
    grad_w = [
        jnp.sum(sent[-1][:, part + k * share : part + (k + 1) * share].astype(F32), axis=0)
        for k in range(2)
    ]
    return (attended, jnp.concatenate(grad_q, axis=0), *grad_w, grad_wo)


def solution(mesh):
    placed = (
        P("db", "head"),
        P(None, "head"),
        P(None, "head"),
        P("head", None),
        P("db", "head", None),
        P("db", None),
        P("db", None),
        P("db"),
        P("db", "head"),
    )
    return jax.shard_map(
        shards,
        mesh=mesh,
        in_specs=placed,
        out_specs=(
            P("db", "head"),
            P("db", "head"),
            P("db", "head"),
            P("db", "head"),
            P("head", "db"),
        ),
        check_vma=False,
    )
```

```python
import functools
import math

import jax
import jax.numpy as jnp
from jax import lax
from jax.experimental import pallas as pl
from jax.experimental.pallas import tpu as pltpu
from jax.sharding import PartitionSpec as P

HD = 128
BF = jnp.bfloat16
F32 = jnp.float32
VMEM_LIMIT = 60 * 1024 * 1024


def mm(a, b, ca, cb):
    return lax.dot_general(a, b, (((ca,), (cb,)), ((), ())), preferred_element_type=F32)


def params():
    return pltpu.CompilerParams(vmem_limit_bytes=VMEM_LIMIT)


ANY = pl.BlockSpec(memory_space=pl.ANY)
HBM = pl.BlockSpec(memory_space=pltpu.HBM)
VM = pl.BlockSpec(memory_space=pltpu.VMEM)
SM = pl.BlockSpec(memory_space=pltpu.SMEM)


def pick_kernel(rows_ref, src_ref, *rest, counts):
    outs, sem = rest[: len(counts)], rest[-1]
    copies, k = [], 0
    for out, count in zip(outs, counts):
        for n in range(count):
            copies.append(pltpu.make_async_copy(src_ref.at[rows_ref[k]], out.at[n], sem.at[k]))
            k += 1
    for copy in copies:
        copy.start()
    for copy in copies:
        copy.wait()


def pick(rows, src, counts):
    item = src.shape[1:]
    return pl.pallas_call(
        functools.partial(pick_kernel, counts=counts),
        out_shape=[jax.ShapeDtypeStruct((n, *item), src.dtype) for n in counts],
        in_specs=[SM, HBM],
        out_specs=[ANY] * len(counts),
        scratch_shapes=[pltpu.SemaphoreType.DMA((sum(counts),))],
        compiler_params=params(),
    )(rows, src)


def stream_out_weight(wo_ref, w_ref, sem):
    step = wo_ref.shape[0] // sem.shape[0]
    loads = [
        pltpu.make_async_copy(wo_ref.at[pl.ds(k * step, step)], w_ref.at[pl.ds(k * step, step)], sem.at[k])
        for k in range(sem.shape[0])
    ]
    for load in loads:
        load.start()
    return loads


def prep_kernel(at_ref, near_ref, far_ref, wo_ref, q_ref, wk_ref, wv_ref, dm_ref, qt_ref, dt_ref, gc_ref, w_ref, sem):
    chips, rows, width = near_ref.shape
    groups = qt_ref.shape[0]
    part = rows // groups
    cuts = gc_ref.shape[0] // (2 * chips)
    piece = width // cuts
    loads = stream_out_weight(wo_ref, w_ref, sem)
    acc = jnp.zeros((rows, width), F32)
    for load in loads:
        load.wait()
    for core, g_ref in enumerate((near_ref, far_ref)):
        for s in range(chips):
            j = lax.rem(at_ref[0] + chips - s, chips) * 2 + lax.rem(at_ref[1] + core, 2)
            cols = pl.ds(pl.multiple_of(j * width, width), width)
            acc += mm(g_ref[s], w_ref[:, cols], 1, 1)
            for p in range(cuts):
                gc_ref[j * cuts + p] = g_ref[s, :, p * piece : (p + 1) * piece]
    dm = acc.astype(BF)
    dm_ref[...] = dm
    for h in range(width // HD):
        cols = slice(h * HD, (h + 1) * HD)
        back_q = mm(q_ref[:, cols], wk_ref[:, cols], 1, 1).astype(BF)
        back_d = mm(dm[:, cols], wv_ref[:, cols], 1, 1).astype(BF)
        for c in range(groups):
            qt_ref[c, h * part : (h + 1) * part] = back_q[c * part : (c + 1) * part]
            dt_ref[c, h * part : (h + 1) * part] = back_d[c * part : (c + 1) * part]


def prep(at, near, far, wo, q, wk, wv, groups, db_count):
    chips, rows, width = near.shape
    heads = width // HD
    enc = wk.shape[0]
    tall = (groups, heads * rows // groups, enc)
    return pl.pallas_call(
        prep_kernel,
        out_shape=[
            jax.ShapeDtypeStruct((rows, width), BF),
            jax.ShapeDtypeStruct(tall, BF),
            jax.ShapeDtypeStruct(tall, BF),
            jax.ShapeDtypeStruct((db_count, rows, 2 * chips * width // db_count), BF),
        ],
        in_specs=[SM, VM, VM, HBM, VM, VM, VM],
        out_specs=[VM] * 4,
        scratch_shapes=[pltpu.VMEM(wo.shape, BF), pltpu.SemaphoreType.DMA((4,))],
        compiler_params=params(),
        cost_estimate=pl.CostEstimate(flops=1_000_000_000, bytes_accessed=10_000_000, transcendentals=0),
    )(at, near, far, wo, q, wk, wv)


def attn_kernel(at_ref, count_ref, *refs, c, pieces, last):
    x_refs, refs = refs[:pieces], refs[pieces:]
    qt_ref, dt_ref, wk_ref, wv_ref, wo_ref = refs[:5]
    refs = refs[5:]
    if last:
        q_ref, dm_ref, t0_ref, u0_ref, send_ref, keep_ref, give_ref, gq_ref, x_ref, w_ref, sem, w_sem = refs
    else:
        send_ref, keep_ref, give_ref, gq_ref, t_ref, u_ref, x_ref, w_ref, sem, w_sem = refs
    slots, sub, enc = x_refs[0].shape
    copies = [
        pltpu.make_async_copy(x_refs[p], x_ref.at[pl.ds(p * slots, slots)], sem.at[p])
        for p in range(pieces)
    ]
    for copy in copies:
        copy.start()
    for copy in copies:
        copy.wait()
    loads = stream_out_weight(wo_ref, w_ref, w_sem)
    factor = 1.0 / math.sqrt(HD)
    x = x_ref[...].reshape(pieces * slots * sub, enc)
    keys = x.shape[0]
    s = mm(qt_ref[c], x, 1, 1) * factor
    slot = (lax.broadcasted_iota(jnp.int32, (1, keys), 1) // sub) % slots
    expo = jnp.where(slot < count_ref[c], jnp.exp(s), 0.0)
    probs = expo / jnp.sum(expo, axis=-1, keepdims=True)
    t = mm(probs.astype(BF), x, 1, 0).astype(BF)
    width = wk_ref.shape[1]
    heads = width // HD
    part = t.shape[0] // heads
    mixed = jnp.concatenate(
        [
            mm(t[h * part : (h + 1) * part], wv_ref[:, h * HD : (h + 1) * HD], 1, 0).astype(BF)
            for h in range(heads)
        ],
        axis=1,
    )
    for load in loads:
        load.wait()
    db_count = send_ref.shape[0]
    for i in range(db_count):
        send_ref[i, :part] = mixed
    chips = keep_ref.shape[0]
    for core, block_ref in enumerate((keep_ref, give_ref)):
        for step in range(chips):
            j = lax.rem(at_ref[0] + step, chips) * 2 + lax.rem(at_ref[1] + core, 2)
            cols = pl.ds(pl.multiple_of(j * width, width), width)
            block_ref[step] = mm(mixed, w_ref[:, cols], 1, 0).astype(BF)
    d = mm(dt_ref[c], x, 1, 1)
    inner = jnp.sum(probs * d, axis=-1, keepdims=True)
    ds = (probs * (d - inner) * factor).astype(BF)
    u = mm(ds, x, 1, 0).astype(BF)
    for h in range(heads):
        cols = slice(h * HD, (h + 1) * HD)
        gq_ref[:, cols] = mm(u[h * part : (h + 1) * part], wk_ref[:, cols], 1, 0).astype(BF)
    if not last:
        t_ref[...] = t
        u_ref[...] = u
        return
    for h in range(heads):
        rows = slice(h * part, (h + 1) * part)
        cols = slice(h * HD, (h + 1) * HD)
        u_all = jnp.concatenate([u0_ref[rows], u[rows]], axis=0)
        t_all = jnp.concatenate([t0_ref[rows], t[rows]], axis=0)
        sums = (mm(u_all, q_ref[:, cols], 0, 0), mm(t_all, dm_ref[:, cols], 0, 0))
        share = enc // db_count
        for k, total in enumerate(sums):
            for i in range(db_count):
                at = part + k * share
                send_ref[i, at : at + share, cols] = total[i * share : (i + 1) * share].astype(BF)


def attn(at, count, xs, qt, dt, wk, wv, wo, c, db_count, head_count, extra=None):
    slots, sub, enc = xs[0].shape
    width = wk.shape[1]
    heads = width // HD
    part = qt.shape[1] // heads
    last = extra is not None
    half = jax.ShapeDtypeStruct((head_count // 2, part, width), BF)
    sent = part + (2 * enc // db_count if last else 0)
    out_shape = [
        jax.ShapeDtypeStruct((db_count, sent, width), BF),
        half,
        half,
        jax.ShapeDtypeStruct((part, width), BF),
    ]
    if not last:
        out_shape += [jax.ShapeDtypeStruct(qt.shape[1:], BF)] * 2
    more = list(extra) if last else []
    return pl.pallas_call(
        functools.partial(attn_kernel, c=c, pieces=len(xs), last=last),
        out_shape=out_shape,
        in_specs=[SM, SM] + [ANY] * len(xs) + [VM] * 4 + [HBM] + [VM] * len(more),
        out_specs=[VM] * len(out_shape),
        scratch_shapes=[
            pltpu.VMEM((len(xs) * slots, sub, enc), BF),
            pltpu.VMEM(wo.shape, BF),
            pltpu.SemaphoreType.DMA((len(xs),)),
            pltpu.SemaphoreType.DMA((4,)),
        ],
        compiler_params=params(),
        cost_estimate=pl.CostEstimate(flops=4_000_000_000, bytes_accessed=12_000_000, transcendentals=262144),
    )(at, count, *xs, qt, dt, wk, wv, wo, *more)


def along(v, step, count):
    chips = count // 2
    return lax.ppermute(v, "head", [(i, ((i // 2 + step) % chips) * 2 + i % 2) for i in range(count)])


def swap(v, count):
    return lax.ppermute(v, "head", [(i, i ^ 1) for i in range(count)])


def ring_steps(count):
    chips = count // 2
    return sorted(range(1, chips), key=lambda s: min(s, chips - s))


def exchange(x, axis):
    return lax.all_to_all(x, axis, split_axis=0, concat_axis=0, tiled=True)


def after(x, *others):
    return lax.optimization_barrier((x, *others))[0]


def shards(queries, w_key, w_value, w_out, encodings, nbr_row, nbr_owner, nbr_count, grad_out):
    db_count = lax.axis_size("db")
    head_count = lax.axis_size("head")
    chips = head_count // 2
    groups, slot_count = nbr_row.shape
    tok_rows, width = queries.shape
    part = tok_rows // groups
    enc = encodings.shape[2]
    head_at = lax.axis_index("head")
    at = jnp.stack([head_at // 2, head_at % 2]).astype(jnp.int32)
    owner_ids = lax.broadcasted_iota(jnp.int32, (db_count, 1, 1), 0)
    wanted = jnp.sum(jnp.where(nbr_owner[None] == owner_ids, nbr_row[None], 0), axis=2)
    incoming = exchange(wanted, "db")
    steps = ring_steps(head_count)
    tables = pick(incoming.T.reshape(-1), encodings, (db_count,) * groups)
    near = [grad_out] + [along(after(grad_out, wanted), s, head_count) for s in steps]
    near = lax.optimization_barrier((*near, *tables))[: len(near)]
    near = jnp.stack([near[([0] + steps).index(s)] for s in range(chips)])
    far = swap(near, head_count)
    dm, qt, dt, grad_cols = prep(at, near, far, w_out, queries, w_key, w_value, groups, db_count)
    ring, tokens = [], []
    for c in range(groups):
        received = exchange(tables[c] if c == 0 else after(tables[c], *tokens), "db")
        if c == 0:
            received = after(received, dm)
        else:
            received, *ring[-1] = lax.optimization_barrier((received, *ring[-1]))
        (token,) = pick(nbr_owner[c], received, (slot_count,))
        tokens.append(token)
        ring.append([token] + [along(token, s, head_count) for s in steps])
    token = tokens[-1]
    spread = []
    for pieces in ring:
        spread.append([*pieces, *(swap(v, head_count) for v in pieces)])
    grad_tok = exchange(after(grad_cols, token), "db")
    sent, keep, give, grad_q, kept = [], [], [], [], []
    for c in range(groups):
        last = c == groups - 1
        extra = (queries, dm, *kept) if last else None
        m, k, g, gq, *kept = attn(
            at, nbr_count, spread[c], qt, dt, w_key, w_value, w_out, c, db_count, head_count, extra
        )
        hold = (grad_tok, *ring[-1]) if c == 0 else sent
        sent.append(exchange(after(m, *hold), "db"))
        keep.append(k)
        give.append(g)
        grad_q.append(gq)
    keep = jnp.concatenate(keep, axis=1)
    other = swap(jnp.concatenate(give, axis=1), head_count)
    pair = (keep.astype(F32) + other.astype(F32)).astype(BF)
    terms = [pair[0]] + [along(pair[s], s, head_count) for s in steps]
    attended = sum(t.astype(F32) for t in terms).astype(BF)
    share = enc // db_count
    grad_tok = grad_tok.reshape(db_count, groups, part, -1)
    grad_wo = sum(
        lax.dot_general(
            sent[c][:, :part], grad_tok[:, c], (((0, 1), (0, 1)), ((), ())), preferred_element_type=F32
        )
        for c in range(groups)
    )
    grad_w = [
        jnp.sum(sent[-1][:, part + k * share : part + (k + 1) * share].astype(F32), axis=0)
        for k in range(2)
    ]
    return (attended, jnp.concatenate(grad_q, axis=0), *grad_w, grad_wo)


def solution(mesh):
    placed = (
        P("db", "head"),
        P(None, "head"),
        P(None, "head"),
        P("head", None),
        P("db", "head", None),
        P("db", None),
        P("db", None),
        P("db"),
        P("db", "head"),
    )
    return jax.shard_map(
        shards,
        mesh=mesh,
        in_specs=placed,
        out_specs=(
            P("db", "head"),
            P("db", "head"),
            P("db", "head"),
            P("db", "head"),
            P("head", "db"),
        ),
        check_vma=False,
    )
```

```python
import functools
import math

import jax
import jax.numpy as jnp
from jax import lax
from jax.experimental import pallas as pl
from jax.experimental.pallas import tpu as pltpu
from jax.sharding import PartitionSpec as P

HD = 128
BF = jnp.bfloat16
F32 = jnp.float32
VMEM_LIMIT = 60 * 1024 * 1024


def mm(a, b, ca, cb):
    return lax.dot_general(a, b, (((ca,), (cb,)), ((), ())), preferred_element_type=F32)


def params():
    return pltpu.CompilerParams(vmem_limit_bytes=VMEM_LIMIT)


ANY = pl.BlockSpec(memory_space=pl.ANY)
HBM = pl.BlockSpec(memory_space=pltpu.HBM)
VM = pl.BlockSpec(memory_space=pltpu.VMEM)
SM = pl.BlockSpec(memory_space=pltpu.SMEM)


def pick_kernel(rows_ref, src_ref, *rest, counts):
    outs, sem = rest[: len(counts)], rest[-1]
    copies, k = [], 0
    for out, count in zip(outs, counts):
        for n in range(count):
            copies.append(pltpu.make_async_copy(src_ref.at[rows_ref[k]], out.at[n], sem.at[k]))
            k += 1
    for copy in copies:
        copy.start()
    for copy in copies:
        copy.wait()


def pick(rows, src, counts, place):
    item = src.shape[1:]
    return pl.pallas_call(
        functools.partial(pick_kernel, counts=counts),
        out_shape=[jax.ShapeDtypeStruct((n, *item), src.dtype) for n in counts],
        in_specs=[SM, place],
        out_specs=[VM] * len(counts),
        scratch_shapes=[pltpu.SemaphoreType.DMA((sum(counts),))],
        compiler_params=params(),
    )(rows, src)


def start_loads(pairs, sem, first=0):
    loads = [pltpu.make_async_copy(src, dst, sem.at[first + k]) for k, (src, dst) in enumerate(pairs)]
    for load in loads:
        load.start()
    return loads


def wait_all(copies):
    for copy in copies:
        copy.wait()


def row_blocks(src, dst, count):
    step = src.shape[0] // count
    return [(src.at[pl.ds(k * step, step)], dst.at[pl.ds(k * step, step)]) for k in range(count)]


def prep_kernel(at_ref, *refs):
    near_in, far_in, wo_in, q_in, wk_in, wv_in = refs[:6]
    dm_ref, qt_ref, dt_ref, gc_ref = refs[6:10]
    near_ref, far_ref, wo_ref, q_ref, wk_ref, wv_ref, sem = refs[10:]
    chips, rows, width = near_ref.shape
    groups = qt_ref.shape[0]
    part = rows // groups
    heads = width // HD
    cuts = gc_ref.shape[0] // (2 * chips)
    piece = width // cuts
    first = start_loads([(q_in, q_ref), (wk_in, wk_ref), (near_in, near_ref), (far_in, far_ref)], sem)
    blocks = start_loads(row_blocks(wo_in, wo_ref, heads), sem, 4)
    late = start_loads([(wv_in, wv_ref)], sem, 4 + heads)

    def split(ref, h, value):
        for c in range(groups):
            ref[c, h * part : (h + 1) * part] = value[c * part : (c + 1) * part].astype(BF)

    wait_all(first[:2])
    for h in range(heads):
        cols = slice(h * HD, (h + 1) * HD)
        split(qt_ref, h, mm(q_ref[:, cols], wk_ref[:, cols], 1, 1))
    wait_all(first[2:])
    wait_all(blocks)
    acc = jnp.zeros((rows, width), F32)
    for core, g_ref in enumerate((near_ref, far_ref)):
        for s in range(chips):
            j = lax.rem(at_ref[0] + chips - s, chips) * 2 + lax.rem(at_ref[1] + core, 2)
            cols = pl.ds(pl.multiple_of(j * width, width), width)
            acc += mm(g_ref[s], wo_ref[:, cols], 1, 1)
            for p in range(cuts):
                gc_ref[j * cuts + p] = g_ref[s, :, p * piece : (p + 1) * piece]
    dm = acc.astype(BF)
    dm_ref[...] = dm
    wait_all(late)
    for h in range(heads):
        cols = slice(h * HD, (h + 1) * HD)
        split(dt_ref, h, mm(dm[:, cols], wv_ref[:, cols], 1, 1))


def prep(at, near, far, wo, q, wk, wv, groups, db_count):
    chips, rows, width = near.shape
    heads = width // HD
    enc = wk.shape[0]
    tall = (groups, heads * rows // groups, enc)
    operands = (near, far, wo, q, wk, wv)
    return pl.pallas_call(
        prep_kernel,
        out_shape=[
            jax.ShapeDtypeStruct((rows, width), BF),
            jax.ShapeDtypeStruct(tall, BF),
            jax.ShapeDtypeStruct(tall, BF),
            jax.ShapeDtypeStruct((db_count, rows, 2 * chips * width // db_count), BF),
        ],
        in_specs=[SM] + [HBM] * 6,
        out_specs=[VM] * 4,
        scratch_shapes=[pltpu.VMEM(v.shape, BF) for v in operands]
        + [pltpu.SemaphoreType.DMA((5 + heads,))],
        compiler_params=params(),
        cost_estimate=pl.CostEstimate(flops=1_000_000_000, bytes_accessed=10_000_000, transcendentals=0),
    )(at, *operands)


def attn_kernel(at_ref, count_ref, *refs, c, pieces, last):
    x_in, refs = refs[:pieces], refs[pieces:]
    more = 9 if last else 5
    ins, refs = refs[:more], refs[more:]
    outs = 4 if last else 6
    send_ref, keep_ref, give_ref, gq_ref, *tu_refs = refs[:outs]
    x_ref, mixed_ref, qt_ref, dt_ref, wk_ref, wv_ref, wo_ref, *refs = refs[outs:]
    sem = refs[-1]
    slots, sub, enc = x_in[0].shape
    qt_in, dt_in, wk_in, wv_in, wo_in = ins[:5]
    chips, part, width = keep_ref.shape
    heads = width // HD
    db_count = send_ref.shape[0]
    used = 0

    def start(pairs):
        nonlocal used
        loads = start_loads(pairs, sem, used)
        used += len(pairs)
        return loads

    x_loads = start(
        [(qt_in.at[c], qt_ref)]
        + [(x_in[p], x_ref.at[pl.ds(p * slots, slots)]) for p in range(pieces)]
    )
    wv_loads = start([(wv_in, wv_ref)])
    wo_loads = start(row_blocks(wo_in, wo_ref, 4))
    dt_loads = start([(dt_in.at[c], dt_ref)])
    wk_loads = start([(wk_in, wk_ref)])
    if last:
        q_ref, dm_ref, t0_ref, u0_ref, gw_ref = refs[:5]
        last_loads = start(list(zip(ins[5:], (q_ref, dm_ref, t0_ref, u0_ref))))
    factor = 1.0 / math.sqrt(HD)
    wait_all(x_loads)
    x = x_ref[...].reshape(pieces * slots * sub, enc)
    keys = x.shape[0]
    s = mm(qt_ref[...], x, 1, 1) * factor
    slot = (lax.broadcasted_iota(jnp.int32, (1, keys), 1) // sub) % slots
    expo = jnp.where(slot < count_ref[c], jnp.exp(s), 0.0)
    probs = expo / jnp.sum(expo, axis=-1, keepdims=True)
    t = mm(probs.astype(BF), x, 1, 0).astype(BF)
    wait_all(wv_loads)
    for h in range(heads):
        cols = slice(h * HD, (h + 1) * HD)
        mixed_ref[:, cols] = mm(t[h * part : (h + 1) * part], wv_ref[:, cols], 1, 0).astype(BF)
    stores = start([(mixed_ref, send_ref.at[i, pl.ds(0, part)]) for i in range(db_count)])
    wait_all(dt_loads)
    d = mm(dt_ref[...], x, 1, 1)
    inner = jnp.sum(probs * d, axis=-1, keepdims=True)
    ds = (probs * (d - inner) * factor).astype(BF)
    u = mm(ds, x, 1, 0).astype(BF)
    wait_all(wk_loads)
    if last:
        wait_all(last_loads)
        share = enc // db_count
        for h in range(heads):
            rows = slice(h * part, (h + 1) * part)
            cols = slice(h * HD, (h + 1) * HD)
            u_all = jnp.concatenate([u0_ref[rows], u[rows]], axis=0)
            t_all = jnp.concatenate([t0_ref[rows], t[rows]], axis=0)
            sums = (mm(u_all, q_ref[:, cols], 0, 0), mm(t_all, dm_ref[:, cols], 0, 0))
            for k, total in enumerate(sums):
                for i in range(db_count):
                    gw_ref[i, k * share : (k + 1) * share, cols] = total[
                        i * share : (i + 1) * share
                    ].astype(BF)
        stores += start(
            [(gw_ref.at[i], send_ref.at[i, pl.ds(part, 2 * share)]) for i in range(db_count)]
        )
    else:
        for ref, value in zip(tu_refs, (t, u)):
            ref[...] = value
    for h in range(heads):
        cols = slice(h * HD, (h + 1) * HD)
        gq_ref[:, cols] = mm(u[h * part : (h + 1) * part], wk_ref[:, cols], 1, 0).astype(BF)
    wait_all(wo_loads)
    mixed = mixed_ref[...]
    for core, block_ref in enumerate((keep_ref, give_ref)):
        for step in range(chips):
            j = lax.rem(at_ref[0] + step, chips) * 2 + lax.rem(at_ref[1] + core, 2)
            cols = pl.ds(pl.multiple_of(j * width, width), width)
            block_ref[step] = mm(mixed, wo_ref[:, cols], 1, 0).astype(BF)
    wait_all(stores)


def attn(at, count, xs, qt, dt, wk, wv, wo, c, db_count, head_count, extra=None):
    slots, sub, enc = xs[0].shape
    width = wk.shape[1]
    heads = width // HD
    part = qt.shape[1] // heads
    last = extra is not None
    half = jax.ShapeDtypeStruct((head_count // 2, part, width), BF)
    grown = 2 * enc // db_count
    out_shape = [
        jax.ShapeDtypeStruct((db_count, part + (grown if last else 0), width), BF),
        half,
        half,
        jax.ShapeDtypeStruct((part, width), BF),
    ]
    more = list(extra) if last else []
    held = [(len(xs) * slots, sub, enc), (part, width), qt.shape[1:], dt.shape[1:]]
    held += [v.shape for v in (wk, wv, wo, *more)]
    copies = len(xs) + 8 + len(more) + db_count
    if last:
        held += [(db_count, grown, width)]
        copies += db_count
    else:
        out_shape += [jax.ShapeDtypeStruct(qt.shape[1:], BF)] * 2
    return pl.pallas_call(
        functools.partial(attn_kernel, c=c, pieces=len(xs), last=last),
        out_shape=out_shape,
        in_specs=[SM, SM] + [HBM] * (len(xs) + 5 + len(more)),
        out_specs=[HBM] + [VM] * (len(out_shape) - 1),
        scratch_shapes=[pltpu.VMEM(shape, BF) for shape in held] + [pltpu.SemaphoreType.DMA((copies,))],
        compiler_params=params(),
        cost_estimate=pl.CostEstimate(flops=4_000_000_000, bytes_accessed=12_000_000, transcendentals=262144),
    )(at, count, *xs, qt, dt, wk, wv, wo, *more)


def along(v, step, count):
    chips = count // 2
    return lax.ppermute(v, "head", [(i, ((i // 2 + step) % chips) * 2 + i % 2) for i in range(count)])


def swap(v, count):
    return lax.ppermute(v, "head", [(i, i ^ 1) for i in range(count)])


def ring_steps(count):
    chips = count // 2
    return sorted(range(1, chips), key=lambda s: min(s, chips - s))


def exchange(x, axis):
    return lax.all_to_all(x, axis, split_axis=0, concat_axis=0, tiled=True)


def after(x, *others):
    return lax.optimization_barrier((x, *others))[0]


def shards(queries, w_key, w_value, w_out, encodings, nbr_row, nbr_owner, nbr_count, grad_out):
    db_count = lax.axis_size("db")
    head_count = lax.axis_size("head")
    chips = head_count // 2
    groups, slot_count = nbr_row.shape
    tok_rows, width = queries.shape
    part = tok_rows // groups
    enc = encodings.shape[2]
    head_at = lax.axis_index("head")
    at = jnp.stack([head_at // 2, head_at % 2]).astype(jnp.int32)
    owner_ids = lax.broadcasted_iota(jnp.int32, (db_count, 1, 1), 0)
    wanted = jnp.sum(jnp.where(nbr_owner[None] == owner_ids, nbr_row[None], 0), axis=2)
    incoming = exchange(wanted, "db")
    steps = ring_steps(head_count)
    (table,) = pick(incoming.reshape(-1), encodings, (db_count * groups,), HBM)
    near = [grad_out] + [along(after(grad_out, wanted), s, head_count) for s in steps]
    near = lax.optimization_barrier((*near, table))[:-1]
    near = jnp.stack([near[([0] + steps).index(s)] for s in range(chips)])
    far = swap(near, head_count)
    dm, qt, dt, grad_cols = prep(at, near, far, w_out, queries, w_key, w_value, groups, db_count)
    received = after(exchange(table, "db"), dm)
    rows = nbr_owner * groups + lax.broadcasted_iota(jnp.int32, nbr_owner.shape, 0)
    mine = pick(rows.reshape(-1), received, (slot_count,) * groups, ANY)
    token = mine[0]
    ring = []
    for c in range(groups):
        held = mine[c] if c == 0 else after(mine[c], *ring[-1])
        ring.append([held] + [along(held, s, head_count) for s in steps])
    spread = []
    for pieces in ring:
        spread.append([*pieces, *(swap(v, head_count) for v in pieces)])
    grad_tok = exchange(after(grad_cols, token), "db")
    sent, keep, give, grad_q, kept = [], [], [], [], []
    for c in range(groups):
        last = c == groups - 1
        extra = (queries, dm, *kept) if last else None
        m, k, g, gq, *kept = attn(
            at, nbr_count, spread[c], qt, dt, w_key, w_value, w_out, c, db_count, head_count, extra
        )
        hold = (grad_tok, *ring[-1]) if c == 0 else sent
        sent.append(exchange(after(m, *hold), "db"))
        keep.append(k)
        give.append(g)
        grad_q.append(gq)
    keep = jnp.concatenate(keep, axis=1)
    other = swap(jnp.concatenate(give, axis=1), head_count)
    pair = (keep.astype(F32) + other.astype(F32)).astype(BF)
    terms = [pair[0]] + [along(pair[s], s, head_count) for s in steps]
    attended = sum(t.astype(F32) for t in terms).astype(BF)
    share = enc // db_count
    grad_tok = grad_tok.reshape(db_count, groups, part, -1)
    grad_wo = sum(
        lax.dot_general(
            sent[c][:, :part], grad_tok[:, c], (((0, 1), (0, 1)), ((), ())), preferred_element_type=F32
        )
        for c in range(groups)
    )
    grad_w = [
        jnp.sum(sent[-1][:, part + k * share : part + (k + 1) * share].astype(F32), axis=0)
        for k in range(2)
    ]
    return (attended, jnp.concatenate(grad_q, axis=0), *grad_w, grad_wo)


def solution(mesh):
    placed = (
        P("db", "head"),
        P(None, "head"),
        P(None, "head"),
        P("head", None),
        P("db", "head", None),
        P("db", None),
        P("db", None),
        P("db"),
        P("db", "head"),
    )
    return jax.shard_map(
        shards,
        mesh=mesh,
        in_specs=placed,
        out_specs=(
            P("db", "head"),
            P("db", "head"),
            P("db", "head"),
            P("db", "head"),
            P("head", "db"),
        ),
        check_vma=False,
    )
```

```python
import functools
import math

import jax
import jax.numpy as jnp
from jax import lax
from jax.experimental import pallas as pl
from jax.experimental.pallas import tpu as pltpu
from jax.sharding import PartitionSpec as P

HD = 128
BF = jnp.bfloat16
F32 = jnp.float32
VMEM_LIMIT = 60 * 1024 * 1024
SMALL_LIMIT = 8 * 1024 * 1024


def mm(a, b, ca, cb):
    return lax.dot_general(a, b, (((ca,), (cb,)), ((), ())), preferred_element_type=F32)


def params():
    return pltpu.CompilerParams(vmem_limit_bytes=VMEM_LIMIT)


ANY = pl.BlockSpec(memory_space=pl.ANY)
HBM = pl.BlockSpec(memory_space=pltpu.HBM)
VM = pl.BlockSpec(memory_space=pltpu.VMEM)
SM = pl.BlockSpec(memory_space=pltpu.SMEM)


def pick_kernel(rows_ref, src_ref, *rest, row_of, count):
    *outs, held, load_sem, store_sem = rest
    places = [out.at[n] for out in outs for n in range(out.shape[0])]
    loads = [
        pltpu.make_async_copy(src_ref.at[row_of(rows_ref, k)], held.at[k], load_sem.at[k])
        for k in range(count)
    ]
    stores = [pltpu.make_async_copy(held.at[k], places[k], store_sem.at[k]) for k in range(count)]
    for load in loads:
        load.start()
    for load, store in zip(loads, stores):
        load.wait()
        store.start()
    for store in stores:
        store.wait()


def pick(rows, row_of, src, counts, place, limit):
    item = src.shape[1:]
    total = sum(counts)
    return pl.pallas_call(
        functools.partial(pick_kernel, row_of=row_of, count=total),
        out_shape=[jax.ShapeDtypeStruct((n, *item), src.dtype) for n in counts],
        in_specs=[SM, place],
        out_specs=[ANY] * len(counts),
        scratch_shapes=[
            pltpu.VMEM((total, *item), src.dtype),
            pltpu.SemaphoreType.DMA((total,)),
            pltpu.SemaphoreType.DMA((total,)),
        ],
        compiler_params=pltpu.CompilerParams(vmem_limit_bytes=limit),
    )(rows, src)


def start_loads(pairs, sem, first=0):
    loads = [pltpu.make_async_copy(src, dst, sem.at[first + k]) for k, (src, dst) in enumerate(pairs)]
    for load in loads:
        load.start()
    return loads


def wait_all(copies):
    for copy in copies:
        copy.wait()


def row_blocks(src, dst, count):
    step = src.shape[0] // count
    return [(src.at[pl.ds(k * step, step)], dst.at[pl.ds(k * step, step)]) for k in range(count)]


def prep_kernel(at_ref, *refs):
    near_in, far_in, wo_in, q_in, wk_in, wv_in = refs[:6]
    dm_ref, qt_ref, dt_ref, gc_ref = refs[6:10]
    near_ref, far_ref, wo_ref, q_ref, wk_ref, wv_ref, sem = refs[10:]
    chips, rows, width = near_ref.shape
    groups = qt_ref.shape[0]
    part = rows // groups
    heads = width // HD
    cuts = gc_ref.shape[0] // (2 * chips)
    piece = width // cuts
    first = start_loads([(q_in, q_ref), (wk_in, wk_ref), (near_in, near_ref), (far_in, far_ref)], sem)
    blocks = start_loads(row_blocks(wo_in, wo_ref, heads), sem, 4)
    late = start_loads([(wv_in, wv_ref)], sem, 4 + heads)

    def split(ref, h, value):
        for c in range(groups):
            ref[c, h * part : (h + 1) * part] = value[c * part : (c + 1) * part].astype(BF)

    wait_all(first[:2])
    for h in range(heads):
        cols = slice(h * HD, (h + 1) * HD)
        split(qt_ref, h, mm(q_ref[:, cols], wk_ref[:, cols], 1, 1))
    wait_all(first[2:])
    wait_all(blocks)
    acc = jnp.zeros((rows, width), F32)
    for core, g_ref in enumerate((near_ref, far_ref)):
        for s in range(chips):
            j = lax.rem(at_ref[0] + chips - s, chips) * 2 + lax.rem(at_ref[1] + core, 2)
            cols = pl.ds(pl.multiple_of(j * width, width), width)
            acc += mm(g_ref[s], wo_ref[:, cols], 1, 1)
            for p in range(cuts):
                gc_ref[j * cuts + p] = g_ref[s, :, p * piece : (p + 1) * piece]
    dm = acc.astype(BF)
    dm_ref[...] = dm
    wait_all(late)
    for h in range(heads):
        cols = slice(h * HD, (h + 1) * HD)
        split(dt_ref, h, mm(dm[:, cols], wv_ref[:, cols], 1, 1))


def prep(at, near, far, wo, q, wk, wv, groups, db_count):
    chips, rows, width = near.shape
    heads = width // HD
    enc = wk.shape[0]
    tall = (groups, heads * rows // groups, enc)
    operands = (near, far, wo, q, wk, wv)
    return pl.pallas_call(
        prep_kernel,
        out_shape=[
            jax.ShapeDtypeStruct((rows, width), BF),
            jax.ShapeDtypeStruct(tall, BF),
            jax.ShapeDtypeStruct(tall, BF),
            jax.ShapeDtypeStruct((db_count, rows, 2 * chips * width // db_count), BF),
        ],
        in_specs=[SM] + [HBM] * 6,
        out_specs=[VM] * 4,
        scratch_shapes=[pltpu.VMEM(v.shape, BF) for v in operands]
        + [pltpu.SemaphoreType.DMA((5 + heads,))],
        compiler_params=params(),
        cost_estimate=pl.CostEstimate(flops=1_000_000_000, bytes_accessed=10_000_000, transcendentals=0),
    )(at, *operands)


def attn_kernel(at_ref, count_ref, *refs, c, pieces, last):
    x_in, refs = refs[:pieces], refs[pieces:]
    more = 9 if last else 5
    ins, refs = refs[:more], refs[more:]
    outs = 4 if last else 6
    send_ref, keep_ref, give_ref, gq_ref, *tu_refs = refs[:outs]
    x_ref, mixed_ref, qt_ref, dt_ref, wk_ref, wv_ref, wo_ref, *refs = refs[outs:]
    sem = refs[-1]
    slots, sub, enc = x_in[0].shape
    qt_in, dt_in, wk_in, wv_in, wo_in = ins[:5]
    chips, part, width = keep_ref.shape
    heads = width // HD
    db_count = send_ref.shape[0]
    used = 0

    def start(pairs):
        nonlocal used
        loads = start_loads(pairs, sem, used)
        used += len(pairs)
        return loads

    x_loads = start(
        [(qt_in.at[c], qt_ref)]
        + [(x_in[p], x_ref.at[pl.ds(p * slots, slots)]) for p in range(pieces)]
    )
    wait_all(x_loads)
    wv_loads = start([(wv_in, wv_ref)])
    dt_loads = start([(dt_in.at[c], dt_ref)])
    wk_loads = start([(wk_in, wk_ref)])
    if last:
        q_ref, dm_ref, t0_ref, u0_ref, gw_ref = refs[:5]
        last_loads = start(list(zip(ins[5:], (q_ref, dm_ref, t0_ref, u0_ref))))
    wo_loads = start(row_blocks(wo_in, wo_ref, 4))
    factor = 1.0 / math.sqrt(HD)
    x = x_ref[...].reshape(pieces * slots * sub, enc)
    keys = x.shape[0]
    s = mm(qt_ref[...], x, 1, 1) * factor
    slot = (lax.broadcasted_iota(jnp.int32, (1, keys), 1) // sub) % slots
    expo = jnp.where(slot < count_ref[c], jnp.exp(s), 0.0)
    probs = expo / jnp.sum(expo, axis=-1, keepdims=True)
    t = mm(probs.astype(BF), x, 1, 0).astype(BF)
    wait_all(wv_loads)
    for h in range(heads):
        cols = slice(h * HD, (h + 1) * HD)
        mixed_ref[:, cols] = mm(t[h * part : (h + 1) * part], wv_ref[:, cols], 1, 0).astype(BF)
    stores = start([(mixed_ref, send_ref.at[i, pl.ds(0, part)]) for i in range(db_count)])
    wait_all(dt_loads)
    d = mm(dt_ref[...], x, 1, 1)
    inner = jnp.sum(probs * d, axis=-1, keepdims=True)
    ds = (probs * (d - inner) * factor).astype(BF)
    u = mm(ds, x, 1, 0).astype(BF)
    wait_all(wk_loads)
    if last:
        wait_all(last_loads)
        share = enc // db_count
        for h in range(heads):
            rows = slice(h * part, (h + 1) * part)
            cols = slice(h * HD, (h + 1) * HD)
            u_all = jnp.concatenate([u0_ref[rows], u[rows]], axis=0)
            t_all = jnp.concatenate([t0_ref[rows], t[rows]], axis=0)
            sums = (mm(u_all, q_ref[:, cols], 0, 0), mm(t_all, dm_ref[:, cols], 0, 0))
            for k, total in enumerate(sums):
                for i in range(db_count):
                    gw_ref[i, k * share : (k + 1) * share, cols] = total[
                        i * share : (i + 1) * share
                    ].astype(BF)
        stores += start(
            [(gw_ref.at[i], send_ref.at[i, pl.ds(part, 2 * share)]) for i in range(db_count)]
        )
    else:
        for ref, value in zip(tu_refs, (t, u)):
            ref[...] = value
    for h in range(heads):
        cols = slice(h * HD, (h + 1) * HD)
        gq_ref[:, cols] = mm(u[h * part : (h + 1) * part], wk_ref[:, cols], 1, 0).astype(BF)
    wait_all(wo_loads)
    mixed = mixed_ref[...]
    for core, block_ref in enumerate((keep_ref, give_ref)):
        for step in range(chips):
            j = lax.rem(at_ref[0] + step, chips) * 2 + lax.rem(at_ref[1] + core, 2)
            cols = pl.ds(pl.multiple_of(j * width, width), width)
            block_ref[step] = mm(mixed, wo_ref[:, cols], 1, 0).astype(BF)
    wait_all(stores)


def attn(at, count, xs, qt, dt, wk, wv, wo, c, db_count, head_count, extra=None):
    slots, sub, enc = xs[0].shape
    width = wk.shape[1]
    heads = width // HD
    part = qt.shape[1] // heads
    last = extra is not None
    half = jax.ShapeDtypeStruct((head_count // 2, part, width), BF)
    grown = 2 * enc // db_count
    out_shape = [
        jax.ShapeDtypeStruct((db_count, part + (grown if last else 0), width), BF),
        half,
        half,
        jax.ShapeDtypeStruct((part, width), BF),
    ]
    more = list(extra) if last else []
    held = [(len(xs) * slots, sub, enc), (part, width), qt.shape[1:], dt.shape[1:]]
    held += [v.shape for v in (wk, wv, wo, *more)]
    copies = len(xs) + 8 + len(more) + db_count
    if last:
        held += [(db_count, grown, width)]
        copies += db_count
    else:
        out_shape += [jax.ShapeDtypeStruct(qt.shape[1:], BF)] * 2
    return pl.pallas_call(
        functools.partial(attn_kernel, c=c, pieces=len(xs), last=last),
        out_shape=out_shape,
        in_specs=[SM, SM] + [HBM] * (len(xs) + 5 + len(more)),
        out_specs=[HBM] + [VM] * (len(out_shape) - 1),
        scratch_shapes=[pltpu.VMEM(shape, BF) for shape in held] + [pltpu.SemaphoreType.DMA((copies,))],
        compiler_params=params(),
        cost_estimate=pl.CostEstimate(flops=4_000_000_000, bytes_accessed=12_000_000, transcendentals=262144),
    )(at, count, *xs, qt, dt, wk, wv, wo, *more)


def along(v, step, count):
    chips = count // 2
    return lax.ppermute(v, "head", [(i, ((i // 2 + step) % chips) * 2 + i % 2) for i in range(count)])


def swap(v, count):
    return lax.ppermute(v, "head", [(i, i ^ 1) for i in range(count)])


def ring_steps(count):
    chips = count // 2
    return sorted(range(1, chips), key=lambda s: min(s, chips - s))


def exchange(x, axis):
    return lax.all_to_all(x, axis, split_axis=0, concat_axis=0, tiled=True)


def after(x, *others):
    return lax.optimization_barrier((x, *others))[0]


def shards(queries, w_key, w_value, w_out, encodings, nbr_row, nbr_owner, nbr_count, grad_out):
    db_count = lax.axis_size("db")
    head_count = lax.axis_size("head")
    chips = head_count // 2
    groups, slot_count = nbr_row.shape
    tok_rows, width = queries.shape
    part = tok_rows // groups
    enc = encodings.shape[2]
    head_at = lax.axis_index("head")
    at = jnp.stack([head_at // 2, head_at % 2]).astype(jnp.int32)
    owner_ids = lax.broadcasted_iota(jnp.int32, (db_count, 1, 1, 1), 0)
    wanted = jnp.sum(jnp.where(nbr_owner[None, None] == owner_ids, nbr_row[None, None], 0), axis=3)
    incoming = exchange(wanted, "db")
    steps = ring_steps(head_count)
    (table,) = pick(
        incoming,
        lambda ref, k: ref[k // groups, 0, k % groups],
        encodings,
        (db_count * groups,),
        HBM,
        VMEM_LIMIT,
    )
    received = exchange(table, "db")
    mine = pick(
        nbr_owner,
        lambda ref, k: ref[k // slot_count, k % slot_count] * groups + k // slot_count,
        received,
        (slot_count,) * groups,
        ANY,
        SMALL_LIMIT,
    )
    token = mine[0]
    near = [grad_out] + [along(after(grad_out, table), s, head_count) for s in steps]
    near = jnp.stack([near[([0] + steps).index(s)] for s in range(chips)])
    far = swap(near, head_count)
    dm, qt, dt, grad_cols = prep(at, near, far, w_out, queries, w_key, w_value, groups, db_count)
    ring = []
    for c in range(groups):
        held = mine[c] if c == 0 else after(mine[c], *ring[-1])
        ring.append([held] + [along(held, s, head_count) for s in steps])
    spread = []
    for pieces in ring:
        spread.append([*pieces, *(swap(v, head_count) for v in pieces)])
    grad_tok = exchange(after(grad_cols, token), "db")
    sent, keep, give, grad_q, kept = [], [], [], [], []
    for c in range(groups):
        last = c == groups - 1
        extra = (queries, dm, *kept) if last else None
        m, k, g, gq, *kept = attn(
            at, nbr_count, spread[c], qt, dt, w_key, w_value, w_out, c, db_count, head_count, extra
        )
        hold = (grad_tok, *ring[-1]) if c == 0 else sent
        sent.append(exchange(after(m, *hold), "db"))
        keep.append(k)
        give.append(g)
        grad_q.append(gq)
    keep = jnp.concatenate(keep, axis=1)
    other = swap(jnp.concatenate(give, axis=1), head_count)
    pair = (keep.astype(F32) + other.astype(F32)).astype(BF)
    terms = [pair[0]] + [along(pair[s], s, head_count) for s in steps]
    attended = sum(t.astype(F32) for t in terms).astype(BF)
    share = enc // db_count
    grad_tok = grad_tok.reshape(db_count, groups, part, -1)
    grad_wo = None
    for c in range(groups):
        term = lax.dot_general(
            sent[c][:, :part], grad_tok[:, c], (((0, 1), (0, 1)), ((), ())), preferred_element_type=F32
        )
        grad_wo = term if grad_wo is None else grad_wo + term
        if c < groups - 1:
            sent[-1], grad_wo = lax.optimization_barrier((sent[-1], grad_wo))
    grad_w = [
        jnp.sum(sent[-1][:, part + k * share : part + (k + 1) * share].astype(F32), axis=0)
        for k in range(2)
    ]
    return (attended, jnp.concatenate(grad_q, axis=0), *grad_w, grad_wo)


def solution(mesh):
    placed = (
        P("db", "head"),
        P(None, "head"),
        P(None, "head"),
        P("head", None),
        P("db", "head", None),
        P("db", None),
        P("db", None),
        P("db"),
        P("db", "head"),
    )
    return jax.shard_map(
        shards,
        mesh=mesh,
        in_specs=placed,
        out_specs=(
            P("db", "head"),
            P("db", "head"),
            P("db", "head"),
            P("db", "head"),
            P("head", "db"),
        ),
        check_vma=False,
    )
```

```python
import functools
import math

import jax
import jax.numpy as jnp
from jax import lax
from jax.experimental import pallas as pl
from jax.experimental.pallas import tpu as pltpu
from jax.sharding import PartitionSpec as P

HD = 128
BF = jnp.bfloat16
F32 = jnp.float32
VMEM_LIMIT = 60 * 1024 * 1024
SMALL_LIMIT = 8 * 1024 * 1024


def mm(a, b, ca, cb):
    return lax.dot_general(a, b, (((ca,), (cb,)), ((), ())), preferred_element_type=F32)


def params():
    return pltpu.CompilerParams(vmem_limit_bytes=VMEM_LIMIT)


ANY = pl.BlockSpec(memory_space=pl.ANY)
HBM = pl.BlockSpec(memory_space=pltpu.HBM)
VM = pl.BlockSpec(memory_space=pltpu.VMEM)
SM = pl.BlockSpec(memory_space=pltpu.SMEM)


def pick_kernel(rows_ref, src_ref, *rest, row_of, count):
    *outs, held, load_sem, store_sem = rest
    places = [out.at[n] for out in outs for n in range(out.shape[0])]
    loads = [
        pltpu.make_async_copy(src_ref.at[row_of(rows_ref, k)], held.at[k], load_sem.at[k])
        for k in range(count)
    ]
    stores = [pltpu.make_async_copy(held.at[k], places[k], store_sem.at[k]) for k in range(count)]
    for load in loads:
        load.start()
    for load, store in zip(loads, stores):
        load.wait()
        store.start()
    for store in stores:
        store.wait()


def pick(rows, row_of, src, counts, place, limit):
    item = src.shape[1:]
    total = sum(counts)
    return pl.pallas_call(
        functools.partial(pick_kernel, row_of=row_of, count=total),
        out_shape=[jax.ShapeDtypeStruct((n, *item), src.dtype) for n in counts],
        in_specs=[SM, place],
        out_specs=[ANY] * len(counts),
        scratch_shapes=[
            pltpu.VMEM((total, *item), src.dtype),
            pltpu.SemaphoreType.DMA((total,)),
            pltpu.SemaphoreType.DMA((total,)),
        ],
        compiler_params=pltpu.CompilerParams(vmem_limit_bytes=limit),
    )(rows, src)


def start_loads(pairs, sem, first=0):
    loads = [pltpu.make_async_copy(src, dst, sem.at[first + k]) for k, (src, dst) in enumerate(pairs)]
    for load in loads:
        load.start()
    return loads


def wait_all(copies):
    for copy in copies:
        copy.wait()


def row_blocks(src, dst, count):
    step = src.shape[0] // count
    return [(src.at[pl.ds(k * step, step)], dst.at[pl.ds(k * step, step)]) for k in range(count)]


def back_kernel(a_in, w_in, out_in, a_ref, w_ref, out_ref, sem):
    loads = start_loads([(a_in, a_ref), *row_blocks(w_in, w_ref, 4)], sem)
    wait_all(loads)
    back_project(a_ref, w_ref, out_ref)
    wait_all(start_loads([(out_ref, out_in)], sem, len(loads)))


def back_project(a_ref, w_ref, out_ref):
    groups = out_ref.shape[0]
    part = a_ref.shape[0] // groups
    for h in range(a_ref.shape[1] // HD):
        cols = slice(h * HD, (h + 1) * HD)
        value = mm(a_ref[:, cols], w_ref[:, cols], 1, 1).astype(BF)
        for c in range(groups):
            out_ref[c, h * part : (h + 1) * part] = value[c * part : (c + 1) * part]


def back(a, w, groups):
    tall = (groups, a.shape[1] // HD * a.shape[0] // groups, w.shape[0])
    return pl.pallas_call(
        back_kernel,
        out_shape=jax.ShapeDtypeStruct(tall, BF),
        in_specs=[HBM, HBM],
        out_specs=HBM,
        scratch_shapes=[pltpu.VMEM(shape, BF) for shape in (a.shape, w.shape, tall)]
        + [pltpu.SemaphoreType.DMA((6,))],
        compiler_params=params(),
        cost_estimate=pl.CostEstimate(flops=120_000_000, bytes_accessed=2_000_000, transcendentals=0),
    )(a, w)


def prep_kernel(at_ref, near_in, far_in, wo_in, wv_in, dm_out, dt_out, gc_out, *refs):
    near_ref, far_ref, wo_ref, wv_ref, dm_ref, dt_ref, gc_ref, sem = refs
    chips, rows, width = near_ref.shape
    cuts = gc_ref.shape[0] // (2 * chips)
    piece = width // cuts
    share = gc_ref.shape[1]
    own = pl.ds(pl.multiple_of((at_ref[0] * 2 + at_ref[1]) * share, share), share)
    first = start_loads([(near_in, near_ref), (far_in, far_ref)], sem)
    blocks = start_loads(row_blocks(wo_in, wo_ref, 8), sem, 2)
    late = start_loads([(wv_in, wv_ref)], sem, 10)
    wait_all(first)
    places = []
    for core, g_ref in enumerate((near_ref, far_ref)):
        for s in range(chips):
            j = lax.rem(at_ref[0] + chips - s, chips) * 2 + lax.rem(at_ref[1] + core, 2)
            places.append((g_ref, s, pl.ds(pl.multiple_of(j * width, width), width)))
            for p in range(cuts):
                gc_ref[j * cuts + p, :, :piece] = g_ref[s, own, p * piece : (p + 1) * piece]
                gc_ref[j * cuts + p, :, piece:] = jnp.zeros((share, width - piece), BF)
    stores = start_loads([(gc_ref, gc_out)], sem, 11)
    wait_all(blocks)
    acc = jnp.zeros((rows, width), F32)
    for g_ref, s, cols in places:
        acc += mm(g_ref[s], wo_ref[:, cols], 1, 1)
    dm_ref[...] = acc.astype(BF)
    wait_all(late)
    back_project(dm_ref, wv_ref, dt_ref)
    stores += start_loads([(dm_ref, dm_out), (dt_ref, dt_out)], sem, 12)
    wait_all(stores)


def prep(at, near, far, wo, wv, groups, db_count):
    chips, rows, width = near.shape
    tall = (groups, width // HD * rows // groups, wv.shape[0])
    made = [(rows, width), tall, (db_count, rows // (2 * chips), width)]
    operands = (near, far, wo, wv)
    return pl.pallas_call(
        prep_kernel,
        out_shape=[jax.ShapeDtypeStruct(shape, BF) for shape in made],
        in_specs=[SM] + [HBM] * 4,
        out_specs=[HBM] * 3,
        scratch_shapes=[pltpu.VMEM(shape, BF) for shape in (*(v.shape for v in operands), *made)]
        + [pltpu.SemaphoreType.DMA((14,))],
        compiler_params=params(),
        cost_estimate=pl.CostEstimate(flops=700_000_000, bytes_accessed=8_000_000, transcendentals=0),
    )(at, *operands)


def attn_kernel(count_ref, *refs, c, pieces, last):
    x_in, refs = refs[:pieces], refs[pieces:]
    more = 7 if last else 4
    ins, refs = refs[:more], refs[more:]
    outs = 2 if last else 3
    (send_ref, *keep_outs), refs = refs[:outs], refs[outs:]
    x_ref, mixed_ref, t_ref, u_ref, qt_ref, dt_ref, wv_ref, *refs = refs
    sem = refs[-1]
    slots, sub, enc = x_in[0].shape
    qt_in, dt_in, wv_in = ins[:3]
    part, width = mixed_ref.shape
    heads = width // HD
    db_count = send_ref.shape[0]
    used = 0

    def start(pairs):
        nonlocal used
        loads = start_loads(pairs, sem, used)
        used += len(pairs)
        return loads

    x_loads = start(
        [(qt_in.at[c], qt_ref)]
        + [(x_in[p], x_ref.at[pl.ds(p * slots, slots)]) for p in range(pieces)]
    )
    dt_loads = start([(dt_in.at[c], dt_ref)])
    wv_loads = start(row_blocks(wv_in, wv_ref, 2))
    if last:
        q_ref, dm_ref, t0_ref, u0_ref, gw_ref = refs[:5]
        last_loads = start(list(zip(ins[3:], (q_ref, dm_ref, t0_ref, u0_ref))))
    else:
        gs_ref = refs[0]
        gs_loads = start([(ins[3], gs_ref)])
    factor = 1.0 / math.sqrt(HD)
    wait_all(x_loads)
    x = x_ref[...].reshape(pieces * slots * sub, enc)
    keys = x.shape[0]
    s = mm(qt_ref[...], x, 1, 1) * factor
    slot = (lax.broadcasted_iota(jnp.int32, (1, keys), 1) // sub) % slots
    expo = jnp.where(slot < count_ref[c], jnp.exp(s), 0.0)
    probs = expo / jnp.sum(expo, axis=-1, keepdims=True)
    t_ref[...] = mm(probs.astype(BF), x, 1, 0).astype(BF)
    wait_all(wv_loads)
    for h in range(heads):
        cols = slice(h * HD, (h + 1) * HD)
        mixed_ref[:, cols] = mm(t_ref[h * part : (h + 1) * part], wv_ref[:, cols], 1, 0).astype(BF)
    stores = start([(mixed_ref, send_ref.at[i, pl.ds(0, part)]) for i in range(db_count)])
    if not last:
        wait_all(gs_loads)
        tail = pl.ds(part, gs_ref.shape[1])
        stores += start([(t_ref, keep_outs[1]), (gs_ref, send_ref.at[:, tail])])
    wait_all(dt_loads)
    d = mm(dt_ref[...], x, 1, 1)
    inner = jnp.sum(probs * d, axis=-1, keepdims=True)
    ds = (probs * (d - inner) * factor).astype(BF)
    u_ref[...] = mm(ds, x, 1, 0).astype(BF)
    stores += start([(u_ref, keep_outs[0])])
    if last:
        wait_all(last_loads)
        share = enc // db_count
        for h in range(heads):
            rows = slice(h * part, (h + 1) * part)
            cols = slice(h * HD, (h + 1) * HD)
            u_all = jnp.concatenate([u0_ref[rows], u_ref[rows]], axis=0)
            t_all = jnp.concatenate([t0_ref[rows], t_ref[rows]], axis=0)
            sums = (mm(u_all, q_ref[:, cols], 0, 0), mm(t_all, dm_ref[:, cols], 0, 0))
            for k, total in enumerate(sums):
                for i in range(db_count):
                    gw_ref[i, k * share : (k + 1) * share, cols] = total[
                        i * share : (i + 1) * share
                    ].astype(BF)
        stores += start([(gw_ref, send_ref.at[:, pl.ds(part, 2 * share)])])
    wait_all(stores)


def attn(count, xs, qt, dt, wv, c, db_count, extra, last):
    slots, sub, enc = xs[0].shape
    width = wv.shape[1]
    tall = qt.shape[1:]
    part = tall[0] * HD // width
    grown = 2 * enc // db_count if last else extra[0].shape[1]
    made = [(db_count, part + grown, width), tall]
    more = list(extra)
    held = [(len(xs) * slots, sub, enc), (part, width), tall, tall, tall, tall, wv.shape]
    held += [v.shape for v in more]
    copies = len(xs) + 8 + len(more) + db_count
    if last:
        held += [(db_count, grown, width)]
    else:
        made += [tall]
    return pl.pallas_call(
        functools.partial(attn_kernel, c=c, pieces=len(xs), last=last),
        out_shape=[jax.ShapeDtypeStruct(shape, BF) for shape in made],
        in_specs=[SM] + [HBM] * (len(xs) + 3 + len(more)),
        out_specs=[HBM] * len(made),
        scratch_shapes=[pltpu.VMEM(shape, BF) for shape in held] + [pltpu.SemaphoreType.DMA((copies,))],
        compiler_params=params(),
        cost_estimate=pl.CostEstimate(flops=3_000_000_000, bytes_accessed=8_000_000, transcendentals=262144),
    )(count, *xs, qt, dt, wv, *more)


def close_kernel(at_ref, *refs, groups):
    sends, us = refs[:groups], refs[groups : 2 * groups]
    wo_in, wk_in, keep_ref, give_ref, gq_ref, mixed_ref, u_ref, wo_ref, wk_ref, sem = refs[2 * groups :]
    chips, rows, width = keep_ref.shape
    part = rows // groups
    first = []
    for c in range(groups):
        pairs = [(sends[c].at[0, pl.ds(0, part)], mixed_ref.at[pl.ds(c * part, part)]), (us[c], u_ref.at[c])]
        first += start_loads(pairs, sem, 2 * c)
    first += start_loads([(wk_in, wk_ref)], sem, 2 * groups)
    loads = start_loads(row_blocks(wo_in, wo_ref, 8), sem, 2 * groups + 1)
    wait_all(first)
    for c in range(groups):
        for h in range(width // HD):
            cols = slice(h * HD, (h + 1) * HD)
            gq_ref[c * part : (c + 1) * part, cols] = mm(
                u_ref[c, h * part : (h + 1) * part], wk_ref[:, cols], 1, 0
            ).astype(BF)
    wait_all(loads)
    mixed = mixed_ref[...]
    for core, block_ref in enumerate((keep_ref, give_ref)):
        for step in range(chips):
            j = lax.rem(at_ref[0] + step, chips) * 2 + lax.rem(at_ref[1] + core, 2)
            cols = pl.ds(pl.multiple_of(j * width, width), width)
            block_ref[step] = mm(mixed, wo_ref[:, cols], 1, 0).astype(BF)


def close(at, sends, us, wo, wk, part, head_count):
    groups = len(us)
    width = wk.shape[1]
    rows = groups * part
    half = jax.ShapeDtypeStruct((head_count // 2, rows, width), BF)
    return pl.pallas_call(
        functools.partial(close_kernel, groups=groups),
        out_shape=[half, half, jax.ShapeDtypeStruct((rows, width), BF)],
        in_specs=[SM] + [HBM] * (2 * groups + 2),
        out_specs=[VM] * 3,
        scratch_shapes=[
            pltpu.VMEM((rows, width), BF),
            pltpu.VMEM((groups, *us[0].shape), BF),
            pltpu.VMEM(wo.shape, BF),
            pltpu.VMEM(wk.shape, BF),
            pltpu.SemaphoreType.DMA((2 * groups + 9,)),
        ],
        compiler_params=params(),
        cost_estimate=pl.CostEstimate(flops=700_000_000, bytes_accessed=8_000_000, transcendentals=0),
    )(at, *sends, *us, wo, wk)


def order_kernel(at_ref, near_ref, far_ref, out_ref):
    chips, _, share, _ = near_ref.shape
    for core, g_ref in enumerate((near_ref, far_ref)):
        for s in range(chips):
            j = lax.rem(at_ref[0] + chips - s, chips) * 2 + lax.rem(at_ref[1] + core, 2)
            out_ref[:, pl.ds(pl.multiple_of(j * share, share), share)] = g_ref[s]


def order(at, near, far):
    chips, db_count, share, piece = near.shape
    return pl.pallas_call(
        order_kernel,
        out_shape=jax.ShapeDtypeStruct((db_count, 2 * chips * share, piece), BF),
        in_specs=[SM, VM, VM],
        out_specs=VM,
        compiler_params=params(),
        cost_estimate=pl.CostEstimate(flops=0, bytes_accessed=2_000_000, transcendentals=0),
    )(at, near, far)


def chips_stack(x, steps, count):
    pieces = {0: x, **{s: along(x, s, count) for s in steps}}
    return jnp.stack([pieces[s] for s in range(count // 2)])


def along(v, step, count):
    chips = count // 2
    return lax.ppermute(v, "head", [(i, ((i // 2 + step) % chips) * 2 + i % 2) for i in range(count)])


def swap(v, count):
    return lax.ppermute(v, "head", [(i, i ^ 1) for i in range(count)])


def ring_steps(count):
    chips = count // 2
    return sorted(range(1, chips), key=lambda s: min(s, chips - s))


def exchange(x, axis):
    return lax.all_to_all(x, axis, split_axis=0, concat_axis=0, tiled=True)


def after(x, *others):
    return lax.optimization_barrier((x, *others))[0]


def shards(queries, w_key, w_value, w_out, encodings, nbr_row, nbr_owner, nbr_count, grad_out):
    db_count = lax.axis_size("db")
    head_count = lax.axis_size("head")
    groups, slot_count = nbr_row.shape
    tok_rows, width = queries.shape
    part = tok_rows // groups
    enc = encodings.shape[2]
    head_at = lax.axis_index("head")
    at = jnp.stack([head_at // 2, head_at % 2]).astype(jnp.int32)
    owner_ids = lax.broadcasted_iota(jnp.int32, (db_count, 1, 1, 1), 0)
    wanted = jnp.sum(jnp.where(nbr_owner[None, None] == owner_ids, nbr_row[None, None], 0), axis=3)
    incoming = exchange(wanted, "db")
    steps = ring_steps(head_count)
    (table,) = pick(
        incoming,
        lambda ref, k: ref[k // groups, 0, k % groups],
        encodings,
        (db_count * groups,),
        HBM,
        VMEM_LIMIT,
    )
    qt = back(after(queries, table), w_key, groups)
    received = after(exchange(table, "db"), qt)
    mine = pick(
        nbr_owner,
        lambda ref, k: ref[k // slot_count, k % slot_count] * groups + k // slot_count,
        received,
        (slot_count,) * groups,
        ANY,
        SMALL_LIMIT,
    )
    token = mine[0]
    near = chips_stack(after(grad_out, table), steps, head_count)
    far = swap(near, head_count)
    dm, dt, grad_cols = prep(at, near, far, w_out, w_value, groups, db_count)
    ring = []
    for c in range(groups):
        held = mine[c] if c == 0 else after(mine[c], *ring[-1])
        came = [along(held, s, head_count) for s in steps]
        if c == 0:
            came = lax.optimization_barrier((*came, dm))[:-1]
        ring.append([held, *came])
    spread = []
    for pieces in ring:
        spread.append([*pieces, *(swap(v, head_count) for v in pieces)])
    sent, sends, us = [], [], []
    extra = (grad_cols,)
    for c in range(groups):
        m, u, *t = attn(nbr_count, spread[c], qt, dt, w_value, c, db_count, extra, c == groups - 1)
        us.append(u)
        sends.append(m)
        sent.append(exchange(after(m, *(ring[-1] if c == 0 else sent)), "db"))
        extra = (queries, dm, *t, u)
    share = tok_rows // head_count
    piece = width * head_count // db_count
    rows_near = chips_stack(sent[0][:, part : part + share, :piece], steps, head_count)
    grad_tok = order(at, rows_near, swap(rows_near, head_count))
    keep, give, grad_q = close(at, sends, us, w_out, w_key, part, head_count)
    other = swap(give, head_count)
    pair = (keep.astype(F32) + other.astype(F32)).astype(BF)
    terms = [pair[0]] + [along(pair[s], s, head_count) for s in steps]
    attended = sum(t.astype(F32) for t in terms).astype(BF)
    share = enc // db_count
    grad_tok = grad_tok.reshape(db_count, groups, part, -1)
    grad_wo = None
    for c in range(groups):
        term = lax.dot_general(
            sent[c][:, :part], grad_tok[:, c], (((0, 1), (0, 1)), ((), ())), preferred_element_type=F32
        )
        grad_wo = term if grad_wo is None else grad_wo + term
        if c < groups - 1:
            sent[-1], grad_wo = lax.optimization_barrier((sent[-1], grad_wo))
    grad_w = [
        jnp.sum(sent[-1][:, part + k * share : part + (k + 1) * share].astype(F32), axis=0)
        for k in range(2)
    ]
    return (attended, grad_q, *grad_w, grad_wo)


def solution(mesh):
    placed = (
        P("db", "head"),
        P(None, "head"),
        P(None, "head"),
        P("head", None),
        P("db", "head", None),
        P("db", None),
        P("db", None),
        P("db"),
        P("db", "head"),
    )
    return jax.shard_map(
        shards,
        mesh=mesh,
        in_specs=placed,
        out_specs=(
            P("db", "head"),
            P("db", "head"),
            P("db", "head"),
            P("db", "head"),
            P("head", "db"),
        ),
        check_vma=False,
    )
```

```python
import functools
import math

import jax
import jax.numpy as jnp
from jax import lax
from jax.experimental import pallas as pl
from jax.experimental.pallas import tpu as pltpu
from jax.sharding import PartitionSpec as P

HD = 128
BF = jnp.bfloat16
F32 = jnp.float32
VMEM_LIMIT = 60 * 1024 * 1024
SMALL_LIMIT = 8 * 1024 * 1024


def mm(a, b, ca, cb):
    return lax.dot_general(a, b, (((ca,), (cb,)), ((), ())), preferred_element_type=F32)


def params():
    return pltpu.CompilerParams(vmem_limit_bytes=VMEM_LIMIT)


ANY = pl.BlockSpec(memory_space=pl.ANY)
HBM = pl.BlockSpec(memory_space=pltpu.HBM)
VM = pl.BlockSpec(memory_space=pltpu.VMEM)
SM = pl.BlockSpec(memory_space=pltpu.SMEM)


def pick_kernel(rows_ref, src_ref, *rest, row_of, count):
    *outs, held, load_sem, store_sem = rest
    loads = [
        pltpu.make_async_copy(src_ref.at[row_of(rows_ref, k)], held.at[k], load_sem.at[k])
        for k in range(count)
    ]
    for load in loads:
        load.start()
    stores, first = [], 0
    for n, out in enumerate(outs):
        size = out.shape[0]
        for load in loads[first : first + size]:
            load.wait()
        stores.append(pltpu.make_async_copy(held.at[pl.ds(first, size)], out, store_sem.at[n]))
        stores[-1].start()
        first += size
    for store in stores:
        store.wait()


def pick(rows, row_of, src, counts, place, limit):
    item = src.shape[1:]
    total = sum(counts)
    return pl.pallas_call(
        functools.partial(pick_kernel, row_of=row_of, count=total),
        out_shape=[jax.ShapeDtypeStruct((n, *item), src.dtype) for n in counts],
        in_specs=[SM, place],
        out_specs=[ANY] * len(counts),
        scratch_shapes=[
            pltpu.VMEM((total, *item), src.dtype),
            pltpu.SemaphoreType.DMA((total,)),
            pltpu.SemaphoreType.DMA((len(counts),)),
        ],
        compiler_params=pltpu.CompilerParams(vmem_limit_bytes=limit),
    )(rows, src)


def start_loads(pairs, sem, first=0):
    loads = [pltpu.make_async_copy(src, dst, sem.at[first + k]) for k, (src, dst) in enumerate(pairs)]
    for load in loads:
        load.start()
    return loads


def wait_all(copies):
    for copy in copies:
        copy.wait()


def row_blocks(src, dst, count):
    step = src.shape[0] // count
    return [(src.at[pl.ds(k * step, step)], dst.at[pl.ds(k * step, step)]) for k in range(count)]


def back_kernel(a_in, w_in, out_in, a_ref, w_ref, out_ref, sem):
    loads = start_loads([(a_in, a_ref), *row_blocks(w_in, w_ref, 4)], sem)
    wait_all(loads)
    back_project(a_ref, w_ref, out_ref)
    wait_all(start_loads([(out_ref, out_in)], sem, len(loads)))


def back_project(a_ref, w_ref, out_ref):
    groups = out_ref.shape[0]
    part = a_ref.shape[0] // groups
    for h in range(a_ref.shape[1] // HD):
        cols = slice(h * HD, (h + 1) * HD)
        value = mm(a_ref[:, cols], w_ref[:, cols], 1, 1).astype(BF)
        for c in range(groups):
            out_ref[c, h * part : (h + 1) * part] = value[c * part : (c + 1) * part]


def back(a, w, groups):
    tall = (groups, a.shape[1] // HD * a.shape[0] // groups, w.shape[0])
    return pl.pallas_call(
        back_kernel,
        out_shape=jax.ShapeDtypeStruct(tall, BF),
        in_specs=[HBM, HBM],
        out_specs=HBM,
        scratch_shapes=[pltpu.VMEM(shape, BF) for shape in (a.shape, w.shape, tall)]
        + [pltpu.SemaphoreType.DMA((6,))],
        compiler_params=params(),
        cost_estimate=pl.CostEstimate(flops=120_000_000, bytes_accessed=2_000_000, transcendentals=0),
    )(a, w)


def prep_kernel(at_ref, near_in, far_in, wo_in, wv_in, dm_out, dt_out, gc_out, *refs):
    near_ref, far_ref, wo_ref, wv_ref, dm_ref, dt_ref, gc_ref, sem = refs
    chips, rows, width = near_ref.shape
    cuts = gc_ref.shape[0] // (2 * chips)
    piece = width // cuts
    share = gc_ref.shape[1]
    own = pl.ds(pl.multiple_of((at_ref[0] * 2 + at_ref[1]) * share, share), share)
    first = start_loads([(near_in, near_ref), (far_in, far_ref)], sem)
    heads = width // HD
    blocks = start_loads(row_blocks(wo_in, wo_ref, heads), sem, 2)
    late = start_loads([(wv_in, wv_ref)], sem, 2 + heads)
    wait_all(first)
    places = []
    for core, g_ref in enumerate((near_ref, far_ref)):
        for s in range(chips):
            j = lax.rem(at_ref[0] + chips - s, chips) * 2 + lax.rem(at_ref[1] + core, 2)
            places.append((g_ref, s, pl.ds(pl.multiple_of(j * width, width), width)))
            for p in range(cuts):
                gc_ref[j * cuts + p, :, :piece] = g_ref[s, own, p * piece : (p + 1) * piece]
                gc_ref[j * cuts + p, :, piece:] = jnp.zeros((share, width - piece), BF)
    stores = start_loads([(gc_ref, gc_out)], sem, 3 + heads)
    groups = dt_ref.shape[0]
    part = rows // groups
    for h in range(heads):
        hd = slice(h * HD, (h + 1) * HD)
        blocks[h].wait()
        acc = jnp.zeros((rows, HD), F32)
        for g_ref, s, cols in places:
            acc += mm(g_ref[s], wo_ref[hd, cols], 1, 1)
        dm = acc.astype(BF)
        dm_ref[:, hd] = dm
        if h == 0:
            wait_all(late)
        value = mm(dm, wv_ref[:, hd], 1, 1).astype(BF)
        for c in range(groups):
            dt_ref[c, h * part : (h + 1) * part] = value[c * part : (c + 1) * part]
    stores += start_loads([(dm_ref, dm_out), (dt_ref, dt_out)], sem, 4 + heads)
    wait_all(stores)


def prep(at, near, far, wo, wv, groups, db_count):
    chips, rows, width = near.shape
    tall = (groups, width // HD * rows // groups, wv.shape[0])
    made = [(rows, width), tall, (db_count, rows // (2 * chips), width)]
    operands = (near, far, wo, wv)
    return pl.pallas_call(
        prep_kernel,
        out_shape=[jax.ShapeDtypeStruct(shape, BF) for shape in made],
        in_specs=[SM] + [HBM] * 4,
        out_specs=[HBM] * 3,
        scratch_shapes=[pltpu.VMEM(shape, BF) for shape in (*(v.shape for v in operands), *made)]
        + [pltpu.SemaphoreType.DMA((6 + width // HD,))],
        compiler_params=params(),
        cost_estimate=pl.CostEstimate(flops=700_000_000, bytes_accessed=8_000_000, transcendentals=0),
    )(at, *operands)


def attn_kernel(count_ref, *refs, c, pieces, last):
    x_in, refs = refs[:pieces], refs[pieces:]
    more = 7 if last else 4
    ins, refs = refs[:more], refs[more:]
    outs = 2 if last else 3
    (send_ref, *keep_outs), refs = refs[:outs], refs[outs:]
    x_ref, mixed_ref, t_ref, u_ref, qt_ref, dt_ref, wv_ref, *refs = refs
    sem = refs[-1]
    slots, sub, enc = x_in[0].shape
    qt_in, dt_in, wv_in = ins[:3]
    part, width = mixed_ref.shape
    heads = width // HD
    db_count = send_ref.shape[0]
    used = 0

    def start(pairs):
        nonlocal used
        loads = start_loads(pairs, sem, used)
        used += len(pairs)
        return loads

    x_loads = start(
        [(qt_in.at[c], qt_ref)]
        + [(x_in[p], x_ref.at[pl.ds(p * slots, slots)]) for p in range(pieces)]
    )
    wait_all(x_loads)
    wv_loads = start(row_blocks(wv_in, wv_ref, 2))
    dt_loads = start([(dt_in.at[c], dt_ref)])
    if last:
        q_ref, dm_ref, t0_ref, u0_ref, gw_ref = refs[:5]
        last_loads = start(list(zip(ins[3:], (q_ref, dm_ref, t0_ref, u0_ref))))
    else:
        gs_ref = refs[0]
        gs_loads = start([(ins[3], gs_ref)])
    factor = 1.0 / math.sqrt(HD)
    x = x_ref[...].reshape(pieces * slots * sub, enc)
    keys = x.shape[0]
    s = mm(qt_ref[...], x, 1, 1) * factor
    slot = (lax.broadcasted_iota(jnp.int32, (1, keys), 1) // sub) % slots
    expo = jnp.where(slot < count_ref[c], jnp.exp(s), 0.0)
    probs = expo / jnp.sum(expo, axis=-1, keepdims=True)
    t_ref[...] = mm(probs.astype(BF), x, 1, 0).astype(BF)
    wait_all(wv_loads)
    for h in range(heads):
        cols = slice(h * HD, (h + 1) * HD)
        mixed_ref[:, cols] = mm(t_ref[h * part : (h + 1) * part], wv_ref[:, cols], 1, 0).astype(BF)
    stores = start([(mixed_ref, send_ref.at[i, pl.ds(0, part)]) for i in range(db_count)])
    if not last:
        wait_all(gs_loads)
        tail = pl.ds(part, gs_ref.shape[1])
        stores += start([(t_ref, keep_outs[1]), (gs_ref, send_ref.at[:, tail])])
    wait_all(dt_loads)
    d = mm(dt_ref[...], x, 1, 1)
    inner = jnp.sum(probs * d, axis=-1, keepdims=True)
    ds = (probs * (d - inner) * factor).astype(BF)
    u_ref[...] = mm(ds, x, 1, 0).astype(BF)
    stores += start([(u_ref, keep_outs[0])])
    if last:
        wait_all(last_loads)
        share = enc // db_count
        for h in range(heads):
            rows = slice(h * part, (h + 1) * part)
            cols = slice(h * HD, (h + 1) * HD)
            u_all = jnp.concatenate([u0_ref[rows], u_ref[rows]], axis=0)
            t_all = jnp.concatenate([t0_ref[rows], t_ref[rows]], axis=0)
            sums = (mm(u_all, q_ref[:, cols], 0, 0), mm(t_all, dm_ref[:, cols], 0, 0))
            for k, total in enumerate(sums):
                for i in range(db_count):
                    gw_ref[i, k * share : (k + 1) * share, cols] = total[
                        i * share : (i + 1) * share
                    ].astype(BF)
            stores += start(
                [(gw_ref.at[:, :, pl.ds(h * HD, HD)], send_ref.at[:, pl.ds(part, 2 * share), pl.ds(h * HD, HD)])]
            )
    wait_all(stores)


def attn(count, xs, qt, dt, wv, c, db_count, extra, last):
    slots, sub, enc = xs[0].shape
    width = wv.shape[1]
    tall = qt.shape[1:]
    part = tall[0] * HD // width
    grown = 2 * enc // db_count if last else extra[0].shape[1]
    made = [(db_count, part + grown, width), tall]
    more = list(extra)
    held = [(len(xs) * slots, sub, enc), (part, width), tall, tall, tall, tall, wv.shape]
    held += [v.shape for v in more]
    copies = len(xs) + 8 + len(more) + db_count + width // HD
    if last:
        held += [(db_count, grown, width)]
    else:
        made += [tall]
    return pl.pallas_call(
        functools.partial(attn_kernel, c=c, pieces=len(xs), last=last),
        out_shape=[jax.ShapeDtypeStruct(shape, BF) for shape in made],
        in_specs=[SM] + [HBM] * (len(xs) + 3 + len(more)),
        out_specs=[HBM] * len(made),
        scratch_shapes=[pltpu.VMEM(shape, BF) for shape in held] + [pltpu.SemaphoreType.DMA((copies,))],
        compiler_params=params(),
        cost_estimate=pl.CostEstimate(flops=3_000_000_000, bytes_accessed=8_000_000, transcendentals=262144),
    )(count, *xs, qt, dt, wv, *more)


def close_kernel(at_ref, *refs, groups):
    sends, us = refs[:groups], refs[groups : 2 * groups]
    wo_in, wk_in, keep_ref, give_ref, gq_ref, mixed_ref, u_ref, wo_ref, wk_ref, sem = refs[2 * groups :]
    chips, rows, width = keep_ref.shape
    part = rows // groups
    first = []
    for c in range(groups):
        pairs = [(sends[c].at[0, pl.ds(0, part)], mixed_ref.at[pl.ds(c * part, part)]), (us[c], u_ref.at[c])]
        first += start_loads(pairs, sem, 2 * c)
    first += start_loads([(wk_in, wk_ref)], sem, 2 * groups)
    loads = start_loads(row_blocks(wo_in, wo_ref, 8), sem, 2 * groups + 1)
    wait_all(first)
    for c in range(groups):
        for h in range(width // HD):
            cols = slice(h * HD, (h + 1) * HD)
            gq_ref[c * part : (c + 1) * part, cols] = mm(
                u_ref[c, h * part : (h + 1) * part], wk_ref[:, cols], 1, 0
            ).astype(BF)
    wait_all(loads)
    mixed = mixed_ref[...]
    for core, block_ref in enumerate((keep_ref, give_ref)):
        for step in range(chips):
            j = lax.rem(at_ref[0] + step, chips) * 2 + lax.rem(at_ref[1] + core, 2)
            cols = pl.ds(pl.multiple_of(j * width, width), width)
            block_ref[step] = mm(mixed, wo_ref[:, cols], 1, 0).astype(BF)


def close(at, sends, us, wo, wk, part, head_count):
    groups = len(us)
    width = wk.shape[1]
    rows = groups * part
    half = jax.ShapeDtypeStruct((head_count // 2, rows, width), BF)
    return pl.pallas_call(
        functools.partial(close_kernel, groups=groups),
        out_shape=[half, half, jax.ShapeDtypeStruct((rows, width), BF)],
        in_specs=[SM] + [HBM] * (2 * groups + 2),
        out_specs=[VM] * 3,
        scratch_shapes=[
            pltpu.VMEM((rows, width), BF),
            pltpu.VMEM((groups, *us[0].shape), BF),
            pltpu.VMEM(wo.shape, BF),
            pltpu.VMEM(wk.shape, BF),
            pltpu.SemaphoreType.DMA((2 * groups + 9,)),
        ],
        compiler_params=params(),
        cost_estimate=pl.CostEstimate(flops=700_000_000, bytes_accessed=8_000_000, transcendentals=0),
    )(at, *sends, *us, wo, wk)


def order_kernel(at_ref, near_ref, far_ref, sent_in, out_ref, wo_ref, mixed_ref, sem):
    chips, db_count, share, piece = near_ref.shape
    part, width = mixed_ref.shape[1:]
    loads = start_loads([(sent_in.at[:, pl.ds(0, part)], mixed_ref)], sem)
    for core, g_ref in enumerate((near_ref, far_ref)):
        for s in range(chips):
            j = lax.rem(at_ref[0] + chips - s, chips) * 2 + lax.rem(at_ref[1] + core, 2)
            out_ref[:, pl.ds(pl.multiple_of(j * share, share), share)] = g_ref[s]
    wait_all(loads)
    mixed = mixed_ref[...].reshape(db_count * part, width)
    wo_ref[...] = mm(mixed, out_ref[:, :part].reshape(db_count * part, piece), 0, 0)


def order(at, near, far, sent, part):
    chips, db_count, share, piece = near.shape
    width = sent.shape[2]
    return pl.pallas_call(
        order_kernel,
        out_shape=[
            jax.ShapeDtypeStruct((db_count, 2 * chips * share, piece), BF),
            jax.ShapeDtypeStruct((width, piece), F32),
        ],
        in_specs=[SM, VM, VM, HBM],
        out_specs=[VM, VM],
        scratch_shapes=[pltpu.VMEM((db_count, part, width), BF), pltpu.SemaphoreType.DMA((1,))],
        compiler_params=params(),
        cost_estimate=pl.CostEstimate(flops=300_000_000, bytes_accessed=4_000_000, transcendentals=0),
    )(at, near, far, sent)


def chips_stack(x, steps, count):
    pieces = {0: x, **{s: along(x, s, count) for s in steps}}
    return jnp.stack([pieces[s] for s in range(count // 2)])


def along(v, step, count):
    chips = count // 2
    return lax.ppermute(v, "head", [(i, ((i // 2 + step) % chips) * 2 + i % 2) for i in range(count)])


def swap(v, count):
    return lax.ppermute(v, "head", [(i, i ^ 1) for i in range(count)])


def ring_steps(count):
    chips = count // 2
    return sorted(range(1, chips), key=lambda s: min(s, chips - s))


def exchange(x, axis):
    return lax.all_to_all(x, axis, split_axis=0, concat_axis=0, tiled=True)


def after(x, *others):
    return lax.optimization_barrier((x, *others))[0]


def shards(queries, w_key, w_value, w_out, encodings, nbr_row, nbr_owner, nbr_count, grad_out):
    db_count = lax.axis_size("db")
    head_count = lax.axis_size("head")
    groups, slot_count = nbr_row.shape
    tok_rows, width = queries.shape
    part = tok_rows // groups
    enc = encodings.shape[2]
    head_at = lax.axis_index("head")
    at = jnp.stack([head_at // 2, head_at % 2]).astype(jnp.int32)
    owner_ids = lax.broadcasted_iota(jnp.int32, (db_count, 1, 1, 1), 0)
    wanted = jnp.sum(jnp.where(nbr_owner[None, None] == owner_ids, nbr_row[None, None], 0), axis=3)
    qt = back(queries, w_key, groups)
    incoming = after(exchange(wanted, "db"), qt)
    steps = ring_steps(head_count)
    (table,) = pick(
        incoming,
        lambda ref, k: ref[k // groups, 0, k % groups],
        encodings,
        (db_count * groups,),
        HBM,
        VMEM_LIMIT,
    )
    received = exchange(table, "db")
    mine = pick(
        nbr_owner,
        lambda ref, k: ref[k // slot_count, k % slot_count] * groups + k // slot_count,
        received,
        (slot_count,) * groups,
        ANY,
        SMALL_LIMIT,
    )
    token = mine[0]
    near = chips_stack(after(grad_out, table), steps, head_count)
    far = swap(near, head_count)
    dm, dt, grad_cols = prep(at, near, far, w_out, w_value, groups, db_count)
    ring = []
    for c in range(groups):
        held = mine[c] if c == 0 else after(mine[c], *ring[-1])
        came = [along(held, s, head_count) for s in steps]
        if c == 0:
            came = lax.optimization_barrier((*came, dm))[:-1]
        ring.append([held, *came])
    spread = []
    for pieces in ring:
        spread.append([*pieces, *(swap(v, head_count) for v in pieces)])
    sent, sends, us = [], [], []
    extra = (grad_cols,)
    for c in range(groups):
        m, u, *t = attn(nbr_count, spread[c], qt, dt, w_value, c, db_count, extra, c == groups - 1)
        us.append(u)
        sends.append(m)
        sent.append(exchange(after(m, *(ring[-1] if c == 0 else sent)), "db"))
        extra = (queries, dm, *t, u)
    share = tok_rows // head_count
    piece = width * head_count // db_count
    rows_near = chips_stack(sent[0][:, part : part + share, :piece], steps, head_count)
    grad_tok, grad_wo = order(at, rows_near, swap(rows_near, head_count), sent[0], part)
    keep, give, grad_q = close(at, sends, us, w_out, w_key, part, head_count)
    other = swap(give, head_count)
    pair = (keep.astype(F32) + other.astype(F32)).astype(BF)
    terms = [pair[0]] + [along(pair[s], s, head_count) for s in steps]
    attended = sum(t.astype(F32) for t in terms).astype(BF)
    share = enc // db_count
    grad_tok = grad_tok.reshape(db_count, groups, part, -1)
    sent[-1], grad_wo = lax.optimization_barrier((sent[-1], grad_wo))
    for c in range(1, groups):
        grad_wo = grad_wo + lax.dot_general(
            sent[c][:, :part], grad_tok[:, c], (((0, 1), (0, 1)), ((), ())), preferred_element_type=F32
        )
    grad_w = [
        jnp.sum(sent[-1][:, part + k * share : part + (k + 1) * share].astype(F32), axis=0)
        for k in range(2)
    ]
    return (attended, grad_q, *grad_w, grad_wo)


def solution(mesh):
    placed = (
        P("db", "head"),
        P(None, "head"),
        P(None, "head"),
        P("head", None),
        P("db", "head", None),
        P("db", None),
        P("db", None),
        P("db"),
        P("db", "head"),
    )
    return jax.shard_map(
        shards,
        mesh=mesh,
        in_specs=placed,
        out_specs=(
            P("db", "head"),
            P("db", "head"),
            P("db", "head"),
            P("db", "head"),
            P("head", "db"),
        ),
        check_vma=False,
    )
```

```python
import functools
import math

import jax
import jax.numpy as jnp
from jax import lax
from jax.experimental import pallas as pl
from jax.experimental.pallas import tpu as pltpu
from jax.sharding import PartitionSpec as P

HD = 128
BF = jnp.bfloat16
F32 = jnp.float32
VMEM_LIMIT = 60 * 1024 * 1024
SMALL_LIMIT = 8 * 1024 * 1024


def mm(a, b, ca, cb):
    return lax.dot_general(a, b, (((ca,), (cb,)), ((), ())), preferred_element_type=F32)


def params():
    return pltpu.CompilerParams(vmem_limit_bytes=VMEM_LIMIT)


ANY = pl.BlockSpec(memory_space=pl.ANY)
HBM = pl.BlockSpec(memory_space=pltpu.HBM)
VM = pl.BlockSpec(memory_space=pltpu.VMEM)
SM = pl.BlockSpec(memory_space=pltpu.SMEM)


def pick_kernel(rows_ref, src_ref, *rest, row_of, count):
    *outs, held, load_sem, store_sem = rest
    loads = [
        pltpu.make_async_copy(src_ref.at[row_of(rows_ref, k)], held.at[k], load_sem.at[k])
        for k in range(count)
    ]
    for load in loads:
        load.start()
    stores, first = [], 0
    for n, out in enumerate(outs):
        size = out.shape[0]
        for load in loads[first : first + size]:
            load.wait()
        stores.append(pltpu.make_async_copy(held.at[pl.ds(first, size)], out, store_sem.at[n]))
        stores[-1].start()
        first += size
    for store in stores:
        store.wait()


def pick(rows, row_of, src, counts, place, limit):
    item = src.shape[1:]
    total = sum(counts)
    return pl.pallas_call(
        functools.partial(pick_kernel, row_of=row_of, count=total),
        out_shape=[jax.ShapeDtypeStruct((n, *item), src.dtype) for n in counts],
        in_specs=[SM, place],
        out_specs=[ANY] * len(counts),
        scratch_shapes=[
            pltpu.VMEM((total, *item), src.dtype),
            pltpu.SemaphoreType.DMA((total,)),
            pltpu.SemaphoreType.DMA((len(counts),)),
        ],
        compiler_params=pltpu.CompilerParams(vmem_limit_bytes=limit),
    )(rows, src)


def start_loads(pairs, sem, first=0):
    loads = [pltpu.make_async_copy(src, dst, sem.at[first + k]) for k, (src, dst) in enumerate(pairs)]
    for load in loads:
        load.start()
    return loads


def wait_all(copies):
    for copy in copies:
        copy.wait()


def row_blocks(src, dst, count):
    step = src.shape[0] // count
    return [(src.at[pl.ds(k * step, step)], dst.at[pl.ds(k * step, step)]) for k in range(count)]


def back_kernel(a_in, w_in, out_in, a_ref, w_ref, out_ref, sem):
    loads = start_loads([(a_in, a_ref), *row_blocks(w_in, w_ref, 4)], sem)
    wait_all(loads)
    back_project(a_ref, w_ref, out_ref)
    wait_all(start_loads([(out_ref, out_in)], sem, len(loads)))


def back_project(a_ref, w_ref, out_ref):
    groups = out_ref.shape[0]
    part = a_ref.shape[0] // groups
    for h in range(a_ref.shape[1] // HD):
        cols = slice(h * HD, (h + 1) * HD)
        value = mm(a_ref[:, cols], w_ref[:, cols], 1, 1).astype(BF)
        for c in range(groups):
            out_ref[c, h * part : (h + 1) * part] = value[c * part : (c + 1) * part]


def back(a, w, groups):
    tall = (groups, a.shape[1] // HD * a.shape[0] // groups, w.shape[0])
    return pl.pallas_call(
        back_kernel,
        out_shape=jax.ShapeDtypeStruct(tall, BF),
        in_specs=[HBM, HBM],
        out_specs=HBM,
        scratch_shapes=[pltpu.VMEM(shape, BF) for shape in (a.shape, w.shape, tall)]
        + [pltpu.SemaphoreType.DMA((6,))],
        compiler_params=params(),
        cost_estimate=pl.CostEstimate(flops=120_000_000, bytes_accessed=2_000_000, transcendentals=0),
    )(a, w)


def prep_kernel(at_ref, near_in, far_in, wo_in, wv_in, dm_out, dt_out, gc_out, *refs):
    near_ref, far_ref, wo_ref, wv_ref, dm_ref, dt_ref, gc_ref, sem = refs
    chips, rows, width = near_ref.shape
    cuts = gc_ref.shape[0] // (2 * chips)
    piece = width // cuts
    share = gc_ref.shape[1]
    own = pl.ds(pl.multiple_of((at_ref[0] * 2 + at_ref[1]) * share, share), share)
    first = start_loads([(near_in, near_ref), (far_in, far_ref)], sem)
    places = []
    for core, g_ref in enumerate((near_ref, far_ref)):
        for s in range(chips):
            j = lax.rem(at_ref[0] + chips - s, chips) * 2 + lax.rem(at_ref[1] + core, 2)
            places.append((g_ref, s, j))
    blocks = start_loads(
        [
            (wo_in.at[:, pl.ds(pl.multiple_of(j * width, width), width)], wo_ref.at[k])
            for k, (_, _, j) in enumerate(places)
        ],
        sem,
        2,
    )
    used = 2 + len(places)
    late = start_loads([(wv_in, wv_ref)], sem, used)
    wait_all(first)
    for g_ref, s, j in places:
        for p in range(cuts):
            gc_ref[j * cuts + p, :, :piece] = g_ref[s, own, p * piece : (p + 1) * piece]
            gc_ref[j * cuts + p, :, piece:] = jnp.zeros((share, width - piece), BF)
    stores = start_loads([(gc_ref, gc_out)], sem, used + 1)
    acc = jnp.zeros((rows, width), F32)
    for k, (g_ref, s, _) in enumerate(places):
        blocks[k].wait()
        acc += mm(g_ref[s], wo_ref[k], 1, 1)
    dm_ref[...] = acc.astype(BF)
    wait_all(late)
    back_project(dm_ref, wv_ref, dt_ref)
    stores += start_loads([(dm_ref, dm_out), (dt_ref, dt_out)], sem, used + 2)
    wait_all(stores)


def prep(at, near, far, wo, wv, groups, db_count):
    chips, rows, width = near.shape
    tall = (groups, width // HD * rows // groups, wv.shape[0])
    made = [(rows, width), tall, (db_count, rows // (2 * chips), width)]
    operands = (near, far, wo, wv)
    return pl.pallas_call(
        prep_kernel,
        out_shape=[jax.ShapeDtypeStruct(shape, BF) for shape in made],
        in_specs=[SM] + [HBM] * 4,
        out_specs=[HBM] * 3,
        scratch_shapes=[
            pltpu.VMEM(shape, BF)
            for shape in (near.shape, far.shape, (2 * chips, width, width), wv.shape, *made)
        ]
        + [pltpu.SemaphoreType.DMA((6 + 2 * chips,))],
        compiler_params=params(),
        cost_estimate=pl.CostEstimate(flops=700_000_000, bytes_accessed=8_000_000, transcendentals=0),
    )(at, *operands)


def attn_kernel(count_ref, *refs, c, pieces, last):
    x_in, refs = refs[:pieces], refs[pieces:]
    more = 7 if last else 4
    ins, refs = refs[:more], refs[more:]
    outs = 2 if last else 3
    (send_ref, *keep_outs), refs = refs[:outs], refs[outs:]
    x_ref, mixed_ref, t_ref, u_ref, qt_ref, dt_ref, wv_ref, *refs = refs
    sem = refs[-1]
    slots, sub, enc = x_in[0].shape
    qt_in, dt_in, wv_in = ins[:3]
    part, width = mixed_ref.shape
    heads = width // HD
    db_count = send_ref.shape[0]
    used = 0

    def start(pairs):
        nonlocal used
        loads = start_loads(pairs, sem, used)
        used += len(pairs)
        return loads

    x_loads = start(
        [(qt_in.at[c], qt_ref)]
        + [(x_in[p], x_ref.at[pl.ds(p * slots, slots)]) for p in range(pieces)]
    )
    wait_all(x_loads)
    wv_loads = start(row_blocks(wv_in, wv_ref, 2))
    dt_loads = start([(dt_in.at[c], dt_ref)])
    if last:
        q_ref, dm_ref, t0_ref, u0_ref, gw_ref = refs[:5]
        last_loads = start(list(zip(ins[3:], (q_ref, dm_ref, t0_ref, u0_ref))))
    else:
        gs_ref = refs[0]
        gs_loads = start([(ins[3], gs_ref)])
    factor = 1.0 / math.sqrt(HD)
    x = x_ref[...].reshape(pieces * slots * sub, enc)
    keys = x.shape[0]
    s = mm(qt_ref[...], x, 1, 1) * factor
    slot = (lax.broadcasted_iota(jnp.int32, (1, keys), 1) // sub) % slots
    expo = jnp.where(slot < count_ref[c], jnp.exp(s), 0.0)
    probs = expo / jnp.sum(expo, axis=-1, keepdims=True)
    t_ref[...] = mm(probs.astype(BF), x, 1, 0).astype(BF)
    wait_all(wv_loads)
    for h in range(heads):
        cols = slice(h * HD, (h + 1) * HD)
        mixed_ref[:, cols] = mm(t_ref[h * part : (h + 1) * part], wv_ref[:, cols], 1, 0).astype(BF)
    stores = start([(mixed_ref, send_ref.at[i, pl.ds(0, part)]) for i in range(db_count)])
    if not last:
        wait_all(gs_loads)
        tail = pl.ds(part, gs_ref.shape[1])
        stores += start([(t_ref, keep_outs[1]), (gs_ref, send_ref.at[:, tail])])
    wait_all(dt_loads)
    d = mm(dt_ref[...], x, 1, 1)
    inner = jnp.sum(probs * d, axis=-1, keepdims=True)
    ds = (probs * (d - inner) * factor).astype(BF)
    u_ref[...] = mm(ds, x, 1, 0).astype(BF)
    stores += start([(u_ref, keep_outs[0])])
    if last:
        wait_all(last_loads)
        share = enc // db_count
        for h in range(heads):
            rows = slice(h * part, (h + 1) * part)
            cols = slice(h * HD, (h + 1) * HD)
            u_all = jnp.concatenate([u0_ref[rows], u_ref[rows]], axis=0)
            t_all = jnp.concatenate([t0_ref[rows], t_ref[rows]], axis=0)
            sums = (mm(u_all, q_ref[:, cols], 0, 0), mm(t_all, dm_ref[:, cols], 0, 0))
            for k, total in enumerate(sums):
                for i in range(db_count):
                    gw_ref[i, k * share : (k + 1) * share, cols] = total[
                        i * share : (i + 1) * share
                    ].astype(BF)
            stores += start(
                [(gw_ref.at[:, :, pl.ds(h * HD, HD)], send_ref.at[:, pl.ds(part, 2 * share), pl.ds(h * HD, HD)])]
            )
    wait_all(stores)


def attn(count, xs, qt, dt, wv, c, db_count, extra, last):
    slots, sub, enc = xs[0].shape
    width = wv.shape[1]
    tall = qt.shape[1:]
    part = tall[0] * HD // width
    grown = 2 * enc // db_count if last else extra[0].shape[1]
    made = [(db_count, part + grown, width), tall]
    more = list(extra)
    held = [(len(xs) * slots, sub, enc), (part, width), tall, tall, tall, tall, wv.shape]
    held += [v.shape for v in more]
    copies = len(xs) + 8 + len(more) + db_count + width // HD
    if last:
        held += [(db_count, grown, width)]
    else:
        made += [tall]
    return pl.pallas_call(
        functools.partial(attn_kernel, c=c, pieces=len(xs), last=last),
        out_shape=[jax.ShapeDtypeStruct(shape, BF) for shape in made],
        in_specs=[SM] + [HBM] * (len(xs) + 3 + len(more)),
        out_specs=[HBM] * len(made),
        scratch_shapes=[pltpu.VMEM(shape, BF) for shape in held] + [pltpu.SemaphoreType.DMA((copies,))],
        compiler_params=params(),
        cost_estimate=pl.CostEstimate(flops=3_000_000_000, bytes_accessed=8_000_000, transcendentals=262144),
    )(count, *xs, qt, dt, wv, *more)


def close_kernel(at_ref, *refs, groups):
    sends, us = refs[:groups], refs[groups : 2 * groups]
    wo_in, wk_in, keep_ref, give_ref, gq_ref, mixed_ref, u_ref, wo_ref, wk_ref, sem = refs[2 * groups :]
    chips, rows, width = keep_ref.shape
    part = rows // groups
    first = []
    for c in range(groups):
        pairs = [(sends[c].at[0, pl.ds(0, part)], mixed_ref.at[pl.ds(c * part, part)]), (us[c], u_ref.at[c])]
        first += start_loads(pairs, sem, 2 * c)
    first += start_loads([(wk_in, wk_ref)], sem, 2 * groups)
    loads = start_loads(row_blocks(wo_in, wo_ref, 8), sem, 2 * groups + 1)
    wait_all(first)
    for c in range(groups):
        for h in range(width // HD):
            cols = slice(h * HD, (h + 1) * HD)
            gq_ref[c * part : (c + 1) * part, cols] = mm(
                u_ref[c, h * part : (h + 1) * part], wk_ref[:, cols], 1, 0
            ).astype(BF)
    wait_all(loads)
    mixed = mixed_ref[...]
    for core, block_ref in enumerate((keep_ref, give_ref)):
        for step in range(chips):
            j = lax.rem(at_ref[0] + step, chips) * 2 + lax.rem(at_ref[1] + core, 2)
            cols = pl.ds(pl.multiple_of(j * width, width), width)
            block_ref[step] = mm(mixed, wo_ref[:, cols], 1, 0).astype(BF)


def close(at, sends, us, wo, wk, part, head_count):
    groups = len(us)
    width = wk.shape[1]
    rows = groups * part
    half = jax.ShapeDtypeStruct((head_count // 2, rows, width), BF)
    return pl.pallas_call(
        functools.partial(close_kernel, groups=groups),
        out_shape=[half, half, jax.ShapeDtypeStruct((rows, width), BF)],
        in_specs=[SM] + [HBM] * (2 * groups + 2),
        out_specs=[VM] * 3,
        scratch_shapes=[
            pltpu.VMEM((rows, width), BF),
            pltpu.VMEM((groups, *us[0].shape), BF),
            pltpu.VMEM(wo.shape, BF),
            pltpu.VMEM(wk.shape, BF),
            pltpu.SemaphoreType.DMA((2 * groups + 9,)),
        ],
        compiler_params=params(),
        cost_estimate=pl.CostEstimate(flops=700_000_000, bytes_accessed=8_000_000, transcendentals=0),
    )(at, *sends, *us, wo, wk)


def order_kernel(at_ref, near_ref, far_ref, out_ref):
    chips, _, share, _ = near_ref.shape
    for core, g_ref in enumerate((near_ref, far_ref)):
        for s in range(chips):
            j = lax.rem(at_ref[0] + chips - s, chips) * 2 + lax.rem(at_ref[1] + core, 2)
            out_ref[:, pl.ds(pl.multiple_of(j * share, share), share)] = g_ref[s]


def order(at, near, far):
    chips, db_count, share, piece = near.shape
    return pl.pallas_call(
        order_kernel,
        out_shape=jax.ShapeDtypeStruct((db_count, 2 * chips * share, piece), BF),
        in_specs=[SM, VM, VM],
        out_specs=VM,
        compiler_params=params(),
        cost_estimate=pl.CostEstimate(flops=0, bytes_accessed=2_000_000, transcendentals=0),
    )(at, near, far)


def chips_stack(x, steps, count):
    pieces = {0: x, **{s: along(x, s, count) for s in steps}}
    return jnp.stack([pieces[s] for s in range(count // 2)])


def along(v, step, count):
    chips = count // 2
    return lax.ppermute(v, "head", [(i, ((i // 2 + step) % chips) * 2 + i % 2) for i in range(count)])


def swap(v, count):
    return lax.ppermute(v, "head", [(i, i ^ 1) for i in range(count)])


def ring_steps(count):
    chips = count // 2
    return sorted(range(1, chips), key=lambda s: min(s, chips - s))


def exchange(x, axis):
    return lax.all_to_all(x, axis, split_axis=0, concat_axis=0, tiled=True)


def after(x, *others):
    return lax.optimization_barrier((x, *others))[0]


def shards(queries, w_key, w_value, w_out, encodings, nbr_row, nbr_owner, nbr_count, grad_out):
    db_count = lax.axis_size("db")
    head_count = lax.axis_size("head")
    groups, slot_count = nbr_row.shape
    tok_rows, width = queries.shape
    part = tok_rows // groups
    enc = encodings.shape[2]
    head_at = lax.axis_index("head")
    at = jnp.stack([head_at // 2, head_at % 2]).astype(jnp.int32)
    owner_ids = lax.broadcasted_iota(jnp.int32, (db_count, 1, 1, 1), 0)
    wanted = jnp.sum(jnp.where(nbr_owner[None, None] == owner_ids, nbr_row[None, None], 0), axis=3)
    qt = back(queries, w_key, groups)
    incoming = after(exchange(wanted, "db"), qt)
    steps = ring_steps(head_count)
    (table,) = pick(
        incoming,
        lambda ref, k: ref[k // groups, 0, k % groups],
        encodings,
        (db_count * groups,),
        HBM,
        VMEM_LIMIT,
    )
    received = exchange(table, "db")
    mine = pick(
        nbr_owner,
        lambda ref, k: ref[k // slot_count, k % slot_count] * groups + k // slot_count,
        received,
        (slot_count,) * groups,
        ANY,
        SMALL_LIMIT,
    )
    token = mine[0]
    near = chips_stack(after(grad_out, table), steps, head_count)
    far = swap(near, head_count)
    crossed = [swap(v, head_count) for v in mine]
    near = after(near, crossed[0])
    dm, dt, grad_cols = prep(at, near, far, w_out, w_value, groups, db_count)
    ring = []
    for c in range(groups):
        held = mine[c] if c == 0 else after(mine[c], *ring[-1])
        came = [along(held, s, head_count) for s in steps]
        if c == 0:
            came = lax.optimization_barrier((*came, dm))[:-1]
        ring.append([held, *came])
    spread = []
    for c, pieces in enumerate(ring):
        spread.append([*pieces, crossed[c], *(swap(v, head_count) for v in pieces[1:])])
    sent, sends, us = [], [], []
    extra = (grad_cols,)
    for c in range(groups):
        m, u, *t = attn(nbr_count, spread[c], qt, dt, w_value, c, db_count, extra, c == groups - 1)
        us.append(u)
        sends.append(m)
        sent.append(exchange(after(m, *(ring[-1] if c == 0 else sent)), "db"))
        extra = (queries, dm, *t, u)
    share = tok_rows // head_count
    piece = width * head_count // db_count
    rows_near = chips_stack(sent[0][:, part : part + share, :piece], steps, head_count)
    grad_tok = order(at, rows_near, swap(rows_near, head_count))
    keep, give, grad_q = close(at, sends, us, w_out, w_key, part, head_count)
    other = swap(give, head_count)
    pair = (keep.astype(F32) + other.astype(F32)).astype(BF)
    terms = [pair[0]] + [along(pair[s], s, head_count) for s in steps]
    attended = sum(t.astype(F32) for t in terms).astype(BF)
    share = enc // db_count
    grad_tok = grad_tok.reshape(db_count, groups, part, -1)
    grad_wo = None
    for c in range(groups):
        term = lax.dot_general(
            sent[c][:, :part], grad_tok[:, c], (((0, 1), (0, 1)), ((), ())), preferred_element_type=F32
        )
        grad_wo = term if grad_wo is None else grad_wo + term
        if c < groups - 1:
            sent[-1], grad_wo = lax.optimization_barrier((sent[-1], grad_wo))
    grad_w = [
        jnp.sum(sent[-1][:, part + k * share : part + (k + 1) * share].astype(F32), axis=0)
        for k in range(2)
    ]
    return (attended, grad_q, *grad_w, grad_wo)


def solution(mesh):
    placed = (
        P("db", "head"),
        P(None, "head"),
        P(None, "head"),
        P("head", None),
        P("db", "head", None),
        P("db", None),
        P("db", None),
        P("db"),
        P("db", "head"),
    )
    return jax.shard_map(
        shards,
        mesh=mesh,
        in_specs=placed,
        out_specs=(
            P("db", "head"),
            P("db", "head"),
            P("db", "head"),
            P("db", "head"),
            P("head", "db"),
        ),
        check_vma=False,
    )
```

```python
import functools
import math

import jax
import jax.numpy as jnp
from jax import lax
from jax.experimental import pallas as pl
from jax.experimental.pallas import tpu as pltpu
from jax.sharding import PartitionSpec as P

HD = 128
BF = jnp.bfloat16
F32 = jnp.float32
VMEM_LIMIT = 60 * 1024 * 1024
SMALL_LIMIT = 8 * 1024 * 1024


def mm(a, b, ca, cb):
    return lax.dot_general(a, b, (((ca,), (cb,)), ((), ())), preferred_element_type=F32)


def params():
    return pltpu.CompilerParams(vmem_limit_bytes=VMEM_LIMIT)


ANY = pl.BlockSpec(memory_space=pl.ANY)
HBM = pl.BlockSpec(memory_space=pltpu.HBM)
VM = pl.BlockSpec(memory_space=pltpu.VMEM)
SM = pl.BlockSpec(memory_space=pltpu.SMEM)


def pick_kernel(rows_ref, src_ref, *rest, row_of, count):
    *outs, held, load_sem, store_sem = rest
    loads = [
        pltpu.make_async_copy(src_ref.at[row_of(rows_ref, k)], held.at[k], load_sem.at[k])
        for k in range(count)
    ]
    for load in loads:
        load.start()
    stores, first = [], 0
    for n, out in enumerate(outs):
        size = out.shape[0]
        for load in loads[first : first + size]:
            load.wait()
        stores.append(pltpu.make_async_copy(held.at[pl.ds(first, size)], out, store_sem.at[n]))
        stores[-1].start()
        first += size
    for store in stores:
        store.wait()


def pick(rows, row_of, src, counts, place, limit):
    item = src.shape[1:]
    total = sum(counts)
    return pl.pallas_call(
        functools.partial(pick_kernel, row_of=row_of, count=total),
        out_shape=[jax.ShapeDtypeStruct((n, *item), src.dtype) for n in counts],
        in_specs=[SM, place],
        out_specs=[ANY] * len(counts),
        scratch_shapes=[
            pltpu.VMEM((total, *item), src.dtype),
            pltpu.SemaphoreType.DMA((total,)),
            pltpu.SemaphoreType.DMA((len(counts),)),
        ],
        compiler_params=pltpu.CompilerParams(vmem_limit_bytes=limit),
    )(rows, src)


def start_loads(pairs, sem, first=0):
    loads = [pltpu.make_async_copy(src, dst, sem.at[first + k]) for k, (src, dst) in enumerate(pairs)]
    for load in loads:
        load.start()
    return loads


def wait_all(copies):
    for copy in copies:
        copy.wait()


def row_blocks(src, dst, count):
    step = src.shape[0] // count
    return [(src.at[pl.ds(k * step, step)], dst.at[pl.ds(k * step, step)]) for k in range(count)]


def back_kernel(a_in, w_in, out_in, a_ref, w_ref, out_ref, sem):
    loads = start_loads([(a_in, a_ref), *row_blocks(w_in, w_ref, 4)], sem)
    wait_all(loads)
    back_project(a_ref, w_ref, out_ref)
    wait_all(start_loads([(out_ref, out_in)], sem, len(loads)))


def back_project(a_ref, w_ref, out_ref):
    groups = out_ref.shape[0]
    part = a_ref.shape[0] // groups
    for h in range(a_ref.shape[1] // HD):
        cols = slice(h * HD, (h + 1) * HD)
        value = mm(a_ref[:, cols], w_ref[:, cols], 1, 1).astype(BF)
        for c in range(groups):
            out_ref[c, h * part : (h + 1) * part] = value[c * part : (c + 1) * part]


def back(a, w, groups):
    tall = (groups, a.shape[1] // HD * a.shape[0] // groups, w.shape[0])
    return pl.pallas_call(
        back_kernel,
        out_shape=jax.ShapeDtypeStruct(tall, BF),
        in_specs=[HBM, HBM],
        out_specs=HBM,
        scratch_shapes=[pltpu.VMEM(shape, BF) for shape in (a.shape, w.shape, tall)]
        + [pltpu.SemaphoreType.DMA((6,))],
        compiler_params=params(),
        cost_estimate=pl.CostEstimate(flops=120_000_000, bytes_accessed=2_000_000, transcendentals=0),
    )(a, w)


def prep_kernel(at_ref, near_in, far_in, wo_in, wv_in, dm_out, dt_out, gc_out, *refs):
    near_ref, far_ref, wo_ref, wv_ref, dm_ref, dt_ref, gc_ref, sem = refs
    chips, rows, width = near_ref.shape
    cuts = gc_ref.shape[0] // (2 * chips)
    piece = width // cuts
    share = gc_ref.shape[1]
    own = pl.ds(pl.multiple_of((at_ref[0] * 2 + at_ref[1]) * share, share), share)
    first = start_loads([(near_in, near_ref), (far_in, far_ref)], sem)
    places = []
    for core, g_ref in enumerate((near_ref, far_ref)):
        for s in range(chips):
            j = lax.rem(at_ref[0] + chips - s, chips) * 2 + lax.rem(at_ref[1] + core, 2)
            places.append((g_ref, s, j))
    blocks = start_loads(
        [
            (wo_in.at[:, pl.ds(pl.multiple_of(j * width, width), width)], wo_ref.at[k])
            for k, (_, _, j) in enumerate(places)
        ],
        sem,
        2,
    )
    used = 2 + len(places)
    late = start_loads([(wv_in, wv_ref)], sem, used)
    wait_all(first)
    for g_ref, s, j in places:
        for p in range(cuts):
            gc_ref[j * cuts + p, :, :piece] = g_ref[s, own, p * piece : (p + 1) * piece]
            gc_ref[j * cuts + p, :, piece:] = jnp.zeros((share, width - piece), BF)
    stores = start_loads([(gc_ref, gc_out)], sem, used + 1)
    acc = jnp.zeros((rows, width), F32)
    for k, (g_ref, s, _) in enumerate(places):
        blocks[k].wait()
        acc += mm(g_ref[s], wo_ref[k], 1, 1)
    dm_ref[...] = acc.astype(BF)
    wait_all(late)
    back_project(dm_ref, wv_ref, dt_ref)
    stores += start_loads([(dm_ref, dm_out), (dt_ref, dt_out)], sem, used + 2)
    wait_all(stores)


def prep(at, near, far, wo, wv, groups, db_count):
    chips, rows, width = near.shape
    tall = (groups, width // HD * rows // groups, wv.shape[0])
    made = [(rows, width), tall, (db_count, rows // (2 * chips), width)]
    operands = (near, far, wo, wv)
    return pl.pallas_call(
        prep_kernel,
        out_shape=[jax.ShapeDtypeStruct(shape, BF) for shape in made],
        in_specs=[SM] + [HBM] * 4,
        out_specs=[HBM] * 3,
        scratch_shapes=[
            pltpu.VMEM(shape, BF)
            for shape in (near.shape, far.shape, (2 * chips, width, width), wv.shape, *made)
        ]
        + [pltpu.SemaphoreType.DMA((6 + 2 * chips,))],
        compiler_params=params(),
        cost_estimate=pl.CostEstimate(flops=700_000_000, bytes_accessed=8_000_000, transcendentals=0),
    )(at, *operands)


def attn_kernel(count_ref, *refs, c, pieces, front, rear):
    x_in, refs = refs[:pieces], refs[pieces:]
    last = front and rear
    more = 7 if last else 4 if front else 3
    ins, refs = refs[:more], refs[more:]
    outs = 1 if rear and not front else 2
    results, refs = refs[:outs], refs[outs:]
    x_ref, mixed_ref, t_ref, u_ref, qt_ref, dt_ref, wv_ref, *refs = refs
    sem = refs[-1]
    send_ref = results[0]
    slots, sub, enc = x_in[0].shape
    qt_in, dt_in, wv_in = ins[:3]
    part, width = mixed_ref.shape
    heads = width // HD
    used = 0

    def start(pairs):
        nonlocal used
        loads = start_loads(pairs, sem, used)
        used += len(pairs)
        return loads

    x_loads = start(
        [(qt_in.at[c], qt_ref)]
        + [(x_in[p], x_ref.at[pl.ds(p * slots, slots)]) for p in range(pieces)]
    )
    wait_all(x_loads)
    if front:
        wv_loads = start(row_blocks(wv_in, wv_ref, 2))
    if rear:
        dt_loads = start([(dt_in.at[c], dt_ref)])
    if last:
        q_ref, dm_ref, t0_ref, u0_ref, gw_ref = refs[:5]
        last_loads = start(list(zip(ins[3:], (q_ref, dm_ref, t0_ref, u0_ref))))
    elif front:
        gs_ref = refs[0]
        gs_loads = start([(ins[3], gs_ref)])
    factor = 1.0 / math.sqrt(HD)
    x = x_ref[...].reshape(pieces * slots * sub, enc)
    keys = x.shape[0]
    s = mm(qt_ref[...], x, 1, 1) * factor
    slot = (lax.broadcasted_iota(jnp.int32, (1, keys), 1) // sub) % slots
    expo = jnp.where(slot < count_ref[c], jnp.exp(s), 0.0)
    probs = expo / jnp.sum(expo, axis=-1, keepdims=True)
    stores = []
    if front:
        db_count = send_ref.shape[0]
        t_ref[...] = mm(probs.astype(BF), x, 1, 0).astype(BF)
        wait_all(wv_loads)
        for h in range(heads):
            cols = slice(h * HD, (h + 1) * HD)
            mixed_ref[:, cols] = mm(t_ref[h * part : (h + 1) * part], wv_ref[:, cols], 1, 0).astype(BF)
        stores = start([(mixed_ref, send_ref.at[i, pl.ds(0, part)]) for i in range(db_count)])
    if front and not rear:
        wait_all(gs_loads)
        tail = pl.ds(part, gs_ref.shape[1])
        stores += start([(t_ref, results[1]), (gs_ref, send_ref.at[:, tail])])
    if rear:
        wait_all(dt_loads)
        d = mm(dt_ref[...], x, 1, 1)
        inner = jnp.sum(probs * d, axis=-1, keepdims=True)
        ds = (probs * (d - inner) * factor).astype(BF)
        u_ref[...] = mm(ds, x, 1, 0).astype(BF)
        stores += start([(u_ref, results[-1])])
    if last:
        wait_all(last_loads)
        share = enc // db_count
        for h in range(heads):
            rows = slice(h * part, (h + 1) * part)
            cols = slice(h * HD, (h + 1) * HD)
            u_all = jnp.concatenate([u0_ref[rows], u_ref[rows]], axis=0)
            t_all = jnp.concatenate([t0_ref[rows], t_ref[rows]], axis=0)
            sums = (mm(u_all, q_ref[:, cols], 0, 0), mm(t_all, dm_ref[:, cols], 0, 0))
            for k, total in enumerate(sums):
                for i in range(db_count):
                    gw_ref[i, k * share : (k + 1) * share, cols] = total[
                        i * share : (i + 1) * share
                    ].astype(BF)
            stores += start(
                [(gw_ref.at[:, :, pl.ds(h * HD, HD)], send_ref.at[:, pl.ds(part, 2 * share), pl.ds(h * HD, HD)])]
            )
    wait_all(stores)


def attn(count, xs, qt, dt, wv, c, db_count, extra, front=True, rear=True):
    slots, sub, enc = xs[0].shape
    width = wv.shape[1]
    tall = qt.shape[1:]
    part = tall[0] * HD // width
    last = front and rear
    more = list(extra)
    grown = 2 * enc // db_count if last else more[0].shape[1] if front else 0
    made = [(db_count, part + grown, width), tall] if front else [tall]
    held = [(len(xs) * slots, sub, enc), (part, width), tall, tall, tall, tall, wv.shape]
    held += [v.shape for v in more]
    copies = len(xs) + 8 + len(more) + db_count + width // HD
    if last:
        held += [(db_count, grown, width)]
    return pl.pallas_call(
        functools.partial(attn_kernel, c=c, pieces=len(xs), front=front, rear=rear),
        out_shape=[jax.ShapeDtypeStruct(shape, BF) for shape in made],
        in_specs=[SM] + [HBM] * (len(xs) + 3 + len(more)),
        out_specs=[HBM] * len(made),
        scratch_shapes=[pltpu.VMEM(shape, BF) for shape in held] + [pltpu.SemaphoreType.DMA((copies,))],
        compiler_params=params(),
        cost_estimate=pl.CostEstimate(flops=100_000, bytes_accessed=100_000, transcendentals=0),
    )(count, *xs, qt, dt, wv, *more)


def close_kernel(at_ref, *refs, groups):
    sends, us = refs[:groups], refs[groups : 2 * groups]
    wo_in, wk_in, keep_ref, give_ref, gq_ref, mixed_ref, u_ref, wo_ref, wk_ref, sem = refs[2 * groups :]
    chips, rows, width = keep_ref.shape
    part = rows // groups
    first = []
    for c in range(groups):
        pairs = [(sends[c].at[0, pl.ds(0, part)], mixed_ref.at[pl.ds(c * part, part)]), (us[c], u_ref.at[c])]
        first += start_loads(pairs, sem, 2 * c)
    first += start_loads([(wk_in, wk_ref)], sem, 2 * groups)
    loads = start_loads(row_blocks(wo_in, wo_ref, 8), sem, 2 * groups + 1)
    wait_all(first)
    for c in range(groups):
        for h in range(width // HD):
            cols = slice(h * HD, (h + 1) * HD)
            gq_ref[c * part : (c + 1) * part, cols] = mm(
                u_ref[c, h * part : (h + 1) * part], wk_ref[:, cols], 1, 0
            ).astype(BF)
    wait_all(loads)
    mixed = mixed_ref[...]
    for core, block_ref in enumerate((keep_ref, give_ref)):
        for step in range(chips):
            j = lax.rem(at_ref[0] + step, chips) * 2 + lax.rem(at_ref[1] + core, 2)
            cols = pl.ds(pl.multiple_of(j * width, width), width)
            block_ref[step] = mm(mixed, wo_ref[:, cols], 1, 0).astype(BF)


def close(at, sends, us, wo, wk, part, head_count):
    groups = len(us)
    width = wk.shape[1]
    rows = groups * part
    half = jax.ShapeDtypeStruct((head_count // 2, rows, width), BF)
    return pl.pallas_call(
        functools.partial(close_kernel, groups=groups),
        out_shape=[half, half, jax.ShapeDtypeStruct((rows, width), BF)],
        in_specs=[SM] + [HBM] * (2 * groups + 2),
        out_specs=[VM] * 3,
        scratch_shapes=[
            pltpu.VMEM((rows, width), BF),
            pltpu.VMEM((groups, *us[0].shape), BF),
            pltpu.VMEM(wo.shape, BF),
            pltpu.VMEM(wk.shape, BF),
            pltpu.SemaphoreType.DMA((2 * groups + 9,)),
        ],
        compiler_params=params(),
        cost_estimate=pl.CostEstimate(flops=700_000_000, bytes_accessed=8_000_000, transcendentals=0),
    )(at, *sends, *us, wo, wk)


def order_kernel(at_ref, near_ref, far_ref, out_ref):
    chips, _, share, _ = near_ref.shape
    for core, g_ref in enumerate((near_ref, far_ref)):
        for s in range(chips):
            j = lax.rem(at_ref[0] + chips - s, chips) * 2 + lax.rem(at_ref[1] + core, 2)
            out_ref[:, pl.ds(pl.multiple_of(j * share, share), share)] = g_ref[s]


def order(at, near, far):
    chips, db_count, share, piece = near.shape
    return pl.pallas_call(
        order_kernel,
        out_shape=jax.ShapeDtypeStruct((db_count, 2 * chips * share, piece), BF),
        in_specs=[SM, VM, VM],
        out_specs=VM,
        compiler_params=params(),
        cost_estimate=pl.CostEstimate(flops=0, bytes_accessed=2_000_000, transcendentals=0),
    )(at, near, far)


def chips_stack(x, steps, count):
    pieces = {0: x, **{s: along(x, s, count) for s in steps}}
    return jnp.stack([pieces[s] for s in range(count // 2)])


def along(v, step, count):
    chips = count // 2
    return lax.ppermute(v, "head", [(i, ((i // 2 + step) % chips) * 2 + i % 2) for i in range(count)])


def swap(v, count):
    return lax.ppermute(v, "head", [(i, i ^ 1) for i in range(count)])


def ring_steps(count):
    chips = count // 2
    return sorted(range(1, chips), key=lambda s: min(s, chips - s))


def exchange(x, axis):
    return lax.all_to_all(x, axis, split_axis=0, concat_axis=0, tiled=True)


def after(x, *others):
    return lax.optimization_barrier((x, *others))[0]


def shards(queries, w_key, w_value, w_out, encodings, nbr_row, nbr_owner, nbr_count, grad_out):
    db_count = lax.axis_size("db")
    head_count = lax.axis_size("head")
    groups, slot_count = nbr_row.shape
    tok_rows, width = queries.shape
    part = tok_rows // groups
    enc = encodings.shape[2]
    head_at = lax.axis_index("head")
    at = jnp.stack([head_at // 2, head_at % 2]).astype(jnp.int32)
    owner_ids = lax.broadcasted_iota(jnp.int32, (db_count, 1, 1, 1), 0)
    wanted = jnp.sum(jnp.where(nbr_owner[None, None] == owner_ids, nbr_row[None, None], 0), axis=3)
    qt = back(queries, w_key, groups)
    incoming = after(exchange(wanted, "db"), qt)
    steps = ring_steps(head_count)
    (table,) = pick(
        incoming,
        lambda ref, k: ref[k // groups, 0, k % groups],
        encodings,
        (db_count * groups,),
        HBM,
        VMEM_LIMIT,
    )
    received = exchange(table, "db")
    mine = pick(
        nbr_owner,
        lambda ref, k: ref[k // slot_count, k % slot_count] * groups + k // slot_count,
        received,
        (slot_count,) * groups,
        ANY,
        SMALL_LIMIT,
    )
    token = mine[0]
    near = chips_stack(after(grad_out, table), steps, head_count)
    far = swap(near, head_count)
    crossed = [swap(v, head_count) for v in mine]
    near = after(near, crossed[0])
    dm, dt, grad_cols = prep(at, near, far, w_out, w_value, groups, db_count)
    ring = []
    for c in range(groups):
        held = mine[c] if c == 0 else after(mine[c], *ring[-1][1:-1])
        came = [along(held, s, head_count) for s in steps]
        if c == 0:
            came = [after(v, dm) for v in came]
        ring.append([held, *came])
    spread = []
    for c, pieces in enumerate(ring):
        spread.append([*pieces, crossed[c], *(swap(v, head_count) for v in pieces[1:])])
    sent, sends, us = [], [], []
    extra = ()
    for c in range(groups):
        if c == groups - 1:
            m, u = attn(nbr_count, spread[c], qt, dt, w_value, c, db_count, extra)
            m = after(m, *sent)
        else:
            m, t = attn(nbr_count, spread[c], qt, dt, w_value, c, db_count, (grad_cols,), rear=False)
            m = after(m, *ring[c + 1])
            held = lax.optimization_barrier((*spread[c], m))[:-1]
            (u,) = attn(nbr_count, held, qt, dt, w_value, c, db_count, (), front=False)
            extra = (queries, dm, t, u)
        us.append(u)
        sends.append(m)
        sent.append(exchange(m, "db"))
    share = tok_rows // head_count
    piece = width * head_count // db_count
    rows_near = chips_stack(sent[0][:, part : part + share, :piece], steps, head_count)
    grad_tok = order(at, rows_near, swap(rows_near, head_count))
    keep, give, grad_q = close(at, sends, us, w_out, w_key, part, head_count)
    other = swap(give, head_count)
    pair = (keep.astype(F32) + other.astype(F32)).astype(BF)
    terms = [pair[0]] + [along(pair[s], s, head_count) for s in steps]
    attended = sum(t.astype(F32) for t in terms).astype(BF)
    share = enc // db_count
    grad_tok = grad_tok.reshape(db_count, groups, part, -1)
    grad_wo = None
    for c in range(groups):
        term = lax.dot_general(
            sent[c][:, :part], grad_tok[:, c], (((0, 1), (0, 1)), ((), ())), preferred_element_type=F32
        )
        grad_wo = term if grad_wo is None else grad_wo + term
        if c < groups - 1:
            sent[-1], grad_wo = lax.optimization_barrier((sent[-1], grad_wo))
    grad_w = [
        jnp.sum(sent[-1][:, part + k * share : part + (k + 1) * share].astype(F32), axis=0)
        for k in range(2)
    ]
    return (attended, grad_q, *grad_w, grad_wo)


def solution(mesh):
    placed = (
        P("db", "head"),
        P(None, "head"),
        P(None, "head"),
        P("head", None),
        P("db", "head", None),
        P("db", None),
        P("db", None),
        P("db"),
        P("db", "head"),
    )
    return jax.shard_map(
        shards,
        mesh=mesh,
        in_specs=placed,
        out_specs=(
            P("db", "head"),
            P("db", "head"),
            P("db", "head"),
            P("db", "head"),
            P("head", "db"),
        ),
        check_vma=False,
    )
```

```python
import functools
import math

import jax
import jax.numpy as jnp
from jax import lax
from jax.experimental import pallas as pl
from jax.experimental.pallas import tpu as pltpu
from jax.sharding import PartitionSpec as P

HD = 128
BF = jnp.bfloat16
F32 = jnp.float32
VMEM_LIMIT = 60 * 1024 * 1024
SMALL_LIMIT = 8 * 1024 * 1024


def mm(a, b, ca, cb):
    return lax.dot_general(a, b, (((ca,), (cb,)), ((), ())), preferred_element_type=F32)


def params():
    return pltpu.CompilerParams(vmem_limit_bytes=VMEM_LIMIT)


ANY = pl.BlockSpec(memory_space=pl.ANY)
HBM = pl.BlockSpec(memory_space=pltpu.HBM)
VM = pl.BlockSpec(memory_space=pltpu.VMEM)
SM = pl.BlockSpec(memory_space=pltpu.SMEM)


def pick_kernel(rows_ref, src_ref, *rest, row_of, count):
    *outs, held, load_sem, store_sem = rest
    loads = [
        pltpu.make_async_copy(src_ref.at[row_of(rows_ref, k)], held.at[k], load_sem.at[k])
        for k in range(count)
    ]
    for load in loads:
        load.start()
    stores, first = [], 0
    for n, out in enumerate(outs):
        size = out.shape[0]
        for load in loads[first : first + size]:
            load.wait()
        stores.append(pltpu.make_async_copy(held.at[pl.ds(first, size)], out, store_sem.at[n]))
        stores[-1].start()
        first += size
    for store in stores:
        store.wait()


def pick(rows, row_of, src, counts, place, limit):
    item = src.shape[1:]
    total = sum(counts)
    return pl.pallas_call(
        functools.partial(pick_kernel, row_of=row_of, count=total),
        out_shape=[jax.ShapeDtypeStruct((n, *item), src.dtype) for n in counts],
        in_specs=[SM, place],
        out_specs=[ANY] * len(counts),
        scratch_shapes=[
            pltpu.VMEM((total, *item), src.dtype),
            pltpu.SemaphoreType.DMA((total,)),
            pltpu.SemaphoreType.DMA((len(counts),)),
        ],
        compiler_params=pltpu.CompilerParams(vmem_limit_bytes=limit),
    )(rows, src)


def start_loads(pairs, sem, first=0):
    loads = [pltpu.make_async_copy(src, dst, sem.at[first + k]) for k, (src, dst) in enumerate(pairs)]
    for load in loads:
        load.start()
    return loads


def wait_all(copies):
    for copy in copies:
        copy.wait()


def row_blocks(src, dst, count):
    step = src.shape[0] // count
    return [(src.at[pl.ds(k * step, step)], dst.at[pl.ds(k * step, step)]) for k in range(count)]


def back_kernel(a_in, w_in, out_in, a_ref, w_ref, out_ref, sem):
    loads = start_loads([(a_in, a_ref), *row_blocks(w_in, w_ref, 4)], sem)
    wait_all(loads)
    back_project(a_ref, w_ref, out_ref)
    wait_all(start_loads([(out_ref, out_in)], sem, len(loads)))


def back_project(a_ref, w_ref, out_ref):
    groups = out_ref.shape[0]
    part = a_ref.shape[0] // groups
    for h in range(a_ref.shape[1] // HD):
        cols = slice(h * HD, (h + 1) * HD)
        value = mm(a_ref[:, cols], w_ref[:, cols], 1, 1).astype(BF)
        for c in range(groups):
            out_ref[c, h * part : (h + 1) * part] = value[c * part : (c + 1) * part]


def back(a, w, groups):
    tall = (groups, a.shape[1] // HD * a.shape[0] // groups, w.shape[0])
    return pl.pallas_call(
        back_kernel,
        out_shape=jax.ShapeDtypeStruct(tall, BF),
        in_specs=[HBM, HBM],
        out_specs=HBM,
        scratch_shapes=[pltpu.VMEM(shape, BF) for shape in (a.shape, w.shape, tall)]
        + [pltpu.SemaphoreType.DMA((6,))],
        compiler_params=params(),
        cost_estimate=pl.CostEstimate(flops=120_000_000, bytes_accessed=2_000_000, transcendentals=0),
    )(a, w)


def prep_kernel(at_ref, near_in, far_in, wo_in, wv_in, dm_out, dt_out, gc_out, *refs):
    near_ref, far_ref, wo_ref, wv_ref, dm_ref, dt_ref, gc_ref, sem = refs
    chips, rows, width = near_ref.shape
    cuts = gc_ref.shape[0] // (2 * chips)
    piece = width // cuts
    half = gc_ref.shape[1]
    share = 2 * half
    own = pl.ds(pl.multiple_of((at_ref[0] * 2 + at_ref[1]) * share, share), share)
    first = start_loads([(near_in, near_ref), (far_in, far_ref)], sem)
    places = []
    for core, g_ref in enumerate((near_ref, far_ref)):
        for s in range(chips):
            j = lax.rem(at_ref[0] + chips - s, chips) * 2 + lax.rem(at_ref[1] + core, 2)
            places.append((g_ref, s, j))
    blocks = start_loads(
        [
            (wo_in.at[:, pl.ds(pl.multiple_of(j * width, width), width)], wo_ref.at[k])
            for k, (_, _, j) in enumerate(places)
        ],
        sem,
        2,
    )
    used = 2 + len(places)
    late = start_loads([(wv_in, wv_ref)], sem, used)
    wait_all(first)
    for g_ref, s, j in places:
        for p in range(cuts):
            rows_of = g_ref[s, own, p * piece : (p + 1) * piece]
            gc_ref[j * cuts + p] = jnp.concatenate([rows_of[:half], rows_of[half:]], axis=1)
    stores = start_loads([(gc_ref, gc_out)], sem, used + 1)
    acc = jnp.zeros((rows, width), F32)
    for k, (g_ref, s, _) in enumerate(places):
        blocks[k].wait()
        acc += mm(g_ref[s], wo_ref[k], 1, 1)
    dm_ref[...] = acc.astype(BF)
    wait_all(late)
    back_project(dm_ref, wv_ref, dt_ref)
    stores += start_loads([(dm_ref, dm_out), (dt_ref, dt_out)], sem, used + 2)
    wait_all(stores)


def prep(at, near, far, wo, wv, groups, db_count):
    chips, rows, width = near.shape
    tall = (groups, width // HD * rows // groups, wv.shape[0])
    made = [(rows, width), tall, (db_count, rows // (4 * chips), width)]
    operands = (near, far, wo, wv)
    return pl.pallas_call(
        prep_kernel,
        out_shape=[jax.ShapeDtypeStruct(shape, BF) for shape in made],
        in_specs=[SM] + [HBM] * 4,
        out_specs=[HBM] * 3,
        scratch_shapes=[
            pltpu.VMEM(shape, BF)
            for shape in (near.shape, far.shape, (2 * chips, width, width), wv.shape, *made)
        ]
        + [pltpu.SemaphoreType.DMA((6 + 2 * chips,))],
        compiler_params=params(),
        cost_estimate=pl.CostEstimate(flops=700_000_000, bytes_accessed=8_000_000, transcendentals=0),
    )(at, *operands)


def attn_kernel(count_ref, *refs, c, pieces, last):
    x_in, refs = refs[:pieces], refs[pieces:]
    more = 7 if last else 4
    ins, refs = refs[:more], refs[more:]
    outs = 2 if last else 3
    (send_ref, *keep_outs), refs = refs[:outs], refs[outs:]
    x_ref, mixed_ref, t_ref, u_ref, qt_ref, dt_ref, wv_ref, *refs = refs
    sem = refs[-1]
    slots, sub, enc = x_in[0].shape
    qt_in, dt_in, wv_in = ins[:3]
    part, width = mixed_ref.shape
    heads = width // HD
    db_count = send_ref.shape[0]
    used = 0

    def start(pairs):
        nonlocal used
        loads = start_loads(pairs, sem, used)
        used += len(pairs)
        return loads

    x_loads = start(
        [(qt_in.at[c], qt_ref)]
        + [(x_in[p], x_ref.at[pl.ds(p * slots, slots)]) for p in range(pieces)]
    )
    wait_all(x_loads)
    wv_loads = start(row_blocks(wv_in, wv_ref, 2))
    dt_loads = start([(dt_in.at[c], dt_ref)])
    if last:
        q_ref, dm_ref, t0_ref, u0_ref, gw_ref = refs[:5]
        last_loads = start(list(zip(ins[3:], (q_ref, dm_ref, t0_ref, u0_ref))))
    else:
        gs_ref, whole_ref = refs[:2]
        gs_loads = start([(ins[3], gs_ref)])
    factor = 1.0 / math.sqrt(HD)
    x = x_ref[...].reshape(pieces * slots * sub, enc)
    keys = x.shape[0]
    s = mm(qt_ref[...], x, 1, 1) * factor
    slot = (lax.broadcasted_iota(jnp.int32, (1, keys), 1) // sub) % slots
    expo = jnp.where(slot < count_ref[c], jnp.exp(s), 0.0)
    probs = expo / jnp.sum(expo, axis=-1, keepdims=True)
    t_ref[...] = mm(probs.astype(BF), x, 1, 0).astype(BF)
    wait_all(wv_loads)
    for h in range(heads):
        cols = slice(h * HD, (h + 1) * HD)
        mixed_ref[:, cols] = mm(t_ref[h * part : (h + 1) * part], wv_ref[:, cols], 1, 0).astype(BF)
    if last:
        stores = start([(mixed_ref, send_ref.at[i, pl.ds(0, part)]) for i in range(db_count)])
    else:
        wait_all(gs_loads)
        mixed = mixed_ref[...]
        for i in range(db_count):
            whole_ref[i, :part] = mixed
            whole_ref[i, part:] = gs_ref[i]
        stores = start([(t_ref, keep_outs[1]), (whole_ref, send_ref)])
    wait_all(dt_loads)
    d = mm(dt_ref[...], x, 1, 1)
    inner = jnp.sum(probs * d, axis=-1, keepdims=True)
    ds = (probs * (d - inner) * factor).astype(BF)
    u_ref[...] = mm(ds, x, 1, 0).astype(BF)
    stores += start([(u_ref, keep_outs[0])])
    if last:
        wait_all(last_loads)
        share = enc // db_count
        for h in range(heads):
            rows = slice(h * part, (h + 1) * part)
            cols = slice(h * HD, (h + 1) * HD)
            u_all = jnp.concatenate([u0_ref[rows], u_ref[rows]], axis=0)
            t_all = jnp.concatenate([t0_ref[rows], t_ref[rows]], axis=0)
            sums = (mm(u_all, q_ref[:, cols], 0, 0), mm(t_all, dm_ref[:, cols], 0, 0))
            for k, total in enumerate(sums):
                for i in range(db_count):
                    gw_ref[i, k * share : (k + 1) * share, cols] = total[
                        i * share : (i + 1) * share
                    ].astype(BF)
            stores += start(
                [(gw_ref.at[:, :, pl.ds(h * HD, HD)], send_ref.at[:, pl.ds(part, 2 * share), pl.ds(h * HD, HD)])]
            )
    wait_all(stores)


def attn(count, xs, qt, dt, wv, c, db_count, extra, last):
    slots, sub, enc = xs[0].shape
    width = wv.shape[1]
    tall = qt.shape[1:]
    part = tall[0] * HD // width
    grown = 2 * enc // db_count if last else extra[0].shape[1]
    made = [(db_count, part + grown, width), tall]
    more = list(extra)
    held = [(len(xs) * slots, sub, enc), (part, width), tall, tall, tall, tall, wv.shape]
    held += [v.shape for v in more]
    copies = len(xs) + 8 + len(more) + db_count + width // HD
    if last:
        held += [(db_count, grown, width)]
    else:
        held += [made[0]]
        made += [tall]
    return pl.pallas_call(
        functools.partial(attn_kernel, c=c, pieces=len(xs), last=last),
        out_shape=[jax.ShapeDtypeStruct(shape, BF) for shape in made],
        in_specs=[SM] + [HBM] * (len(xs) + 3 + len(more)),
        out_specs=[HBM] * len(made),
        scratch_shapes=[pltpu.VMEM(shape, BF) for shape in held] + [pltpu.SemaphoreType.DMA((copies,))],
        compiler_params=params(),
        cost_estimate=pl.CostEstimate(flops=3_000_000_000, bytes_accessed=8_000_000, transcendentals=262144),
    )(count, *xs, qt, dt, wv, *more)


def close_kernel(at_ref, *refs, groups):
    sends, us = refs[:groups], refs[groups : 2 * groups]
    wo_in, wk_in, keep_ref, give_ref, gq_ref, mixed_ref, u_ref, wo_ref, wk_ref, sem = refs[2 * groups :]
    chips, rows, width = keep_ref.shape
    part = rows // groups
    first = []
    for c in range(groups):
        pairs = [(sends[c].at[0, pl.ds(0, part)], mixed_ref.at[pl.ds(c * part, part)]), (us[c], u_ref.at[c])]
        first += start_loads(pairs, sem, 2 * c)
    first += start_loads([(wk_in, wk_ref)], sem, 2 * groups)
    loads = start_loads(row_blocks(wo_in, wo_ref, 8), sem, 2 * groups + 1)
    wait_all(first)
    for c in range(groups):
        for h in range(width // HD):
            cols = slice(h * HD, (h + 1) * HD)
            gq_ref[c * part : (c + 1) * part, cols] = mm(
                u_ref[c, h * part : (h + 1) * part], wk_ref[:, cols], 1, 0
            ).astype(BF)
    wait_all(loads)
    mixed = mixed_ref[...]
    for core, block_ref in enumerate((keep_ref, give_ref)):
        for step in range(chips):
            j = lax.rem(at_ref[0] + step, chips) * 2 + lax.rem(at_ref[1] + core, 2)
            cols = pl.ds(pl.multiple_of(j * width, width), width)
            block_ref[step] = mm(mixed, wo_ref[:, cols], 1, 0).astype(BF)


def close(at, sends, us, wo, wk, part, head_count):
    groups = len(us)
    width = wk.shape[1]
    rows = groups * part
    half = jax.ShapeDtypeStruct((head_count // 2, rows, width), BF)
    return pl.pallas_call(
        functools.partial(close_kernel, groups=groups),
        out_shape=[half, half, jax.ShapeDtypeStruct((rows, width), BF)],
        in_specs=[SM] + [HBM] * (2 * groups + 2),
        out_specs=[VM] * 3,
        scratch_shapes=[
            pltpu.VMEM((rows, width), BF),
            pltpu.VMEM((groups, *us[0].shape), BF),
            pltpu.VMEM(wo.shape, BF),
            pltpu.VMEM(wk.shape, BF),
            pltpu.SemaphoreType.DMA((2 * groups + 9,)),
        ],
        compiler_params=params(),
        cost_estimate=pl.CostEstimate(flops=700_000_000, bytes_accessed=8_000_000, transcendentals=0),
    )(at, *sends, *us, wo, wk)


def order_kernel(at_ref, near_ref, far_ref, out_ref):
    chips, _, half, width = near_ref.shape
    share, piece = 2 * half, width // 2
    for core, g_ref in enumerate((near_ref, far_ref)):
        for s in range(chips):
            j = lax.rem(at_ref[0] + chips - s, chips) * 2 + lax.rem(at_ref[1] + core, 2)
            rows = jnp.concatenate([g_ref[s, :, :, :piece], g_ref[s, :, :, piece:]], axis=1)
            out_ref[:, pl.ds(pl.multiple_of(j * share, share), share)] = rows


def order(at, near, far):
    chips, db_count, half, width = near.shape
    return pl.pallas_call(
        order_kernel,
        out_shape=jax.ShapeDtypeStruct((db_count, 4 * chips * half, width // 2), BF),
        in_specs=[SM, VM, VM],
        out_specs=VM,
        compiler_params=params(),
        cost_estimate=pl.CostEstimate(flops=0, bytes_accessed=2_000_000, transcendentals=0),
    )(at, near, far)


def chips_stack(x, steps, count):
    pieces = {0: x, **{s: along(x, s, count) for s in steps}}
    return jnp.stack([pieces[s] for s in range(count // 2)])


def along(v, step, count):
    chips = count // 2
    return lax.ppermute(v, "head", [(i, ((i // 2 + step) % chips) * 2 + i % 2) for i in range(count)])


def swap(v, count):
    return lax.ppermute(v, "head", [(i, i ^ 1) for i in range(count)])


def ring_steps(count):
    chips = count // 2
    return sorted(range(1, chips), key=lambda s: min(s, chips - s))


def exchange(x, axis):
    return lax.all_to_all(x, axis, split_axis=0, concat_axis=0, tiled=True)


def after(x, *others):
    return lax.optimization_barrier((x, *others))[0]


def shards(queries, w_key, w_value, w_out, encodings, nbr_row, nbr_owner, nbr_count, grad_out):
    db_count = lax.axis_size("db")
    head_count = lax.axis_size("head")
    groups, slot_count = nbr_row.shape
    tok_rows, width = queries.shape
    part = tok_rows // groups
    enc = encodings.shape[2]
    head_at = lax.axis_index("head")
    at = jnp.stack([head_at // 2, head_at % 2]).astype(jnp.int32)
    owner_ids = lax.broadcasted_iota(jnp.int32, (db_count, 1, 1, 1), 0)
    wanted = jnp.sum(jnp.where(nbr_owner[None, None] == owner_ids, nbr_row[None, None], 0), axis=3)
    incoming = exchange(wanted, "db")
    steps = ring_steps(head_count)
    (table,) = pick(
        incoming,
        lambda ref, k: ref[k // groups, 0, k % groups],
        encodings,
        (db_count * groups,),
        HBM,
        VMEM_LIMIT,
    )
    received = exchange(table, "db")
    mine = pick(
        nbr_owner,
        lambda ref, k: ref[k // slot_count, k % slot_count] * groups + k // slot_count,
        received,
        (slot_count,) * groups,
        ANY,
        SMALL_LIMIT,
    )
    token = mine[0]
    near = chips_stack(after(grad_out, table), steps, head_count)
    far = swap(near, head_count)
    crossed = [swap(v, head_count) for v in mine]
    near = after(near, crossed[0])
    qt = back(after(queries, crossed[0]), w_key, groups)
    dm, dt, grad_cols = prep(at, near, far, w_out, w_value, groups, db_count)
    ring = []
    for c in range(groups):
        held = mine[c] if c == 0 else after(mine[c], *ring[-1])
        came = [along(held, s, head_count) for s in steps]
        if c == 0:
            came = lax.optimization_barrier((*came, dm, qt))[:-2]
        ring.append([held, *came])
    spread = []
    for c, pieces in enumerate(ring):
        spread.append([*pieces, crossed[c], *(swap(v, head_count) for v in pieces[1:])])
    sent, sends, us = [], [], []
    extra = (grad_cols,)
    for c in range(groups):
        m, u, *t = attn(nbr_count, spread[c], qt, dt, w_value, c, db_count, extra, c == groups - 1)
        us.append(u)
        sends.append(m)
        sent.append(exchange(after(m, *(ring[-1] if c == 0 else sent)), "db"))
        extra = (queries, dm, *t, u)
    rows_near = chips_stack(sent[0][:, part:], steps, head_count)
    grad_tok = order(at, rows_near, swap(rows_near, head_count))
    keep, give, grad_q = close(at, sends, us, w_out, w_key, part, head_count)
    other = swap(give, head_count)
    pair = (keep.astype(F32) + other.astype(F32)).astype(BF)
    terms = [pair[0]] + [along(pair[s], s, head_count) for s in steps]
    attended = sum(t.astype(F32) for t in terms).astype(BF)
    share = enc // db_count
    grad_tok = grad_tok.reshape(db_count, groups, part, -1)
    grad_wo = None
    for c in range(groups):
        term = lax.dot_general(
            sent[c][:, :part], grad_tok[:, c], (((0, 1), (0, 1)), ((), ())), preferred_element_type=F32
        )
        grad_wo = term if grad_wo is None else grad_wo + term
        if c < groups - 1:
            sent[-1], grad_wo = lax.optimization_barrier((sent[-1], grad_wo))
    grad_w = [
        jnp.sum(sent[-1][:, part + k * share : part + (k + 1) * share].astype(F32), axis=0)
        for k in range(2)
    ]
    return (attended, grad_q, *grad_w, grad_wo)


def solution(mesh):
    placed = (
        P("db", "head"),
        P(None, "head"),
        P(None, "head"),
        P("head", None),
        P("db", "head", None),
        P("db", None),
        P("db", None),
        P("db"),
        P("db", "head"),
    )
    return jax.shard_map(
        shards,
        mesh=mesh,
        in_specs=placed,
        out_specs=(
            P("db", "head"),
            P("db", "head"),
            P("db", "head"),
            P("db", "head"),
            P("head", "db"),
        ),
        check_vma=False,
    )
```

```python
import functools
import math

import jax
import jax.numpy as jnp
from jax import lax
from jax.experimental import pallas as pl
from jax.experimental.pallas import tpu as pltpu
from jax.sharding import PartitionSpec as P

HD = 128
BF = jnp.bfloat16
F32 = jnp.float32
VMEM_LIMIT = 60 * 1024 * 1024
SMALL_LIMIT = 8 * 1024 * 1024


def mm(a, b, ca, cb):
    return lax.dot_general(a, b, (((ca,), (cb,)), ((), ())), preferred_element_type=F32)


def params():
    return pltpu.CompilerParams(vmem_limit_bytes=VMEM_LIMIT)


ANY = pl.BlockSpec(memory_space=pl.ANY)
HBM = pl.BlockSpec(memory_space=pltpu.HBM)
VM = pl.BlockSpec(memory_space=pltpu.VMEM)
SM = pl.BlockSpec(memory_space=pltpu.SMEM)


def pick_kernel(rows_ref, src_ref, *rest, row_of, count):
    *outs, held, load_sem, store_sem = rest
    loads = [
        pltpu.make_async_copy(src_ref.at[row_of(rows_ref, k)], held.at[k], load_sem.at[k])
        for k in range(count)
    ]
    for load in loads:
        load.start()
    stores, first = [], 0
    for n, out in enumerate(outs):
        size = out.shape[0]
        for load in loads[first : first + size]:
            load.wait()
        stores.append(pltpu.make_async_copy(held.at[pl.ds(first, size)], out, store_sem.at[n]))
        stores[-1].start()
        first += size
    for store in stores:
        store.wait()


def pick(rows, row_of, src, counts, place, limit):
    item = src.shape[1:]
    total = sum(counts)
    return pl.pallas_call(
        functools.partial(pick_kernel, row_of=row_of, count=total),
        out_shape=[jax.ShapeDtypeStruct((n, *item), src.dtype) for n in counts],
        in_specs=[SM, place],
        out_specs=[ANY] * len(counts),
        scratch_shapes=[
            pltpu.VMEM((total, *item), src.dtype),
            pltpu.SemaphoreType.DMA((total,)),
            pltpu.SemaphoreType.DMA((len(counts),)),
        ],
        compiler_params=pltpu.CompilerParams(vmem_limit_bytes=limit),
    )(rows, src)


def start_loads(pairs, sem, first=0):
    loads = [pltpu.make_async_copy(src, dst, sem.at[first + k]) for k, (src, dst) in enumerate(pairs)]
    for load in loads:
        load.start()
    return loads


def wait_all(copies):
    for copy in copies:
        copy.wait()


def row_blocks(src, dst, count):
    step = src.shape[0] // count
    return [(src.at[pl.ds(k * step, step)], dst.at[pl.ds(k * step, step)]) for k in range(count)]


def back_project(a_ref, w_ref, out_ref):
    groups = out_ref.shape[0]
    part = a_ref.shape[0] // groups
    for h in range(a_ref.shape[1] // HD):
        cols = slice(h * HD, (h + 1) * HD)
        value = mm(a_ref[:, cols], w_ref[:, cols], 1, 1).astype(BF)
        for c in range(groups):
            out_ref[c, h * part : (h + 1) * part] = value[c * part : (c + 1) * part]


def prep_kernel(at_ref, *refs):
    q_in, wk_in, near_in, far_in, wo_in, wv_in, qt_out, dm_out, dt_out, gc_out = refs[:10]
    q_ref, wk_ref, near_ref, far_ref, wo_ref, wv_ref, qt_ref, dm_ref, dt_ref, gc_ref, sem = refs[10:]
    chips, rows, width = near_ref.shape
    cuts = gc_ref.shape[0] // (2 * chips)
    piece = width // cuts
    half = gc_ref.shape[1]
    share = 2 * half
    own = pl.ds(pl.multiple_of((at_ref[0] * 2 + at_ref[1]) * share, share), share)
    ahead = start_loads([(q_in, q_ref), (wk_in, wk_ref)], sem)
    first = start_loads([(near_in, near_ref), (far_in, far_ref)], sem, 2)
    places = []
    for core, g_ref in enumerate((near_ref, far_ref)):
        for s in range(chips):
            j = lax.rem(at_ref[0] + chips - s, chips) * 2 + lax.rem(at_ref[1] + core, 2)
            places.append((g_ref, s, j))
    blocks = start_loads(
        [
            (wo_in.at[:, pl.ds(pl.multiple_of(j * width, width), width)], wo_ref.at[k])
            for k, (_, _, j) in enumerate(places)
        ],
        sem,
        4,
    )
    used = 4 + len(places)
    late = start_loads([(wv_in, wv_ref)], sem, used)
    wait_all(ahead)
    back_project(q_ref, wk_ref, qt_ref)
    stores = start_loads([(qt_ref, qt_out)], sem, used + 1)
    wait_all(first)
    for g_ref, s, j in places:
        for p in range(cuts):
            rows_of = g_ref[s, own, p * piece : (p + 1) * piece]
            gc_ref[j * cuts + p] = jnp.concatenate([rows_of[:half], rows_of[half:]], axis=1)
    stores += start_loads([(gc_ref, gc_out)], sem, used + 2)
    acc = jnp.zeros((rows, width), F32)
    for k, (g_ref, s, _) in enumerate(places):
        blocks[k].wait()
        acc += mm(g_ref[s], wo_ref[k], 1, 1)
    dm_ref[...] = acc.astype(BF)
    wait_all(late)
    back_project(dm_ref, wv_ref, dt_ref)
    stores += start_loads([(dm_ref, dm_out), (dt_ref, dt_out)], sem, used + 3)
    wait_all(stores)


def prep(at, q, wk, near, far, wo, wv, groups, db_count):
    chips, rows, width = near.shape
    tall = (groups, width // HD * rows // groups, wv.shape[0])
    made = [tall, (rows, width), tall, (db_count, rows // (4 * chips), width)]
    operands = (q, wk, near, far, wo, wv)
    return pl.pallas_call(
        prep_kernel,
        out_shape=[jax.ShapeDtypeStruct(shape, BF) for shape in made],
        in_specs=[SM] + [HBM] * 6,
        out_specs=[HBM] * 4,
        scratch_shapes=[
            pltpu.VMEM(shape, BF)
            for shape in (q.shape, wk.shape, near.shape, far.shape, (2 * chips, width, width), wv.shape, *made)
        ]
        + [pltpu.SemaphoreType.DMA((10 + 2 * chips,))],
        compiler_params=params(),
        cost_estimate=pl.CostEstimate(flops=700_000_000, bytes_accessed=8_000_000, transcendentals=0),
    )(at, *operands)


def attn_kernel(count_ref, *refs, c, pieces, last):
    x_in, refs = refs[:pieces], refs[pieces:]
    more = 7 if last else 4
    ins, refs = refs[:more], refs[more:]
    outs = 2 if last else 3
    (send_ref, *keep_outs), refs = refs[:outs], refs[outs:]
    x_ref, mixed_ref, t_ref, u_ref, qt_ref, dt_ref, wv_ref, *refs = refs
    sem = refs[-1]
    slots, sub, enc = x_in[0].shape
    qt_in, dt_in, wv_in = ins[:3]
    part, width = mixed_ref.shape
    heads = width // HD
    db_count = send_ref.shape[0]
    used = 0

    def start(pairs):
        nonlocal used
        loads = start_loads(pairs, sem, used)
        used += len(pairs)
        return loads

    x_loads = start(
        [(qt_in.at[c], qt_ref)]
        + [(x_in[p], x_ref.at[pl.ds(p * slots, slots)]) for p in range(pieces)]
    )
    wait_all(x_loads)
    wv_loads = start(row_blocks(wv_in, wv_ref, 2))
    dt_loads = start([(dt_in.at[c], dt_ref)])
    if last:
        q_ref, dm_ref, t0_ref, u0_ref, gw_ref = refs[:5]
        last_loads = start(list(zip(ins[3:], (q_ref, dm_ref, t0_ref, u0_ref))))
    else:
        gs_ref, whole_ref = refs[:2]
        gs_loads = start([(ins[3], gs_ref)])
    factor = 1.0 / math.sqrt(HD)
    x = x_ref[...].reshape(pieces * slots * sub, enc)
    keys = x.shape[0]
    s = mm(qt_ref[...], x, 1, 1) * factor
    slot = (lax.broadcasted_iota(jnp.int32, (1, keys), 1) // sub) % slots
    expo = jnp.where(slot < count_ref[c], jnp.exp(s), 0.0)
    probs = expo / jnp.sum(expo, axis=-1, keepdims=True)
    t_ref[...] = mm(probs.astype(BF), x, 1, 0).astype(BF)
    wait_all(wv_loads)
    for h in range(heads):
        cols = slice(h * HD, (h + 1) * HD)
        mixed_ref[:, cols] = mm(t_ref[h * part : (h + 1) * part], wv_ref[:, cols], 1, 0).astype(BF)
    if last:
        stores = start([(mixed_ref, send_ref.at[i, pl.ds(0, part)]) for i in range(db_count)])
    else:
        wait_all(gs_loads)
        mixed = mixed_ref[...]
        for i in range(db_count):
            whole_ref[i, :part] = mixed
            whole_ref[i, part:] = gs_ref[i]
        stores = start([(t_ref, keep_outs[1]), (whole_ref, send_ref)])
    wait_all(dt_loads)
    d = mm(dt_ref[...], x, 1, 1)
    inner = jnp.sum(probs * d, axis=-1, keepdims=True)
    ds = (probs * (d - inner) * factor).astype(BF)
    u_ref[...] = mm(ds, x, 1, 0).astype(BF)
    stores += start([(u_ref, keep_outs[0])])
    if last:
        wait_all(last_loads)
        share = enc // db_count
        for h in range(heads):
            rows = slice(h * part, (h + 1) * part)
            cols = slice(h * HD, (h + 1) * HD)
            u_all = jnp.concatenate([u0_ref[rows], u_ref[rows]], axis=0)
            t_all = jnp.concatenate([t0_ref[rows], t_ref[rows]], axis=0)
            sums = (mm(u_all, q_ref[:, cols], 0, 0), mm(t_all, dm_ref[:, cols], 0, 0))
            for k, total in enumerate(sums):
                for i in range(db_count):
                    gw_ref[i, k * share : (k + 1) * share, cols] = total[
                        i * share : (i + 1) * share
                    ].astype(BF)
            stores += start(
                [(gw_ref.at[:, :, pl.ds(h * HD, HD)], send_ref.at[:, pl.ds(part, 2 * share), pl.ds(h * HD, HD)])]
            )
    wait_all(stores)


def attn(count, xs, qt, dt, wv, c, db_count, extra, last):
    slots, sub, enc = xs[0].shape
    width = wv.shape[1]
    tall = qt.shape[1:]
    part = tall[0] * HD // width
    grown = 2 * enc // db_count if last else extra[0].shape[1]
    made = [(db_count, part + grown, width), tall]
    more = list(extra)
    held = [(len(xs) * slots, sub, enc), (part, width), tall, tall, tall, tall, wv.shape]
    held += [v.shape for v in more]
    copies = len(xs) + 8 + len(more) + db_count + width // HD
    if last:
        held += [(db_count, grown, width)]
    else:
        held += [made[0]]
        made += [tall]
    return pl.pallas_call(
        functools.partial(attn_kernel, c=c, pieces=len(xs), last=last),
        out_shape=[jax.ShapeDtypeStruct(shape, BF) for shape in made],
        in_specs=[SM] + [HBM] * (len(xs) + 3 + len(more)),
        out_specs=[HBM] * len(made),
        scratch_shapes=[pltpu.VMEM(shape, BF) for shape in held] + [pltpu.SemaphoreType.DMA((copies,))],
        compiler_params=params(),
        cost_estimate=pl.CostEstimate(flops=3_000_000_000, bytes_accessed=8_000_000, transcendentals=262144),
    )(count, *xs, qt, dt, wv, *more)


def close_kernel(at_ref, *refs, groups):
    sends, us = refs[:groups], refs[groups : 2 * groups]
    wo_in, wk_in, keep_ref, give_ref, gq_ref, mixed_ref, u_ref, wo_ref, wk_ref, sem = refs[2 * groups :]
    chips, rows, width = keep_ref.shape
    part = rows // groups
    first = []
    for c in range(groups):
        pairs = [(sends[c].at[0, pl.ds(0, part)], mixed_ref.at[pl.ds(c * part, part)]), (us[c], u_ref.at[c])]
        first += start_loads(pairs, sem, 2 * c)
    first += start_loads([(wk_in, wk_ref)], sem, 2 * groups)
    loads = start_loads(row_blocks(wo_in, wo_ref, 8), sem, 2 * groups + 1)
    wait_all(first)
    for c in range(groups):
        for h in range(width // HD):
            cols = slice(h * HD, (h + 1) * HD)
            gq_ref[c * part : (c + 1) * part, cols] = mm(
                u_ref[c, h * part : (h + 1) * part], wk_ref[:, cols], 1, 0
            ).astype(BF)
    wait_all(loads)
    mixed = mixed_ref[...]
    for core, block_ref in enumerate((keep_ref, give_ref)):
        for step in range(chips):
            j = lax.rem(at_ref[0] + step, chips) * 2 + lax.rem(at_ref[1] + core, 2)
            cols = pl.ds(pl.multiple_of(j * width, width), width)
            block_ref[step] = mm(mixed, wo_ref[:, cols], 1, 0).astype(BF)


def close(at, sends, us, wo, wk, part, head_count):
    groups = len(us)
    width = wk.shape[1]
    rows = groups * part
    half = jax.ShapeDtypeStruct((head_count // 2, rows, width), BF)
    return pl.pallas_call(
        functools.partial(close_kernel, groups=groups),
        out_shape=[half, half, jax.ShapeDtypeStruct((rows, width), BF)],
        in_specs=[SM] + [HBM] * (2 * groups + 2),
        out_specs=[VM] * 3,
        scratch_shapes=[
            pltpu.VMEM((rows, width), BF),
            pltpu.VMEM((groups, *us[0].shape), BF),
            pltpu.VMEM(wo.shape, BF),
            pltpu.VMEM(wk.shape, BF),
            pltpu.SemaphoreType.DMA((2 * groups + 9,)),
        ],
        compiler_params=params(),
        cost_estimate=pl.CostEstimate(flops=700_000_000, bytes_accessed=8_000_000, transcendentals=0),
    )(at, *sends, *us, wo, wk)


def order_kernel(at_ref, near_ref, far_ref, out_ref):
    chips, _, half, width = near_ref.shape
    share, piece = 2 * half, width // 2
    for core, g_ref in enumerate((near_ref, far_ref)):
        for s in range(chips):
            j = lax.rem(at_ref[0] + chips - s, chips) * 2 + lax.rem(at_ref[1] + core, 2)
            rows = jnp.concatenate([g_ref[s, :, :, :piece], g_ref[s, :, :, piece:]], axis=1)
            out_ref[:, pl.ds(pl.multiple_of(j * share, share), share)] = rows


def order(at, near, far):
    chips, db_count, half, width = near.shape
    return pl.pallas_call(
        order_kernel,
        out_shape=jax.ShapeDtypeStruct((db_count, 4 * chips * half, width // 2), BF),
        in_specs=[SM, VM, VM],
        out_specs=VM,
        compiler_params=params(),
        cost_estimate=pl.CostEstimate(flops=0, bytes_accessed=2_000_000, transcendentals=0),
    )(at, near, far)


def chips_stack(x, steps, count):
    pieces = {0: x, **{s: along(x, s, count) for s in steps}}
    return jnp.stack([pieces[s] for s in range(count // 2)])


def along(v, step, count):
    chips = count // 2
    return lax.ppermute(v, "head", [(i, ((i // 2 + step) % chips) * 2 + i % 2) for i in range(count)])


def swap(v, count):
    return lax.ppermute(v, "head", [(i, i ^ 1) for i in range(count)])


def ring_steps(count):
    chips = count // 2
    return sorted(range(1, chips), key=lambda s: min(s, chips - s))


def exchange(x, axis):
    return lax.all_to_all(x, axis, split_axis=0, concat_axis=0, tiled=True)


def after(x, *others):
    return lax.optimization_barrier((x, *others))[0]


def shards(queries, w_key, w_value, w_out, encodings, nbr_row, nbr_owner, nbr_count, grad_out):
    db_count = lax.axis_size("db")
    head_count = lax.axis_size("head")
    groups, slot_count = nbr_row.shape
    tok_rows, width = queries.shape
    part = tok_rows // groups
    enc = encodings.shape[2]
    head_at = lax.axis_index("head")
    at = jnp.stack([head_at // 2, head_at % 2]).astype(jnp.int32)
    owner_ids = lax.broadcasted_iota(jnp.int32, (db_count, 1, 1, 1), 0)
    wanted = jnp.sum(jnp.where(nbr_owner[None, None] == owner_ids, nbr_row[None, None], 0), axis=3)
    incoming = exchange(wanted, "db")
    steps = ring_steps(head_count)
    (table,) = pick(
        incoming,
        lambda ref, k: ref[k // groups, 0, k % groups],
        encodings,
        (db_count * groups,),
        HBM,
        VMEM_LIMIT,
    )
    received = exchange(table, "db")
    mine = pick(
        nbr_owner,
        lambda ref, k: ref[k // slot_count, k % slot_count] * groups + k // slot_count,
        received,
        (slot_count,) * groups,
        ANY,
        SMALL_LIMIT,
    )
    token = mine[0]
    near = chips_stack(after(grad_out, table), steps, head_count)
    far = swap(near, head_count)
    crossed = [swap(v, head_count) for v in mine]
    qt, dm, dt, grad_cols = prep(at, queries, w_key, near, far, w_out, w_value, groups, db_count)
    ring = []
    for c in range(groups):
        held = mine[c] if c == 0 else after(mine[c], *ring[-1])
        came = [along(held, s, head_count) for s in steps]
        if c == 0:
            came = lax.optimization_barrier((*came, dm, qt))[:-2]
        ring.append([held, *came])
    spread = []
    for c, pieces in enumerate(ring):
        spread.append([*pieces, crossed[c], *(swap(v, head_count) for v in pieces[1:])])
    sent, sends, us = [], [], []
    extra = (grad_cols,)
    for c in range(groups):
        m, u, *t = attn(nbr_count, spread[c], qt, dt, w_value, c, db_count, extra, c == groups - 1)
        us.append(u)
        sends.append(m)
        sent.append(exchange(after(m, *(ring[-1] if c == 0 else sent)), "db"))
        extra = (queries, dm, *t, u)
    rows_near = chips_stack(sent[0][:, part:], steps, head_count)
    grad_tok = order(at, rows_near, swap(rows_near, head_count))
    keep, give, grad_q = close(at, sends, us, w_out, w_key, part, head_count)
    other = swap(give, head_count)
    pair = (keep.astype(F32) + other.astype(F32)).astype(BF)
    terms = [pair[0]] + [along(pair[s], s, head_count) for s in steps]
    attended = sum(t.astype(F32) for t in terms).astype(BF)
    share = enc // db_count
    grad_tok = grad_tok.reshape(db_count, groups, part, -1)
    grad_wo = None
    for c in range(groups):
        term = lax.dot_general(
            sent[c][:, :part], grad_tok[:, c], (((0, 1), (0, 1)), ((), ())), preferred_element_type=F32
        )
        grad_wo = term if grad_wo is None else grad_wo + term
        if c < groups - 1:
            sent[-1], grad_wo = lax.optimization_barrier((sent[-1], grad_wo))
    grad_w = [
        jnp.sum(sent[-1][:, part + k * share : part + (k + 1) * share].astype(F32), axis=0)
        for k in range(2)
    ]
    return (attended, grad_q, *grad_w, grad_wo)


def solution(mesh):
    placed = (
        P("db", "head"),
        P(None, "head"),
        P(None, "head"),
        P("head", None),
        P("db", "head", None),
        P("db", None),
        P("db", None),
        P("db"),
        P("db", "head"),
    )
    return jax.shard_map(
        shards,
        mesh=mesh,
        in_specs=placed,
        out_specs=(
            P("db", "head"),
            P("db", "head"),
            P("db", "head"),
            P("db", "head"),
            P("head", "db"),
        ),
        check_vma=False,
    )
```

```python
import functools
import math

import jax
import jax.numpy as jnp
from jax import lax
from jax.experimental import pallas as pl
from jax.experimental.pallas import tpu as pltpu
from jax.sharding import PartitionSpec as P

HD = 128
BF = jnp.bfloat16
F32 = jnp.float32
VMEM_LIMIT = 60 * 1024 * 1024
SMALL_LIMIT = 8 * 1024 * 1024


def mm(a, b, ca, cb):
    return lax.dot_general(a, b, (((ca,), (cb,)), ((), ())), preferred_element_type=F32)


def params():
    return pltpu.CompilerParams(vmem_limit_bytes=VMEM_LIMIT)


ANY = pl.BlockSpec(memory_space=pl.ANY)
HBM = pl.BlockSpec(memory_space=pltpu.HBM)
VM = pl.BlockSpec(memory_space=pltpu.VMEM)
SM = pl.BlockSpec(memory_space=pltpu.SMEM)


def pick_kernel(rows_ref, src_ref, *rest, row_of, count):
    *outs, held, load_sem, store_sem = rest
    loads = [
        pltpu.make_async_copy(src_ref.at[row_of(rows_ref, k)], held.at[k], load_sem.at[k])
        for k in range(count)
    ]
    for load in loads:
        load.start()
    stores, first = [], 0
    for n, out in enumerate(outs):
        size = out.shape[0]
        for load in loads[first : first + size]:
            load.wait()
        stores.append(pltpu.make_async_copy(held.at[pl.ds(first, size)], out, store_sem.at[n]))
        stores[-1].start()
        first += size
    for store in stores:
        store.wait()


def select_kernel(rows_ref, src_ref, *rest, row_of, count):
    *outs, sem = rest
    places = [out.at[n] for out in outs for n in range(out.shape[0])]
    copies = [
        pltpu.make_async_copy(src_ref.at[row_of(rows_ref, k)], places[k], sem.at[k]) for k in range(count)
    ]
    for copy in copies:
        copy.start()
    for copy in copies:
        copy.wait()


def select(rows, row_of, src, counts):
    total = sum(counts)
    return pl.pallas_call(
        functools.partial(select_kernel, row_of=row_of, count=total),
        out_shape=[jax.ShapeDtypeStruct((n, *src.shape[1:]), src.dtype) for n in counts],
        in_specs=[SM, ANY],
        out_specs=[VM] * len(counts),
        scratch_shapes=[pltpu.SemaphoreType.DMA((total,))],
        compiler_params=pltpu.CompilerParams(vmem_limit_bytes=SMALL_LIMIT),
    )(rows, src)


def pick(rows, row_of, src, counts, place, limit):
    item = src.shape[1:]
    total = sum(counts)
    return pl.pallas_call(
        functools.partial(pick_kernel, row_of=row_of, count=total),
        out_shape=[jax.ShapeDtypeStruct((n, *item), src.dtype) for n in counts],
        in_specs=[SM, place],
        out_specs=[ANY] * len(counts),
        scratch_shapes=[
            pltpu.VMEM((total, *item), src.dtype),
            pltpu.SemaphoreType.DMA((total,)),
            pltpu.SemaphoreType.DMA((len(counts),)),
        ],
        compiler_params=pltpu.CompilerParams(vmem_limit_bytes=limit),
    )(rows, src)


def start_loads(pairs, sem, first=0):
    loads = [pltpu.make_async_copy(src, dst, sem.at[first + k]) for k, (src, dst) in enumerate(pairs)]
    for load in loads:
        load.start()
    return loads


def wait_all(copies):
    for copy in copies:
        copy.wait()


def row_blocks(src, dst, count):
    step = src.shape[0] // count
    return [(src.at[pl.ds(k * step, step)], dst.at[pl.ds(k * step, step)]) for k in range(count)]


def back_project(a_ref, w_ref, out_ref):
    groups = out_ref.shape[0]
    part = a_ref.shape[0] // groups
    for h in range(a_ref.shape[1] // HD):
        cols = slice(h * HD, (h + 1) * HD)
        value = mm(a_ref[:, cols], w_ref[:, cols], 1, 1).astype(BF)
        for c in range(groups):
            out_ref[c, h * part : (h + 1) * part] = value[c * part : (c + 1) * part]


def prep_kernel(at_ref, *refs):
    q_in, wk_in, near_in, far_in, wo_in, wv_in, qt_out, dm_out, dt_out, gc_out = refs[:10]
    q_ref, wk_ref, near_ref, far_ref, wo_ref, wv_ref, qt_ref, dm_ref, dt_ref, gc_ref, sem = refs[10:]
    chips, rows, width = near_ref.shape
    cuts = gc_ref.shape[0] // (2 * chips)
    piece = width // cuts
    half = gc_ref.shape[1]
    share = 2 * half
    own = pl.ds(pl.multiple_of((at_ref[0] * 2 + at_ref[1]) * share, share), share)
    ahead = start_loads([(q_in, q_ref), (wk_in, wk_ref)], sem)
    first = start_loads([(near_in, near_ref), (far_in, far_ref)], sem, 2)
    places = []
    for core, g_ref in enumerate((near_ref, far_ref)):
        for s in range(chips):
            j = lax.rem(at_ref[0] + chips - s, chips) * 2 + lax.rem(at_ref[1] + core, 2)
            places.append((g_ref, s, j))
    blocks = start_loads(
        [
            (wo_in.at[:, pl.ds(pl.multiple_of(j * width, width), width)], wo_ref.at[k])
            for k, (_, _, j) in enumerate(places)
        ],
        sem,
        4,
    )
    used = 4 + len(places)
    late = start_loads([(wv_in, wv_ref)], sem, used)
    wait_all(ahead)
    back_project(q_ref, wk_ref, qt_ref)
    stores = start_loads([(qt_ref, qt_out)], sem, used + 1)
    wait_all(first)
    for g_ref, s, j in places:
        for p in range(cuts):
            rows_of = g_ref[s, own, p * piece : (p + 1) * piece]
            gc_ref[j * cuts + p] = jnp.concatenate([rows_of[:half], rows_of[half:]], axis=1)
    stores += start_loads([(gc_ref, gc_out)], sem, used + 2)
    acc = jnp.zeros((rows, width), F32)
    for k, (g_ref, s, _) in enumerate(places):
        blocks[k].wait()
        acc += mm(g_ref[s], wo_ref[k], 1, 1)
    dm_ref[...] = acc.astype(BF)
    wait_all(late)
    back_project(dm_ref, wv_ref, dt_ref)
    stores += start_loads([(dm_ref, dm_out), (dt_ref, dt_out)], sem, used + 3)
    wait_all(stores)


def prep(at, q, wk, near, far, wo, wv, groups, db_count):
    chips, rows, width = near.shape
    tall = (groups, width // HD * rows // groups, wv.shape[0])
    made = [tall, (rows, width), tall, (db_count, rows // (4 * chips), width)]
    operands = (q, wk, near, far, wo, wv)
    return pl.pallas_call(
        prep_kernel,
        out_shape=[jax.ShapeDtypeStruct(shape, BF) for shape in made],
        in_specs=[SM] + [HBM] * 6,
        out_specs=[HBM] * 4,
        scratch_shapes=[
            pltpu.VMEM(shape, BF)
            for shape in (q.shape, wk.shape, near.shape, far.shape, (2 * chips, width, width), wv.shape, *made)
        ]
        + [pltpu.SemaphoreType.DMA((10 + 2 * chips,))],
        compiler_params=params(),
        cost_estimate=pl.CostEstimate(flops=700_000_000, bytes_accessed=8_000_000, transcendentals=0),
    )(at, *operands)


def attn_kernel(count_ref, *refs, c, pieces, last):
    x_in, refs = refs[:pieces], refs[pieces:]
    more = 7 if last else 4
    ins, refs = refs[:more], refs[more:]
    outs = 2 if last else 3
    (send_ref, *keep_outs), refs = refs[:outs], refs[outs:]
    x_ref, mixed_ref, t_ref, u_ref, qt_ref, dt_ref, wv_ref, *refs = refs
    sem = refs[-1]
    slots, sub, enc = x_in[0].shape
    qt_in, dt_in, wv_in = ins[:3]
    part, width = mixed_ref.shape
    heads = width // HD
    db_count = send_ref.shape[0]
    used = 0

    def start(pairs):
        nonlocal used
        loads = start_loads(pairs, sem, used)
        used += len(pairs)
        return loads

    x_loads = start(
        [(qt_in.at[c], qt_ref)]
        + [(x_in[p], x_ref.at[pl.ds(p * slots, slots)]) for p in range(pieces)]
    )
    wait_all(x_loads)
    wv_loads = start(row_blocks(wv_in, wv_ref, 2))
    dt_loads = start([(dt_in.at[c], dt_ref)])
    if last:
        q_ref, dm_ref, t0_ref, u0_ref, gw_ref = refs[:5]
        last_loads = start(list(zip(ins[3:], (q_ref, dm_ref, t0_ref, u0_ref))))
    else:
        gs_ref, whole_ref = refs[:2]
        gs_loads = start([(ins[3], gs_ref)])
    factor = 1.0 / math.sqrt(HD)
    x = x_ref[...].reshape(pieces * slots * sub, enc)
    keys = x.shape[0]
    s = mm(qt_ref[...], x, 1, 1) * factor
    slot = (lax.broadcasted_iota(jnp.int32, (1, keys), 1) // sub) % slots
    expo = jnp.where(slot < count_ref[c], jnp.exp(s), 0.0)
    probs = expo / jnp.sum(expo, axis=-1, keepdims=True)
    t_ref[...] = mm(probs.astype(BF), x, 1, 0).astype(BF)
    wait_all(wv_loads)
    for h in range(heads):
        cols = slice(h * HD, (h + 1) * HD)
        mixed_ref[:, cols] = mm(t_ref[h * part : (h + 1) * part], wv_ref[:, cols], 1, 0).astype(BF)
    if last:
        stores = start([(mixed_ref, send_ref.at[i, pl.ds(0, part)]) for i in range(db_count)])
    else:
        wait_all(gs_loads)
        mixed = mixed_ref[...]
        for i in range(db_count):
            whole_ref[i, :part] = mixed
            whole_ref[i, part:] = gs_ref[i]
        stores = start([(t_ref, keep_outs[1]), (whole_ref, send_ref)])
    wait_all(dt_loads)
    d = mm(dt_ref[...], x, 1, 1)
    inner = jnp.sum(probs * d, axis=-1, keepdims=True)
    ds = (probs * (d - inner) * factor).astype(BF)
    u_ref[...] = mm(ds, x, 1, 0).astype(BF)
    stores += start([(u_ref, keep_outs[0])])
    if last:
        wait_all(last_loads)
        share = enc // db_count
        for h in range(heads):
            rows = slice(h * part, (h + 1) * part)
            cols = slice(h * HD, (h + 1) * HD)
            u_all = jnp.concatenate([u0_ref[rows], u_ref[rows]], axis=0)
            t_all = jnp.concatenate([t0_ref[rows], t_ref[rows]], axis=0)
            sums = (mm(u_all, q_ref[:, cols], 0, 0), mm(t_all, dm_ref[:, cols], 0, 0))
            for k, total in enumerate(sums):
                for i in range(db_count):
                    gw_ref[i, k * share : (k + 1) * share, cols] = total[
                        i * share : (i + 1) * share
                    ].astype(BF)
            stores += start(
                [(gw_ref.at[:, :, pl.ds(h * HD, HD)], send_ref.at[:, pl.ds(part, 2 * share), pl.ds(h * HD, HD)])]
            )
    wait_all(stores)


def attn(count, xs, qt, dt, wv, c, db_count, extra, last):
    slots, sub, enc = xs[0].shape
    width = wv.shape[1]
    tall = qt.shape[1:]
    part = tall[0] * HD // width
    grown = 2 * enc // db_count if last else extra[0].shape[1]
    made = [(db_count, part + grown, width), tall]
    more = list(extra)
    held = [(len(xs) * slots, sub, enc), (part, width), tall, tall, tall, tall, wv.shape]
    held += [v.shape for v in more]
    copies = len(xs) + 8 + len(more) + db_count + width // HD
    if last:
        held += [(db_count, grown, width)]
    else:
        held += [made[0]]
        made += [tall]
    return pl.pallas_call(
        functools.partial(attn_kernel, c=c, pieces=len(xs), last=last),
        out_shape=[jax.ShapeDtypeStruct(shape, BF) for shape in made],
        in_specs=[SM] + [HBM] * (len(xs) + 3 + len(more)),
        out_specs=[HBM] * len(made),
        scratch_shapes=[pltpu.VMEM(shape, BF) for shape in held] + [pltpu.SemaphoreType.DMA((copies,))],
        compiler_params=params(),
        cost_estimate=pl.CostEstimate(flops=3_000_000_000, bytes_accessed=8_000_000, transcendentals=262144),
    )(count, *xs, qt, dt, wv, *more)


def close_kernel(at_ref, *refs, groups):
    sends, us = refs[:groups], refs[groups : 2 * groups]
    wo_in, wk_in, keep_ref, give_ref, gq_ref, mixed_ref, u_ref, wo_ref, wk_ref, sem = refs[2 * groups :]
    chips, rows, width = keep_ref.shape
    part = rows // groups
    first = []
    for c in range(groups):
        pairs = [(sends[c].at[0, pl.ds(0, part)], mixed_ref.at[pl.ds(c * part, part)]), (us[c], u_ref.at[c])]
        first += start_loads(pairs, sem, 2 * c)
    first += start_loads([(wk_in, wk_ref)], sem, 2 * groups)
    loads = start_loads(row_blocks(wo_in, wo_ref, 8), sem, 2 * groups + 1)
    wait_all(first)
    for c in range(groups):
        for h in range(width // HD):
            cols = slice(h * HD, (h + 1) * HD)
            gq_ref[c * part : (c + 1) * part, cols] = mm(
                u_ref[c, h * part : (h + 1) * part], wk_ref[:, cols], 1, 0
            ).astype(BF)
    wait_all(loads)
    mixed = mixed_ref[...]
    for core, block_ref in enumerate((keep_ref, give_ref)):
        for step in range(chips):
            j = lax.rem(at_ref[0] + step, chips) * 2 + lax.rem(at_ref[1] + core, 2)
            cols = pl.ds(pl.multiple_of(j * width, width), width)
            block_ref[step] = mm(mixed, wo_ref[:, cols], 1, 0).astype(BF)


def close(at, sends, us, wo, wk, part, head_count):
    groups = len(us)
    width = wk.shape[1]
    rows = groups * part
    half = jax.ShapeDtypeStruct((head_count // 2, rows, width), BF)
    return pl.pallas_call(
        functools.partial(close_kernel, groups=groups),
        out_shape=[half, half, jax.ShapeDtypeStruct((rows, width), BF)],
        in_specs=[SM] + [HBM] * (2 * groups + 2),
        out_specs=[VM] * 3,
        scratch_shapes=[
            pltpu.VMEM((rows, width), BF),
            pltpu.VMEM((groups, *us[0].shape), BF),
            pltpu.VMEM(wo.shape, BF),
            pltpu.VMEM(wk.shape, BF),
            pltpu.SemaphoreType.DMA((2 * groups + 9,)),
        ],
        compiler_params=params(),
        cost_estimate=pl.CostEstimate(flops=700_000_000, bytes_accessed=8_000_000, transcendentals=0),
    )(at, *sends, *us, wo, wk)


def order_kernel(at_ref, near_ref, far_ref, out_ref):
    chips, _, half, width = near_ref.shape
    share, piece = 2 * half, width // 2
    for core, g_ref in enumerate((near_ref, far_ref)):
        for s in range(chips):
            j = lax.rem(at_ref[0] + chips - s, chips) * 2 + lax.rem(at_ref[1] + core, 2)
            rows = jnp.concatenate([g_ref[s, :, :, :piece], g_ref[s, :, :, piece:]], axis=1)
            out_ref[:, pl.ds(pl.multiple_of(j * share, share), share)] = rows


def order(at, near, far):
    chips, db_count, half, width = near.shape
    return pl.pallas_call(
        order_kernel,
        out_shape=jax.ShapeDtypeStruct((db_count, 4 * chips * half, width // 2), BF),
        in_specs=[SM, VM, VM],
        out_specs=VM,
        compiler_params=params(),
        cost_estimate=pl.CostEstimate(flops=0, bytes_accessed=2_000_000, transcendentals=0),
    )(at, near, far)


def chips_stack(x, steps, count):
    pieces = {0: x, **{s: along(x, s, count) for s in steps}}
    return jnp.stack([pieces[s] for s in range(count // 2)])


def along(v, step, count):
    chips = count // 2
    return lax.ppermute(v, "head", [(i, ((i // 2 + step) % chips) * 2 + i % 2) for i in range(count)])


def swap(v, count):
    return lax.ppermute(v, "head", [(i, i ^ 1) for i in range(count)])


def ring_steps(count):
    chips = count // 2
    return sorted(range(1, chips), key=lambda s: -min(s, chips - s))


def exchange(x, axis):
    return lax.all_to_all(x, axis, split_axis=0, concat_axis=0, tiled=True)


def after(x, *others):
    return lax.optimization_barrier((x, *others))[0]


def shards(queries, w_key, w_value, w_out, encodings, nbr_row, nbr_owner, nbr_count, grad_out):
    db_count = lax.axis_size("db")
    head_count = lax.axis_size("head")
    groups, slot_count = nbr_row.shape
    tok_rows, width = queries.shape
    part = tok_rows // groups
    enc = encodings.shape[2]
    head_at = lax.axis_index("head")
    at = jnp.stack([head_at // 2, head_at % 2]).astype(jnp.int32)
    owner_ids = lax.broadcasted_iota(jnp.int32, (db_count, 1, 1, 1), 0)
    wanted = jnp.sum(jnp.where(nbr_owner[None, None] == owner_ids, nbr_row[None, None], 0), axis=3)
    incoming = exchange(wanted, "db")
    steps = ring_steps(head_count)
    (table,) = pick(
        incoming,
        lambda ref, k: ref[k // groups, 0, k % groups],
        encodings,
        (db_count * groups,),
        HBM,
        VMEM_LIMIT,
    )
    received = exchange(table, "db")
    mine = select(
        nbr_owner,
        lambda ref, k: ref[k // slot_count, k % slot_count] * groups + k // slot_count,
        received,
        (slot_count,) * groups,
    )
    near = chips_stack(after(grad_out, table), steps, head_count)
    far = swap(near, head_count)
    crossed = [swap(v, head_count) for v in mine]
    qt, dm, dt, grad_cols = prep(at, queries, w_key, near, far, w_out, w_value, groups, db_count)
    ring = []
    for c in range(groups):
        held = mine[c] if c == 0 else after(mine[c], *ring[-1])
        came = [along(held, s, head_count) for s in steps]
        if c == 0:
            came = lax.optimization_barrier((*came, dm, qt))[:-2]
        ring.append([held, *came])
    spread = []
    for c, pieces in enumerate(ring):
        spread.append([*pieces, crossed[c], *(swap(v, head_count) for v in pieces[1:])])
    sent, sends, us = [], [], []
    extra = (grad_cols,)
    for c in range(groups):
        m, u, *t = attn(nbr_count, spread[c], qt, dt, w_value, c, db_count, extra, c == groups - 1)
        us.append(u)
        sends.append(m)
        sent.append(exchange(after(m, *(ring[-1] if c == 0 else sent)), "db"))
        extra = (queries, dm, *t, u)
    rows_near = chips_stack(sent[0][:, part:], steps, head_count)
    grad_tok = order(at, rows_near, swap(rows_near, head_count))
    keep, give, grad_q = close(at, sends, us, w_out, w_key, part, head_count)
    other = swap(give, head_count)
    pair = (keep.astype(F32) + other.astype(F32)).astype(BF)
    terms = [pair[0]] + [along(pair[s], s, head_count) for s in steps]
    attended = sum(t.astype(F32) for t in terms).astype(BF)
    share = enc // db_count
    grad_tok = grad_tok.reshape(db_count, groups, part, -1)
    grad_wo = None
    for c in range(groups):
        term = lax.dot_general(
            sent[c][:, :part], grad_tok[:, c], (((0, 1), (0, 1)), ((), ())), preferred_element_type=F32
        )
        grad_wo = term if grad_wo is None else grad_wo + term
        if c < groups - 1:
            sent[-1], grad_wo = lax.optimization_barrier((sent[-1], grad_wo))
    grad_w = [
        jnp.sum(sent[-1][:, part + k * share : part + (k + 1) * share].astype(F32), axis=0)
        for k in range(2)
    ]
    return (attended, grad_q, *grad_w, grad_wo)


def solution(mesh):
    placed = (
        P("db", "head"),
        P(None, "head"),
        P(None, "head"),
        P("head", None),
        P("db", "head", None),
        P("db", None),
        P("db", None),
        P("db"),
        P("db", "head"),
    )
    return jax.shard_map(
        shards,
        mesh=mesh,
        in_specs=placed,
        out_specs=(
            P("db", "head"),
            P("db", "head"),
            P("db", "head"),
            P("db", "head"),
            P("head", "db"),
        ),
        check_vma=False,
    )
```

```python
import functools
import math

import jax
import jax.numpy as jnp
from jax import lax
from jax.experimental import pallas as pl
from jax.experimental.pallas import tpu as pltpu
from jax.sharding import PartitionSpec as P

HD = 128
BF = jnp.bfloat16
F32 = jnp.float32
VMEM_LIMIT = 60 * 1024 * 1024
PARTS = 4
SMALL_LIMIT = 8 * 1024 * 1024


def mm(a, b, ca, cb):
    return lax.dot_general(a, b, (((ca,), (cb,)), ((), ())), preferred_element_type=F32)


def params():
    return pltpu.CompilerParams(vmem_limit_bytes=VMEM_LIMIT)


ANY = pl.BlockSpec(memory_space=pl.ANY)
HBM = pl.BlockSpec(memory_space=pltpu.HBM)
VM = pl.BlockSpec(memory_space=pltpu.VMEM)
SM = pl.BlockSpec(memory_space=pltpu.SMEM)


def pick_kernel(rows_ref, src_ref, *rest, row_of, count):
    *outs, held, load_sem, store_sem = rest
    loads = [
        pltpu.make_async_copy(src_ref.at[row_of(rows_ref, k)], held.at[k], load_sem.at[k])
        for k in range(count)
    ]
    for load in loads:
        load.start()
    stores, first = [], 0
    for n, out in enumerate(outs):
        size = out.shape[0]
        step = size // PARTS
        for p in range(PARTS):
            for load in loads[first : first + step]:
                load.wait()
            part = out.at[pl.ds(p * step, step)]
            stores.append(
                pltpu.make_async_copy(held.at[pl.ds(first, step)], part, store_sem.at[n * PARTS + p])
            )
            stores[-1].start()
            first += step
    for store in stores:
        store.wait()


def select_kernel(rows_ref, src_ref, *rest, row_of, count):
    *outs, sem = rest
    places = [out.at[n] for out in outs for n in range(out.shape[0])]
    copies = [
        pltpu.make_async_copy(src_ref.at[row_of(rows_ref, k)], places[k], sem.at[k]) for k in range(count)
    ]
    for copy in copies:
        copy.start()
    for copy in copies:
        copy.wait()


def select(rows, row_of, src, counts):
    total = sum(counts)
    return pl.pallas_call(
        functools.partial(select_kernel, row_of=row_of, count=total),
        out_shape=[jax.ShapeDtypeStruct((n, *src.shape[1:]), src.dtype) for n in counts],
        in_specs=[SM, ANY],
        out_specs=[VM] * len(counts),
        scratch_shapes=[pltpu.SemaphoreType.DMA((total,))],
        compiler_params=pltpu.CompilerParams(vmem_limit_bytes=SMALL_LIMIT),
    )(rows, src)


def pick(rows, row_of, src, counts, place, limit):
    item = src.shape[1:]
    total = sum(counts)
    return pl.pallas_call(
        functools.partial(pick_kernel, row_of=row_of, count=total),
        out_shape=[jax.ShapeDtypeStruct((n, *item), src.dtype) for n in counts],
        in_specs=[SM, place],
        out_specs=[ANY] * len(counts),
        scratch_shapes=[
            pltpu.VMEM((total, *item), src.dtype),
            pltpu.SemaphoreType.DMA((total,)),
            pltpu.SemaphoreType.DMA((len(counts) * PARTS,)),
        ],
        compiler_params=pltpu.CompilerParams(vmem_limit_bytes=limit),
    )(rows, src)


def start_loads(pairs, sem, first=0):
    loads = [pltpu.make_async_copy(src, dst, sem.at[first + k]) for k, (src, dst) in enumerate(pairs)]
    for load in loads:
        load.start()
    return loads


def wait_all(copies):
    for copy in copies:
        copy.wait()


def row_blocks(src, dst, count):
    step = src.shape[0] // count
    return [(src.at[pl.ds(k * step, step)], dst.at[pl.ds(k * step, step)]) for k in range(count)]


def back_project(a_ref, w_ref, out_ref):
    groups = out_ref.shape[0]
    part = a_ref.shape[0] // groups
    for h in range(a_ref.shape[1] // HD):
        cols = slice(h * HD, (h + 1) * HD)
        value = mm(a_ref[:, cols], w_ref[:, cols], 1, 1).astype(BF)
        for c in range(groups):
            out_ref[c, h * part : (h + 1) * part] = value[c * part : (c + 1) * part]


def prep_kernel(at_ref, *refs):
    q_in, wk_in, near_in, far_in, wo_in, wv_in, qt_out, dm_out, dt_out, gc_out = refs[:10]
    q_ref, wk_ref, near_ref, far_ref, wo_ref, wv_ref, qt_ref, dm_ref, dt_ref, gc_ref, sem = refs[10:]
    chips, rows, width = near_ref.shape
    cuts = gc_ref.shape[0] // (2 * chips)
    piece = width // cuts
    half = gc_ref.shape[1]
    share = 2 * half
    own = pl.ds(pl.multiple_of((at_ref[0] * 2 + at_ref[1]) * share, share), share)
    ahead = start_loads([(q_in, q_ref), (wk_in, wk_ref)], sem)
    first = start_loads([(near_in, near_ref), (far_in, far_ref)], sem, 2)
    places = []
    for core, g_ref in enumerate((near_ref, far_ref)):
        for s in range(chips):
            j = lax.rem(at_ref[0] + chips - s, chips) * 2 + lax.rem(at_ref[1] + core, 2)
            places.append((g_ref, s, j))
    blocks = start_loads(
        [
            (wo_in.at[:, pl.ds(pl.multiple_of(j * width, width), width)], wo_ref.at[k])
            for k, (_, _, j) in enumerate(places)
        ],
        sem,
        4,
    )
    used = 4 + len(places)
    late = start_loads([(wv_in, wv_ref)], sem, used)
    wait_all(ahead)
    back_project(q_ref, wk_ref, qt_ref)
    stores = start_loads([(qt_ref, qt_out)], sem, used + 1)
    wait_all(first)
    for g_ref, s, j in places:
        for p in range(cuts):
            rows_of = g_ref[s, own, p * piece : (p + 1) * piece]
            gc_ref[j * cuts + p] = jnp.concatenate([rows_of[:half], rows_of[half:]], axis=1)
    stores += start_loads([(gc_ref, gc_out)], sem, used + 2)
    acc = jnp.zeros((rows, width), F32)
    for k, (g_ref, s, _) in enumerate(places):
        blocks[k].wait()
        acc += mm(g_ref[s], wo_ref[k], 1, 1)
    dm_ref[...] = acc.astype(BF)
    wait_all(late)
    back_project(dm_ref, wv_ref, dt_ref)
    stores += start_loads([(dm_ref, dm_out), (dt_ref, dt_out)], sem, used + 3)
    wait_all(stores)


def prep(at, q, wk, near, far, wo, wv, groups, db_count):
    chips, rows, width = near.shape
    tall = (groups, width // HD * rows // groups, wv.shape[0])
    made = [tall, (rows, width), tall, (db_count, rows // (4 * chips), width)]
    operands = (q, wk, near, far, wo, wv)
    return pl.pallas_call(
        prep_kernel,
        out_shape=[jax.ShapeDtypeStruct(shape, BF) for shape in made],
        in_specs=[SM] + [HBM] * 6,
        out_specs=[HBM] * 4,
        scratch_shapes=[
            pltpu.VMEM(shape, BF)
            for shape in (q.shape, wk.shape, near.shape, far.shape, (2 * chips, width, width), wv.shape, *made)
        ]
        + [pltpu.SemaphoreType.DMA((10 + 2 * chips,))],
        compiler_params=params(),
        cost_estimate=pl.CostEstimate(flops=700_000_000, bytes_accessed=8_000_000, transcendentals=0),
    )(at, *operands)


def attn_kernel(count_ref, *refs, c, pieces, last):
    x_in, refs = refs[:pieces], refs[pieces:]
    more = 7 if last else 4
    ins, refs = refs[:more], refs[more:]
    outs = 2 if last else 3
    (send_ref, *keep_outs), refs = refs[:outs], refs[outs:]
    x_ref, mixed_ref, t_ref, u_ref, qt_ref, dt_ref, wv_ref, *refs = refs
    sem = refs[-1]
    slots, sub, enc = x_in[0].shape
    qt_in, dt_in, wv_in = ins[:3]
    part, width = mixed_ref.shape
    heads = width // HD
    db_count = send_ref.shape[0]
    used = 0

    def start(pairs):
        nonlocal used
        loads = start_loads(pairs, sem, used)
        used += len(pairs)
        return loads

    x_loads = start(
        [(qt_in.at[c], qt_ref)]
        + [(x_in[p], x_ref.at[pl.ds(p * slots, slots)]) for p in range(pieces)]
    )
    wait_all(x_loads)
    wv_loads = start(row_blocks(wv_in, wv_ref, 2))
    dt_loads = start([(dt_in.at[c], dt_ref)])
    if last:
        q_ref, dm_ref, t0_ref, u0_ref, gw_ref = refs[:5]
        last_loads = start(list(zip(ins[3:], (q_ref, dm_ref, t0_ref, u0_ref))))
    else:
        gs_ref, whole_ref = refs[:2]
        gs_loads = start([(ins[3], gs_ref)])
    factor = 1.0 / math.sqrt(HD)
    x = x_ref[...].reshape(pieces * slots * sub, enc)
    keys = x.shape[0]
    s = mm(qt_ref[...], x, 1, 1) * factor
    slot = (lax.broadcasted_iota(jnp.int32, (1, keys), 1) // sub) % slots
    expo = jnp.where(slot < count_ref[c], jnp.exp(s), 0.0)
    probs = expo / jnp.sum(expo, axis=-1, keepdims=True)
    t_ref[...] = mm(probs.astype(BF), x, 1, 0).astype(BF)
    wait_all(wv_loads)
    for h in range(heads):
        cols = slice(h * HD, (h + 1) * HD)
        mixed_ref[:, cols] = mm(t_ref[h * part : (h + 1) * part], wv_ref[:, cols], 1, 0).astype(BF)
    if last:
        stores = start([(mixed_ref, send_ref.at[i, pl.ds(0, part)]) for i in range(db_count)])
    else:
        wait_all(gs_loads)
        mixed = mixed_ref[...]
        for i in range(db_count):
            whole_ref[i, :part] = mixed
            whole_ref[i, part:] = gs_ref[i]
        stores = start([(t_ref, keep_outs[1]), (whole_ref, send_ref)])
    wait_all(dt_loads)
    d = mm(dt_ref[...], x, 1, 1)
    inner = jnp.sum(probs * d, axis=-1, keepdims=True)
    ds = (probs * (d - inner) * factor).astype(BF)
    u_ref[...] = mm(ds, x, 1, 0).astype(BF)
    stores += start([(u_ref, keep_outs[0])])
    if last:
        wait_all(last_loads)
        share = enc // db_count
        for h in range(heads):
            rows = slice(h * part, (h + 1) * part)
            cols = slice(h * HD, (h + 1) * HD)
            u_all = jnp.concatenate([u0_ref[rows], u_ref[rows]], axis=0)
            t_all = jnp.concatenate([t0_ref[rows], t_ref[rows]], axis=0)
            sums = (mm(u_all, q_ref[:, cols], 0, 0), mm(t_all, dm_ref[:, cols], 0, 0))
            for k, total in enumerate(sums):
                for i in range(db_count):
                    gw_ref[i, k * share : (k + 1) * share, cols] = total[
                        i * share : (i + 1) * share
                    ].astype(BF)
            stores += start(
                [(gw_ref.at[:, :, pl.ds(h * HD, HD)], send_ref.at[:, pl.ds(part, 2 * share), pl.ds(h * HD, HD)])]
            )
    wait_all(stores)


def attn(count, xs, qt, dt, wv, c, db_count, extra, last):
    slots, sub, enc = xs[0].shape
    width = wv.shape[1]
    tall = qt.shape[1:]
    part = tall[0] * HD // width
    grown = 2 * enc // db_count if last else extra[0].shape[1]
    made = [(db_count, part + grown, width), tall]
    more = list(extra)
    held = [(len(xs) * slots, sub, enc), (part, width), tall, tall, tall, tall, wv.shape]
    held += [v.shape for v in more]
    copies = len(xs) + 8 + len(more) + db_count + width // HD
    if last:
        held += [(db_count, grown, width)]
    else:
        held += [made[0]]
        made += [tall]
    return pl.pallas_call(
        functools.partial(attn_kernel, c=c, pieces=len(xs), last=last),
        out_shape=[jax.ShapeDtypeStruct(shape, BF) for shape in made],
        in_specs=[SM] + [HBM] * (len(xs) + 3 + len(more)),
        out_specs=[HBM] * len(made),
        scratch_shapes=[pltpu.VMEM(shape, BF) for shape in held] + [pltpu.SemaphoreType.DMA((copies,))],
        compiler_params=params(),
        cost_estimate=pl.CostEstimate(flops=3_000_000_000, bytes_accessed=8_000_000, transcendentals=262144),
    )(count, *xs, qt, dt, wv, *more)


def close_kernel(at_ref, *refs, groups):
    sends, us = refs[:groups], refs[groups : 2 * groups]
    wo_in, wk_in, keep_ref, give_ref, gq_ref, mixed_ref, u_ref, wo_ref, wk_ref, sem = refs[2 * groups :]
    chips, rows, width = keep_ref.shape
    part = rows // groups
    first = []
    for c in range(groups):
        pairs = [(sends[c].at[0, pl.ds(0, part)], mixed_ref.at[pl.ds(c * part, part)]), (us[c], u_ref.at[c])]
        first += start_loads(pairs, sem, 2 * c)
    first += start_loads([(wk_in, wk_ref)], sem, 2 * groups)
    loads = start_loads(row_blocks(wo_in, wo_ref, 8), sem, 2 * groups + 1)
    wait_all(first)
    for c in range(groups):
        for h in range(width // HD):
            cols = slice(h * HD, (h + 1) * HD)
            gq_ref[c * part : (c + 1) * part, cols] = mm(
                u_ref[c, h * part : (h + 1) * part], wk_ref[:, cols], 1, 0
            ).astype(BF)
    wait_all(loads)
    mixed = mixed_ref[...]
    for core, block_ref in enumerate((keep_ref, give_ref)):
        for step in range(chips):
            j = lax.rem(at_ref[0] + step, chips) * 2 + lax.rem(at_ref[1] + core, 2)
            cols = pl.ds(pl.multiple_of(j * width, width), width)
            block_ref[step] = mm(mixed, wo_ref[:, cols], 1, 0).astype(BF)


def close(at, sends, us, wo, wk, part, head_count):
    groups = len(us)
    width = wk.shape[1]
    rows = groups * part
    half = jax.ShapeDtypeStruct((head_count // 2, rows, width), BF)
    return pl.pallas_call(
        functools.partial(close_kernel, groups=groups),
        out_shape=[half, half, jax.ShapeDtypeStruct((rows, width), BF)],
        in_specs=[SM] + [HBM] * (2 * groups + 2),
        out_specs=[VM] * 3,
        scratch_shapes=[
            pltpu.VMEM((rows, width), BF),
            pltpu.VMEM((groups, *us[0].shape), BF),
            pltpu.VMEM(wo.shape, BF),
            pltpu.VMEM(wk.shape, BF),
            pltpu.SemaphoreType.DMA((2 * groups + 9,)),
        ],
        compiler_params=params(),
        cost_estimate=pl.CostEstimate(flops=700_000_000, bytes_accessed=8_000_000, transcendentals=0),
    )(at, *sends, *us, wo, wk)


def order_kernel(at_ref, near_ref, far_ref, out_ref):
    chips, _, half, width = near_ref.shape
    share, piece = 2 * half, width // 2
    for core, g_ref in enumerate((near_ref, far_ref)):
        for s in range(chips):
            j = lax.rem(at_ref[0] + chips - s, chips) * 2 + lax.rem(at_ref[1] + core, 2)
            rows = jnp.concatenate([g_ref[s, :, :, :piece], g_ref[s, :, :, piece:]], axis=1)
            out_ref[:, pl.ds(pl.multiple_of(j * share, share), share)] = rows


def order(at, near, far):
    chips, db_count, half, width = near.shape
    return pl.pallas_call(
        order_kernel,
        out_shape=jax.ShapeDtypeStruct((db_count, 4 * chips * half, width // 2), BF),
        in_specs=[SM, VM, VM],
        out_specs=VM,
        compiler_params=params(),
        cost_estimate=pl.CostEstimate(flops=0, bytes_accessed=2_000_000, transcendentals=0),
    )(at, near, far)


def chips_stack(x, steps, count):
    pieces = {0: x, **{s: along(x, s, count) for s in steps}}
    return jnp.stack([pieces[s] for s in range(count // 2)])


def along(v, step, count):
    chips = count // 2
    return lax.ppermute(v, "head", [(i, ((i // 2 + step) % chips) * 2 + i % 2) for i in range(count)])


def swap(v, count):
    return lax.ppermute(v, "head", [(i, i ^ 1) for i in range(count)])


def ring_steps(count):
    chips = count // 2
    return sorted(range(1, chips), key=lambda s: -min(s, chips - s))


def exchange(x, axis):
    return lax.all_to_all(x, axis, split_axis=0, concat_axis=0, tiled=True)


def after(x, *others):
    return lax.optimization_barrier((x, *others))[0]


def shards(queries, w_key, w_value, w_out, encodings, nbr_row, nbr_owner, nbr_count, grad_out):
    db_count = lax.axis_size("db")
    head_count = lax.axis_size("head")
    groups, slot_count = nbr_row.shape
    tok_rows, width = queries.shape
    part = tok_rows // groups
    enc = encodings.shape[2]
    head_at = lax.axis_index("head")
    at = jnp.stack([head_at // 2, head_at % 2]).astype(jnp.int32)
    owner_ids = lax.broadcasted_iota(jnp.int32, (db_count, 1, 1, 1), 0)
    wanted = jnp.sum(jnp.where(nbr_owner[None, None] == owner_ids, nbr_row[None, None], 0), axis=3)
    incoming = exchange(wanted, "db")
    steps = ring_steps(head_count)
    (table,) = pick(
        incoming,
        lambda ref, k: ref[k // groups, 0, k % groups],
        encodings,
        (db_count * groups,),
        HBM,
        VMEM_LIMIT,
    )
    received = exchange(table, "db")
    mine = select(
        nbr_owner,
        lambda ref, k: ref[k // slot_count, k % slot_count] * groups + k // slot_count,
        received,
        (slot_count,) * groups,
    )
    near = chips_stack(after(grad_out, table), steps, head_count)
    far = swap(near, head_count)
    crossed = [swap(v, head_count) for v in mine]
    qt, dm, dt, grad_cols = prep(at, queries, w_key, near, far, w_out, w_value, groups, db_count)
    ring = []
    for c in range(groups):
        held = mine[c] if c == 0 else after(mine[c], *ring[-1])
        came = [along(held, s, head_count) for s in steps]
        if c == 0:
            came = lax.optimization_barrier((*came, dm, qt))[:-2]
        ring.append([held, *came])
    spread = []
    for c, pieces in enumerate(ring):
        spread.append([*pieces, crossed[c], *(swap(v, head_count) for v in pieces[1:])])
    sent, sends, us = [], [], []
    extra = (grad_cols,)
    for c in range(groups):
        m, u, *t = attn(nbr_count, spread[c], qt, dt, w_value, c, db_count, extra, c == groups - 1)
        us.append(u)
        sends.append(m)
        sent.append(exchange(after(m, *(ring[-1] if c == 0 else sent)), "db"))
        extra = (queries, dm, *t, u)
    rows_near = chips_stack(sent[0][:, part:], steps, head_count)
    grad_tok = order(at, rows_near, swap(rows_near, head_count))
    keep, give, grad_q = close(at, sends, us, w_out, w_key, part, head_count)
    other = swap(give, head_count)
    pair = (keep.astype(F32) + other.astype(F32)).astype(BF)
    terms = [pair[0]] + [along(pair[s], s, head_count) for s in steps]
    attended = sum(t.astype(F32) for t in terms).astype(BF)
    share = enc // db_count
    grad_tok = grad_tok.reshape(db_count, groups, part, -1)
    grad_wo = None
    for c in range(groups):
        term = lax.dot_general(
            sent[c][:, :part], grad_tok[:, c], (((0, 1), (0, 1)), ((), ())), preferred_element_type=F32
        )
        grad_wo = term if grad_wo is None else grad_wo + term
        if c < groups - 1:
            sent[-1], grad_wo = lax.optimization_barrier((sent[-1], grad_wo))
    grad_w = [
        jnp.sum(sent[-1][:, part + k * share : part + (k + 1) * share].astype(F32), axis=0)
        for k in range(2)
    ]
    return (attended, grad_q, *grad_w, grad_wo)


def solution(mesh):
    placed = (
        P("db", "head"),
        P(None, "head"),
        P(None, "head"),
        P("head", None),
        P("db", "head", None),
        P("db", None),
        P("db", None),
        P("db"),
        P("db", "head"),
    )
    return jax.shard_map(
        shards,
        mesh=mesh,
        in_specs=placed,
        out_specs=(
            P("db", "head"),
            P("db", "head"),
            P("db", "head"),
            P("db", "head"),
            P("head", "db"),
        ),
        check_vma=False,
    )
```
